32 devices in a mesh: row: 8 (over y, x, core), col: 4 (over z).
Axes of the slice: x: 2, y: 2, z: 4, core: 2. Of those that a mesh axis runs over, the one named last changes fastest.
Arguments:
- tokens: bfloat16 [512, 8192], P('col', 'row'), may hold values from -6 to 6
- w_packed: bfloat16 [8, 4, 448, 128, 128], P('row', 'col'), may hold values from -0.09375 to 0.09375
- kept_rows: int32 [8, 4, 448], P('row', 'col'), may hold values from 0 to 7, as said below
- kept_cols: int32 [8, 4, 448], P('row', 'col'), may hold values from 0 to 55, as said below
- kept_count: int32 [8, 4], P('row', 'col'), may hold values from 1 to 448, as said below
- grad_act: bfloat16 [512, 28672], P('row', 'col'), may hold values from -6 to 6
Outputs:
- activation: bfloat16 [512, 28672], P('row', 'col')
- input_grad: bfloat16 [512, 8192], P('col', 'row')
- weight_grad: bfloat16 [8, 4, 448, 128, 128], P('row', 'col')
The draws below stay inside these ranges and needn't reach their ends.
Inputs may be any that keep to these rules, and one draw needn't show every extreme that they name: Within each tile, the 448 slots name every block of the tile once (kept_rows[r, c, s] * 56 + kept_cols[r, c, s] runs over all block places). `kept_cols`: see kept_rows. `kept_count`: some tile in every draw keeps all 448 blocks.
All inputs are finite; a program needn't handle non-finite values.
Results may differ from the reference program's by a relative error of at most 0.0049.
Values may be sent and summed in bfloat16 or wider, within the bound.
No kernel may reach another device: no remote copies, remote signals or barrier semaphores. Data moves between devices by JAX's collectives and lax.ppermute only.
A program may use at most 384 MiB of HBM per device.

```python
import jax
import jax.numpy as jnp

D = 8192
FF = 28672
BLK = 128
TOKENS = 512
RB = 8
CB = 56
CAP = 448
N_ROW = 8
N_COL = 4


def kept_layout(key):
    tile_keys = jax.random.split(jax.random.fold_in(key, 11), N_ROW * N_COL)
    shuffled = jax.vmap(lambda one_key: jax.random.permutation(one_key, CAP))(tile_keys)
    return shuffled.reshape(N_ROW, N_COL, CAP).astype(jnp.int32)


def draw_kept_rows(key, part):
    return (kept_layout(key) // CB).astype(jnp.int32)


def draw_kept_cols(key, part):
    return (kept_layout(key) % CB).astype(jnp.int32)


def draw_kept_count(key, part):
    counts = jax.random.randint(jax.random.fold_in(key, 12), (N_ROW * N_COL,), 1, CAP + 1)
    fullest = jax.random.randint(jax.random.fold_in(key, 13), (), 0, N_ROW * N_COL)
    counts = jnp.where(jnp.arange(N_ROW * N_COL) == fullest, CAP, counts)
    return counts.reshape(N_ROW, N_COL).astype(jnp.int32)


def level_of(key, shape, cuts, smallest, largest):
    level = 1.0
    for axis_at, blocks in cuts:
        steps = jax.random.uniform(jax.random.fold_in(jax.random.fold_in(key, 6), axis_at), (blocks,), jnp.float32, smallest / len(cuts), largest / len(cuts))
        level = level * jnp.repeat(jnp.exp(steps), shape[axis_at] // blocks).reshape((-1,) + (1,) * (len(shape) - 1 - axis_at))
    return level


def noise(stream_key, extent, deviation, most, cuts=(), kind=jnp.bfloat16):
    array = deviation * jax.random.normal(stream_key, extent, jnp.float32)
    if cuts:
        array = array * level_of(stream_key, extent, cuts, -0.22, 0.18)
    return jnp.clip(array, -most, most).astype(kind)


def setup_inputs(seed: int = 0) -> dict:
    key_list = jax.random.split(jax.random.key(seed), 7)
    tokens = noise(key_list[0], (TOKENS, D), 1.0, 6.0, ((0, 4), (1, 8)))
    w_packed = noise(key_list[1], (N_ROW, N_COL, CAP, BLK, BLK), (D // 2) ** -0.5, 0.09375, ((0, 8), (1, 4)))
    kept_rows = draw_kept_rows(jax.random.fold_in(key_list[6], 71), 0)
    kept_cols = draw_kept_cols(jax.random.fold_in(key_list[6], 71), 0)
    kept_count = draw_kept_count(jax.random.fold_in(key_list[6], 71), 0)
    grad_act = noise(key_list[5], (TOKENS, FF), 1.0, 6.0, ((0, 8), (1, 4)))
    return dict(tokens=tokens, w_packed=w_packed, kept_rows=kept_rows, kept_cols=kept_cols, kept_count=kept_count, grad_act=grad_act)


gelu_scale = 0.7978845608
gelu_cubic = 0.044715


def dense_weight(w_packed, kept_rows, kept_cols, kept_count):
    live_slots = jnp.arange(CAP)[None, None, :] < kept_count[:, :, None]
    blocks = jnp.where(live_slots[..., None, None], w_packed, jnp.zeros_like(w_packed))
    places = (kept_rows * CB + kept_cols).astype(jnp.int32)
    row_index = jnp.broadcast_to(jnp.arange(N_ROW)[:, None, None], places.shape)
    col_index = jnp.broadcast_to(jnp.arange(N_COL)[None, :, None], places.shape)
    grid = jnp.zeros((N_ROW, N_COL, RB * CB, BLK, BLK), w_packed.dtype)
    grid = grid.at[row_index, col_index, places].set(blocks)
    grid = grid.reshape(N_ROW, N_COL, RB, CB, BLK, BLK).transpose(0, 2, 4, 1, 3, 5)
    return grid.reshape(D, FF), places, live_slots


def reference(tokens, w_packed, kept_rows, kept_cols, kept_count, grad_act):
    weight, places, live_slots = dense_weight(w_packed, kept_rows, kept_cols, kept_count)
    hidden = jnp.dot(tokens, weight, preferred_element_type=jnp.float32)
    inner = gelu_scale * (hidden + gelu_cubic * hidden * hidden * hidden)
    tangent = jnp.tanh(inner)
    activation = (0.5 * hidden * (1.0 + tangent)).astype(jnp.bfloat16)
    slope = 0.5 * (1.0 + tangent) + 0.5 * hidden * (1.0 - tangent * tangent) * gelu_scale * (1.0 + 3.0 * gelu_cubic * hidden * hidden)
    slope_grad = (grad_act.astype(jnp.float32) * slope).astype(jnp.bfloat16)
    input_grad = jnp.dot(slope_grad, weight.T, preferred_element_type=jnp.float32).astype(jnp.bfloat16)
    full_grad = jnp.dot(tokens.T, slope_grad, preferred_element_type=jnp.float32)
    tiles = full_grad.reshape(N_ROW, RB, BLK, N_COL, CB, BLK).transpose(0, 3, 1, 4, 2, 5)
    tiles = tiles.reshape(N_ROW, N_COL, RB * CB, BLK, BLK)
    picked = jnp.take_along_axis(tiles, places[..., None, None], axis=2)
    weight_grad = jnp.where(live_slots[..., None, None], picked, jnp.zeros_like(picked)).astype(jnp.bfloat16)
    return activation, input_grad, weight_grad
```

```python
import functools

import jax
import jax.numpy as jnp
import numpy as np
from jax import lax
from jax.experimental import pallas as pl
from jax.experimental.pallas import tpu as pltpu
from jax.sharding import PartitionSpec as P

gelu_scale = 0.7978845608
gelu_cubic = 0.044715
chunk_goal = 4
vmem_limit = 56 * 1024 * 1024


def gelu_pair(hidden, cotangent):
    inner = gelu_scale * (hidden + gelu_cubic * hidden * hidden * hidden)
    tangent = jnp.tanh(inner)
    activation = (0.5 * hidden * (1.0 + tangent)).astype(jnp.bfloat16)
    slope = 0.5 * (1.0 + tangent) + 0.5 * hidden * (1.0 - tangent * tangent) * gelu_scale * (
        1.0 + 3.0 * gelu_cubic * hidden * hidden
    )
    slope_grad = (cotangent.astype(jnp.float32) * slope).astype(jnp.bfloat16)
    return (activation, slope_grad)


def group_of(blocks, goal):
    return max(n for n in range(1, goal + 1) if blocks % n == 0)


def dense_kernel(row_blocks, col_blocks, per_step, depth, code, w_ref, out_ref, held, empty, sems):
    step = pl.program_id(0)
    steps = pl.num_programs(0)
    blk = w_ref.shape[-1]

    def load(at):
        slot_at = lax.rem(at, depth)
        for r in range(row_blocks):
            for c in range(per_step):
                entry = code[r * col_blocks + at * per_step + c]
                target = held.at[slot_at, pl.ds(r * blk, blk), pl.ds(c * blk, blk)]

                @pl.when(lax.rem(entry, 2) == 1)
                def _():
                    pltpu.make_async_copy(
                        w_ref.at[0, 0, lax.div(entry, 2)], target, sems.at[slot_at]
                    ).start()

                @pl.when(lax.rem(entry, 2) == 0)
                def _():
                    pltpu.make_async_copy(empty, target, sems.at[slot_at]).start()

    @pl.when(step == 0)
    def _():
        empty[...] = jnp.zeros_like(empty)
        for ahead in range(min(depth - 1, col_blocks // per_step)):
            load(jnp.int32(ahead))

    @pl.when(step + depth - 1 < steps)
    def _():
        load(step + depth - 1)

    slot_here = lax.rem(step, depth)
    pltpu.make_async_copy(held.at[slot_here], held.at[slot_here], sems.at[slot_here]).wait()
    out_ref[...] = held[slot_here]


def dense_tile(w_packed, code, row_blocks, col_blocks):
    blk = w_packed.shape[-1]
    per_step = group_of(col_blocks, 4)
    depth = 4
    wide = per_step * blk
    tall = row_blocks * blk
    return pl.pallas_call(
        functools.partial(dense_kernel, row_blocks, col_blocks, per_step, depth),
        out_shape=jax.ShapeDtypeStruct((tall, col_blocks * blk), w_packed.dtype),
        grid_spec=pltpu.PrefetchScalarGridSpec(
            num_scalar_prefetch=1,
            grid=(col_blocks // per_step,),
            in_specs=[pl.BlockSpec(memory_space=pl.ANY)],
            out_specs=pl.BlockSpec((tall, wide), lambda j, code: (0, j)),
            scratch_shapes=[
                pltpu.VMEM((depth, tall, wide), w_packed.dtype),
                pltpu.VMEM((blk, blk), w_packed.dtype),
                pltpu.SemaphoreType.DMA((depth,)),
            ],
        ),
        compiler_params=pltpu.CompilerParams(vmem_limit_bytes=vmem_limit),
        name="dense_tile",
    )(code, w_packed)


def forward_kernel(groups, rows, pick, x_ref, w_ref, keep_ref, send_ref, xs_ref):
    @pl.when(pl.program_id(0) == 0)
    def _():
        for t in range(groups):
            xs_ref[pl.ds(t * rows, rows), :] = x_ref[pick[t]]

    half = groups * rows // 2
    product = jnp.dot(xs_ref[...], w_ref[...], preferred_element_type=jnp.float32)
    keep_ref[...] = product[:half]
    send_ref[...] = product[half:].astype(jnp.bfloat16)


def forward(features, weight, pick):
    groups, rows, tall = features.shape
    hidden_here = weight.shape[1]
    wide = 128 * group_of(hidden_here // 128, 8)
    half = groups * rows // 2
    return pl.pallas_call(
        functools.partial(forward_kernel, groups, rows),
        out_shape=(
            jax.ShapeDtypeStruct((half, hidden_here), jnp.float32),
            jax.ShapeDtypeStruct((half, hidden_here), jnp.bfloat16),
            jax.ShapeDtypeStruct((groups * rows, tall), features.dtype),
        ),
        grid_spec=pltpu.PrefetchScalarGridSpec(
            num_scalar_prefetch=1,
            grid=(hidden_here // wide,),
            in_specs=[
                pl.BlockSpec((groups, rows, tall), lambda j, pick: (0, 0, 0)),
                pl.BlockSpec((tall, wide), lambda j, pick: (0, j)),
            ],
            out_specs=[
                pl.BlockSpec((half, wide), lambda j, pick: (0, j)),
                pl.BlockSpec((half, wide), lambda j, pick: (0, j)),
                pl.BlockSpec((groups * rows, tall), lambda j, pick: (0, 0)),
            ],
        ),
        compiler_params=pltpu.CompilerParams(vmem_limit_bytes=vmem_limit),
        name="forward",
    )(pick, features, weight)


def input_kernel(groups, rows, place, near_ref, far_ref, w_ref, out_ref, total):
    step = pl.program_id(0)

    @pl.when(step == 0)
    def _():
        total[...] = jnp.zeros_like(total)

    grad = jnp.concatenate([near_ref[...], far_ref[...]], axis=0)
    total[...] += lax.dot_general(
        grad, w_ref[...], (((1,), (1,)), ((), ())), preferred_element_type=jnp.float32
    )

    @pl.when(step == pl.num_programs(0) - 1)
    def _():
        for i in range(groups):
            start = pl.multiple_of(place[i] * rows, rows)
            out_ref[pl.ds(i * rows, rows), :] = total[pl.ds(start, rows), :]


def input_partial(near, far, weight, place):
    half, hidden_here = near.shape
    tall = weight.shape[0]
    groups = place.shape[0]
    rows = 2 * half // groups
    wide = 128 * group_of(hidden_here // 128, 8)
    return pl.pallas_call(
        functools.partial(input_kernel, groups, rows),
        out_shape=jax.ShapeDtypeStruct((2 * half, tall), jnp.float32),
        grid_spec=pltpu.PrefetchScalarGridSpec(
            num_scalar_prefetch=1,
            grid=(hidden_here // wide,),
            in_specs=[
                pl.BlockSpec((half, wide), lambda j, place: (0, j)),
                pl.BlockSpec((half, wide), lambda j, place: (0, j)),
                pl.BlockSpec((tall, wide), lambda j, place: (0, j)),
            ],
            out_specs=pl.BlockSpec((2 * half, tall), lambda j, place: (0, 0)),
            scratch_shapes=[pltpu.VMEM((2 * half, tall), jnp.float32)],
        ),
        compiler_params=pltpu.CompilerParams(vmem_limit_bytes=vmem_limit),
        name="input_partial",
    )(place, near, far, weight)


def weight_kernel(row_blocks, col_blocks, per_step, chunks, code, *refs):
    xs = refs[:chunks]
    grads = refs[chunks : 3 * chunks]
    out_ref, turned, made, sems = refs[3 * chunks :]
    step = pl.program_id(0)
    steps = pl.num_programs(0)
    blk = made.shape[-1]
    slot_here = lax.rem(step, 2)
    per_slot = row_blocks * per_step

    def finish(at):
        pltpu.make_async_copy(
            made.at[at], out_ref.at[0, 0, pl.ds(0, per_slot)], sems.at[at]
        ).wait()

    @pl.when(step == 0)
    def _():
        turned[...] = jnp.concatenate([x[...] for x in xs], axis=0).T

    @pl.when(step >= 2)
    def _():
        finish(slot_here)

    grad = jnp.concatenate([g[...] for g in grads], axis=0)
    product = jnp.dot(turned[...], grad, preferred_element_type=jnp.float32)
    for r in range(row_blocks):
        for c in range(per_step):
            entry = code[r * col_blocks + step * per_step + c]
            live = (lax.rem(entry, 2) == 1).astype(jnp.float32)
            block = product[r * blk : (r + 1) * blk, c * blk : (c + 1) * blk] * live
            made[slot_here, r * per_step + c] = block.astype(made.dtype)
            pltpu.make_async_copy(
                made.at[slot_here, r * per_step + c],
                out_ref.at[0, 0, lax.div(entry, 2)],
                sems.at[slot_here],
            ).start()

    @pl.when(step == steps - 1)
    def _():
        finish(slot_here)

        @pl.when(steps > 1)
        def _():
            finish(1 - slot_here)


def weight_gradient(features, grads, code, row_blocks, col_blocks, blk):
    chunks = len(features)
    tall = features[0].shape[1]
    tokens_all = sum(x.shape[0] for x in features)
    per_step = group_of(col_blocks, 4)
    wide = per_step * blk
    return pl.pallas_call(
        functools.partial(weight_kernel, row_blocks, col_blocks, per_step, chunks),
        out_shape=jax.ShapeDtypeStruct((1, 1, row_blocks * col_blocks, blk, blk), jnp.bfloat16),
        grid_spec=pltpu.PrefetchScalarGridSpec(
            num_scalar_prefetch=1,
            grid=(col_blocks // per_step,),
            in_specs=[pl.BlockSpec(x.shape, lambda j, code: (0, 0)) for x in features]
            + [pl.BlockSpec((g.shape[0], wide), lambda j, code: (0, j)) for g in grads],
            out_specs=pl.BlockSpec(memory_space=pl.ANY),
            scratch_shapes=[
                pltpu.VMEM((tall, tokens_all), jnp.bfloat16),
                pltpu.VMEM((2, row_blocks * per_step, blk, blk), jnp.bfloat16),
                pltpu.SemaphoreType.DMA((2,)),
            ],
        ),
        compiler_params=pltpu.CompilerParams(vmem_limit_bytes=vmem_limit),
        name="weight_gradient",
    )(code, *features, *grads)


def span_of(bits):
    span = [0]
    for bit in reversed(bits):
        span = span + [s ^ bit for s in span]
    return span


def swap(array, axis, size, bit):
    return lax.ppermute(array, axis, [(i, i ^ bit) for i in range(size)])


def on_device(tokens, w_packed, kept_rows, kept_cols, kept_count, grad_act):
    blk = w_packed.shape[-1]
    slot_count = w_packed.shape[2]
    tall = tokens.shape[1]
    hidden_here = grad_act.shape[1]
    row_blocks = tall // blk
    col_blocks = hidden_here // blk
    n_row = lax.axis_size("row")
    n_col = lax.axis_size("col")
    row_me = lax.axis_index("row")
    col_me = lax.axis_index("col")
    row_tokens = grad_act.shape[0]
    col_groups = tokens.shape[0] // row_tokens
    chunks = group_of(max(1, row_tokens // 16), chunk_goal)
    rows = row_tokens // chunks
    direct = n_col <= 8

    places = kept_rows[0, 0] * col_blocks + kept_cols[0, 0]
    slots = jnp.arange(slot_count, dtype=jnp.int32)
    coded = slots * 2 + (slots < kept_count[0, 0]).astype(jnp.int32)
    code = jnp.sum(jnp.where(places[None, :] == slots[:, None], coded[None, :], 0), axis=1)

    parts = tokens.reshape(col_groups, chunks, rows, tall)
    features = []
    for k in range(chunks):
        mine = parts[:, k]
        if direct:
            arrived = [mine] + [swap(mine, "col", n_col, m) for m in range(1, n_col)]
            features.append(jnp.concatenate(arrived, axis=0))
        else:
            features.append(lax.all_gather(mine, "col", axis=0, tiled=True))
    weight = dense_tile(w_packed, code, row_blocks, col_blocks)

    core_first = [1 << b for b in range(n_row.bit_length() - 1)]
    orders = [core_first, core_first[:1] + core_first[:0:-1]]
    picks, homes = [], []
    everyone = np.arange(n_row, dtype=np.int32)
    for bits in orders:
        owner = row_me ^ jnp.asarray(np.array(span_of(bits), np.int32))
        if direct:
            pick = (col_me ^ (owner // col_groups)) * col_groups + owner % col_groups
            home = (col_me ^ (everyone // col_groups)) * col_groups + everyone % col_groups
        else:
            pick = owner
            home = jnp.asarray(everyone)
        apart = row_me ^ home
        place = jnp.zeros_like(apart)
        for at, bit in enumerate(reversed(bits)):
            place = place + jnp.where((apart & bit) != 0, 1 << at, 0)
        picks.append(pick.astype(jnp.int32))
        homes.append(place.astype(jnp.int32))

    activations, near, far, sorted_features, input_grads = [], [], [], [], []
    for k in range(chunks):
        bits = orders[k % 2]
        keep, send, xs = forward(features[k], weight, picks[k % 2])
        sorted_features.append(xs)
        for at, bit in enumerate(bits):
            total = keep + swap(send, "row", n_row, bit).astype(jnp.float32)
            if at + 1 < len(bits):
                half = total.shape[0] // 2
                keep = total[:half]
                send = total[half:].astype(jnp.bfloat16)
        activation, slope_grad = gelu_pair(total, grad_act[k * rows : (k + 1) * rows])
        activations.append(activation)
        held = slope_grad
        for bit in reversed(bits):
            arrived = swap(held, "row", n_row, bit)
            if bit != bits[0]:
                held = jnp.concatenate([held, arrived], axis=0)
        near.append(held)
        far.append(arrived)
        partial = input_partial(held, arrived, weight, homes[k % 2])
        partial = partial.reshape(n_col, col_groups * rows, tall)
        if direct:
            total = partial[0]
            for m in range(1, n_col):
                total = total + swap(partial[m].astype(jnp.bfloat16), "col", n_col, m).astype(
                    jnp.float32
                )
        else:
            total = lax.psum_scatter(partial, "col", scatter_dimension=0, tiled=True)[0]
        input_grads.append(total.astype(jnp.bfloat16).reshape(col_groups, 1, rows, tall))
    weight_grad = weight_gradient(
        sorted_features,
        [g for pair in zip(near, far) for g in pair],
        code,
        row_blocks,
        col_blocks,
        blk,
    )
    activation = jnp.concatenate(activations, axis=0)
    input_grad = jnp.concatenate(input_grads, axis=1).reshape(tokens.shape)
    return (activation, input_grad, weight_grad)


def solution(mesh):
    placed = (
        P("col", "row"),
        P("row", "col", None, None, None),
        P("row", "col", None),
        P("row", "col", None),
        P("row", "col"),
        P("row", "col"),
    )
    return jax.shard_map(
        on_device,
        mesh=mesh,
        in_specs=placed,
        out_specs=(P("row", "col"), P("col", "row"), P("row", "col", None, None, None)),
        check_vma=False,
    )
```

```python
import functools

import jax
import jax.numpy as jnp
import numpy as np
from jax import lax
from jax.experimental import pallas as pl
from jax.experimental.pallas import tpu as pltpu
from jax.sharding import PartitionSpec as P

gelu_scale = 0.7978845608
gelu_cubic = 0.044715
token_parts = 2
column_parts = 2
vmem_limit = 20 * 1024 * 1024
in_vmem = pl.BlockSpec(memory_space=pltpu.VMEM)
in_smem = pl.BlockSpec(memory_space=pltpu.SMEM)
anywhere = pl.BlockSpec(memory_space=pltpu.HBM)


def gelu_pair(hidden, cotangent):
    inner = gelu_scale * (hidden + gelu_cubic * hidden * hidden * hidden)
    tangent = jnp.tanh(inner)
    activation = (0.5 * hidden * (1.0 + tangent)).astype(jnp.bfloat16)
    slope = 0.5 * (1.0 + tangent) + 0.5 * hidden * (1.0 - tangent * tangent) * gelu_scale * (
        1.0 + 3.0 * gelu_cubic * hidden * hidden
    )
    slope_grad = (cotangent.astype(jnp.float32) * slope).astype(jnp.bfloat16)
    return (activation, slope_grad)


def group_of(blocks, goal):
    return max(n for n in range(1, goal + 1) if blocks % n == 0)


def on_core(kernel, name, out_shape, out_specs, in_specs, operands, scratch=(), aliases=None):
    homes = {id(in_vmem): pltpu.VMEM, id(anywhere): pltpu.HBM}
    placed = [
        pltpu.with_memory_space_constraint(x, homes[id(spec)]) if id(spec) in homes else x
        for x, spec in zip(operands, in_specs)
    ]
    return pl.pallas_call(
        kernel,
        out_shape=out_shape,
        in_specs=in_specs,
        out_specs=out_specs,
        scratch_shapes=list(scratch),
        input_output_aliases=aliases or {},
        compiler_params=pltpu.CompilerParams(vmem_limit_bytes=vmem_limit),
        name=name,
    )(*placed)


def dense_kernel(row_blocks, col_blocks, code, w_ref, out_ref, empty, sem):
    blk = w_ref.shape[-1]
    empty[...] = jnp.zeros_like(empty)

    def load(at, carry):
        for r in range(row_blocks):
            entry = code[r * col_blocks + at]
            start = pl.multiple_of(at * blk, blk)
            target = out_ref.at[pl.ds(r * blk, blk), pl.ds(start, blk)]

            @pl.when(lax.rem(entry, 2) == 1)
            def _():
                pltpu.make_async_copy(w_ref.at[0, 0, lax.div(entry, 2)], target, sem).start()

            @pl.when(lax.rem(entry, 2) == 0)
            def _():
                pltpu.make_async_copy(empty, target, sem).start()

        return carry

    lax.fori_loop(0, col_blocks, load, 0)
    pltpu.make_async_copy(out_ref, out_ref, sem).wait()


def dense_tile(w_packed, code, row_blocks, col_blocks):
    blk = w_packed.shape[-1]
    return on_core(
        functools.partial(dense_kernel, row_blocks, col_blocks),
        "dense_tile",
        pltpu.VMEM((row_blocks * blk, col_blocks * blk), w_packed.dtype),
        in_vmem,
        [in_smem, anywhere],
        (code, w_packed),
        scratch=[pltpu.VMEM((blk, blk), w_packed.dtype), pltpu.SemaphoreType.DMA],
    )


def arrange_kernel(groups, rows, pieces, pick, *refs):
    out_ref, all_ref = refs[pieces:]
    each = groups // pieces
    for m in range(pieces):
        for j in range(each):
            all_ref[m * each + j] = refs[m][j]
    for t in range(groups):
        out_ref[pl.ds(t * rows, rows), :] = all_ref[pick[t]]


def arrange(pieces, pick):
    groups = pick.shape[0]
    rows, tall = pieces[0].shape[1:]
    return on_core(
        functools.partial(arrange_kernel, groups, rows, len(pieces)),
        "arrange",
        pltpu.VMEM((groups * rows, tall), pieces[0].dtype),
        in_vmem,
        [in_smem] + [in_vmem] * len(pieces),
        (pick, *pieces),
        scratch=[pltpu.VMEM((groups, rows, tall), pieces[0].dtype)],
    )


def forward_kernel(first, wide, x_ref, w_ref, keep_ref, send_ref):
    half, width = keep_ref.shape
    for at in range(0, width, wide):
        product = jnp.dot(
            x_ref[...], w_ref[:, first + at : first + at + wide], preferred_element_type=jnp.float32
        )
        keep_ref[:, at : at + wide] = product[:half]
        send_ref[:, at : at + wide] = product[half:].astype(jnp.bfloat16)


def forward(features, weight, first, width):
    half = features.shape[0] // 2
    wide = 128 * group_of(width // 128, 4)
    return on_core(
        functools.partial(forward_kernel, first, wide),
        "forward",
        (pltpu.VMEM((half, width), jnp.float32), pltpu.VMEM((half, width), jnp.bfloat16)),
        (in_vmem, in_vmem),
        [in_vmem, in_vmem],
        (features, weight),
    )


def gelu_kernel(top, first, keep_ref, arrived_ref, cotangent_ref, activation_ref, slope_ref):
    rows, width = keep_ref.shape
    hidden = keep_ref[...] + arrived_ref[...].astype(jnp.float32)
    cotangent = cotangent_ref[top : top + rows, first : first + width]
    activation_ref[...], slope_ref[...] = gelu_pair(hidden, cotangent)


def gelu(keep, arrived, cotangent, top, first):
    out = pltpu.VMEM(keep.shape, jnp.bfloat16)
    return on_core(
        functools.partial(gelu_kernel, top, first),
        "gelu",
        (out, out),
        (in_vmem, in_vmem),
        [in_vmem] * 3,
        (keep, arrived, cotangent),
    )


def input_kernel(first, groups, has_before, last, *refs):
    place = refs[0]
    refs = refs[1:]
    near_ref, far_ref, w_ref = refs[:3]
    refs = refs[3:]
    half, width = near_ref.shape
    rows = 2 * half // groups
    tall = w_ref.shape[0]
    wide = 128 * group_of(tall // 128, 2)
    if has_before:
        before = refs[0]
        refs = refs[1:]
    total = refs[-1] if last else refs[0]
    for at in range(0, tall, wide):
        part = w_ref[at : at + wide, first : first + width]
        for side, grad_ref in enumerate((near_ref, far_ref)):
            product = lax.dot_general(
                grad_ref[...], part, (((1,), (1,)), ((), ())), preferred_element_type=jnp.float32
            )
            spot = (slice(side * half, (side + 1) * half), slice(at, at + wide))
            total[spot] = product + before[spot] if has_before else product
    if last:
        full_ref, short_ref = refs[:2]
        for i in range(groups):
            start = pl.multiple_of(place[i] * rows, rows)
            block = total[pl.ds(start, rows), :]
            full_ref[pl.ds(i * rows, rows), :] = block
            short_ref[pl.ds(i * rows, rows), :] = block.astype(jnp.bfloat16)


def input_partial(near, far, weight, first, place, before, last):
    half, width = near.shape
    tall = weight.shape[0]
    full = pltpu.VMEM((2 * half, tall), jnp.float32)
    short = pltpu.VMEM((2 * half, tall), jnp.bfloat16)
    has_before = before is not None
    return on_core(
        functools.partial(input_kernel, first, place.shape[0], has_before, last),
        "input_partial",
        (full, short) if last else full,
        (in_vmem, in_vmem) if last else in_vmem,
        [in_smem] + [in_vmem] * (4 if has_before else 3),
        (place, near, far, weight) + ((before,) if has_before else ()),
        scratch=[full] if last else [],
    )


def weight_kernel(row_blocks, col_blocks, first, parts, has_before, code, *refs):
    turned = refs[:parts]
    grads = refs[parts : 3 * parts]
    out_ref, made, sem = refs[3 * parts + has_before :]
    blk = made.shape[-1]
    width = grads[0].shape[1]
    here = width // blk
    per_step = group_of(here, 2)
    wide = per_step * blk
    for j in range(here // per_step):
        product = None
        for k in range(parts):
            grad = jnp.concatenate(
                [g[:, j * wide : (j + 1) * wide] for g in grads[2 * k : 2 * k + 2]], axis=0
            )
            term = jnp.dot(turned[k][...], grad, preferred_element_type=jnp.float32)
            product = term if product is None else product + term
        for r in range(row_blocks):
            for c in range(per_step):
                entry = code[r * col_blocks + first // blk + j * per_step + c]
                live = lax.rem(entry, 2).astype(jnp.float32)
                at = (j * row_blocks + r) * per_step + c
                block = product[r * blk : (r + 1) * blk, c * blk : (c + 1) * blk] * live
                made[at] = block.astype(made.dtype)
                pltpu.make_async_copy(
                    made.at[at], out_ref.at[0, 0, lax.div(entry, 2)], sem
                ).start()
    pltpu.make_async_copy(made, out_ref.at[0, 0, pl.ds(0, made.shape[0])], sem).wait()


def weight_gradient(turned, grads, code, first, row_blocks, col_blocks, blk, before):
    parts = len(turned)
    has_before = before is not None
    here = row_blocks * grads[0].shape[1] // blk
    arrays = [*turned, *grads]
    return on_core(
        functools.partial(weight_kernel, row_blocks, col_blocks, first, parts, has_before),
        "weight_gradient",
        jax.ShapeDtypeStruct((1, 1, row_blocks * col_blocks, blk, blk), jnp.bfloat16),
        anywhere,
        [in_smem] + [in_vmem] * len(arrays) + [anywhere] * has_before,
        (code, *arrays) + ((before,) if has_before else ()),
        scratch=[pltpu.VMEM((here, blk, blk), jnp.bfloat16), pltpu.SemaphoreType.DMA],
        aliases={1 + len(arrays): 0} if has_before else None,
    )


def swap(array, axis, size, bit):
    return lax.ppermute(array, axis, [(i, i ^ bit) for i in range(size)])


def on_device(tokens, w_packed, kept_rows, kept_cols, kept_count, grad_act):
    blk = w_packed.shape[-1]
    slot_count = w_packed.shape[2]
    tall = tokens.shape[1]
    row_tokens, hidden_here = grad_act.shape
    row_blocks = tall // blk
    col_blocks = hidden_here // blk
    n_row = lax.axis_size("row")
    n_col = lax.axis_size("col")
    row_me = lax.axis_index("row")
    col_me = lax.axis_index("col")
    col_groups = tokens.shape[0] // row_tokens
    parts = group_of(max(1, row_tokens // 16), token_parts)
    rows = row_tokens // parts
    slabs = group_of(col_blocks, column_parts)
    width = hidden_here // slabs
    direct = n_col <= 8

    places = kept_rows[0, 0] * col_blocks + kept_cols[0, 0]
    slots = jnp.arange(slot_count, dtype=jnp.int32)
    coded = slots * 2 + (slots < kept_count[0, 0]).astype(jnp.int32)
    code = jnp.sum(jnp.where(places[None, :] == slots[:, None], coded[None, :], 0), axis=1)

    apart = row_me ^ (col_me * col_groups) if direct else row_me
    everyone = np.arange(n_row)
    order = np.concatenate([everyone[::2], everyone[1::2]]).astype(np.int32)
    pick = (jnp.asarray(order) ^ apart).astype(jnp.int32)
    distance = jnp.asarray(everyone.astype(np.int32)) ^ apart
    place = ((distance & 1) * (n_row // 2) + (distance >> 1)).astype(jnp.int32)

    mine = tokens.reshape(col_groups, parts, rows, tall)
    pieces = []
    for k in range(parts):
        if direct:
            pieces.append(
                [mine[:, k]] + [swap(mine[:, k], "col", n_col, m) for m in range(1, n_col)]
            )
        else:
            pieces.append([lax.all_gather(mine[:, k], "col", axis=0, tiled=True)])
    weight = dense_tile(w_packed, code, row_blocks, col_blocks)
    features = [arrange(p, pick) for p in pieces]
    turned = [x.T for x in features]

    far_bits = [1 << b for b in range(1, n_row.bit_length() - 1)]
    activations = [[None] * slabs for _ in range(parts)]
    grads = [[None] * slabs for _ in range(parts)]
    input_grads = []
    weight_grad = None
    for k in range(parts):
        before = None
        for c in range(slabs):
            first = c * width
            keep, send = forward(features[k], weight, first, width)
            total = keep + swap(send, "row", n_row, 1).astype(jnp.float32)
            left = far_bits[::-1]
            total = total.reshape((2,) * len(left) + (rows, width))
            path = far_bits if (k * slabs + c) % 2 == 0 else left
            for bit in path:
                axis = left.index(bit)
                keep = lax.index_in_dim(total, 0, axis, keepdims=False)
                send = lax.index_in_dim(total, 1, axis, keepdims=False).astype(jnp.bfloat16)
                flat = send.reshape(-1, width)
                arrived = swap(flat, "row", n_row, bit).reshape(send.shape)
                total = keep + arrived.astype(jnp.float32)
                left = [b for b in left if b != bit]
            activation, slope_grad = gelu(keep, arrived, grad_act, k * rows, first)
            activations[k][c] = activation
            near = slope_grad
            held = []
            for bit in reversed(path):
                flat = near.reshape(-1, width)
                arrived = swap(flat, "row", n_row, bit).reshape(near.shape)
                held = sorted(held + [bit], reverse=True)
                near = jnp.stack([near, arrived], axis=held.index(bit))
            near = near.reshape(-1, width)
            far = swap(near, "row", n_row, 1)
            grads[k][c] = (near, far)
            before = input_partial(near, far, weight, first, place, before, c + 1 == slabs)
            if k + 1 == parts:
                weight_grad = weight_gradient(
                    turned,
                    [g for part in grads for g in part[c]],
                    code,
                    first,
                    row_blocks,
                    col_blocks,
                    blk,
                    weight_grad,
                )
        full, short = (x.reshape(n_col, col_groups * rows, tall) for x in before)
        if direct:
            total = full[0]
            for m in range(1, n_col):
                total = total + swap(short[m], "col", n_col, m).astype(jnp.float32)
        else:
            total = lax.psum_scatter(full, "col", scatter_dimension=0, tiled=True)[0]
        input_grads.append(total.astype(jnp.bfloat16).reshape(col_groups, 1, rows, tall))
    activation = jnp.concatenate([jnp.concatenate(a, axis=1) for a in activations], axis=0)
    input_grad = jnp.concatenate(input_grads, axis=1).reshape(tokens.shape)
    return (activation, input_grad, weight_grad)


def solution(mesh):
    placed = (
        P("col", "row"),
        P("row", "col", None, None, None),
        P("row", "col", None),
        P("row", "col", None),
        P("row", "col"),
        P("row", "col"),
    )
    return jax.shard_map(
        on_device,
        mesh=mesh,
        in_specs=placed,
        out_specs=(P("row", "col"), P("col", "row"), P("row", "col", None, None, None)),
        check_vma=False,
    )
```

```python
import functools

import jax
import jax.numpy as jnp
import numpy as np
from jax import lax
from jax.experimental import pallas as pl
from jax.experimental.pallas import tpu as pltpu
from jax.sharding import PartitionSpec as P

gelu_scale = 0.7978845608
gelu_cubic = 0.044715
token_parts = 2
column_parts = 2
vmem_limit = 16 * 1024 * 1024
in_vmem = pl.BlockSpec(memory_space=pltpu.VMEM)
in_smem = pl.BlockSpec(memory_space=pltpu.SMEM)
anywhere = pl.BlockSpec(memory_space=pltpu.HBM)


def gelu_pair(hidden, cotangent):
    inner = gelu_scale * (hidden + gelu_cubic * hidden * hidden * hidden)
    tangent = jnp.tanh(inner)
    activation = (0.5 * hidden * (1.0 + tangent)).astype(jnp.bfloat16)
    slope = 0.5 * (1.0 + tangent) + 0.5 * hidden * (1.0 - tangent * tangent) * gelu_scale * (
        1.0 + 3.0 * gelu_cubic * hidden * hidden
    )
    slope_grad = (cotangent.astype(jnp.float32) * slope).astype(jnp.bfloat16)
    return (activation, slope_grad)


def group_of(blocks, goal):
    return max(n for n in range(1, goal + 1) if blocks % n == 0)


class Core:
    def __init__(self):
        self.turn = None

    def __call__(self, kernel, name, out_shape, out_specs, in_specs, operands, scratch=(), aliases=None):
        homes = {id(in_vmem): pltpu.VMEM, id(anywhere): pltpu.HBM}
        in_specs, operands = list(in_specs), list(operands)
        if self.turn is not None:
            in_specs.append(in_vmem)
            operands.append(self.turn)
        taken = len(operands)
        given = len(out_shape)
        extra = self.turn is not None

        def body(*refs):
            refs[taken + given][...] = jnp.zeros((8, 128), jnp.float32)
            kernel(*refs[: taken - extra], *refs[taken : taken + given], *refs[taken + given + 1 :])

        placed = [
            pltpu.with_memory_space_constraint(x, homes[id(spec)]) if id(spec) in homes else x
            for x, spec in zip(operands, in_specs)
        ]
        *out, self.turn = pl.pallas_call(
            body,
            out_shape=[*out_shape, pltpu.VMEM((8, 128), jnp.float32)],
            in_specs=in_specs,
            out_specs=[*out_specs, in_vmem],
            scratch_shapes=list(scratch),
            input_output_aliases=aliases or {},
            compiler_params=pltpu.CompilerParams(vmem_limit_bytes=vmem_limit),
            cost_estimate=pl.CostEstimate(flops=1, transcendentals=0, bytes_accessed=1),
            name=name,
        )(*placed)
        return out


def dense_kernel(row_blocks, col_blocks, code, w_ref, out_ref, empty, sem):
    blk = w_ref.shape[-1]
    empty[...] = jnp.zeros_like(empty)

    def load(at, carry):
        for r in range(row_blocks):
            entry = code[r * col_blocks + at]
            start = pl.multiple_of(at * blk, blk)
            target = out_ref.at[pl.ds(r * blk, blk), pl.ds(start, blk)]

            @pl.when(lax.rem(entry, 2) == 1)
            def _():
                pltpu.make_async_copy(w_ref.at[0, 0, lax.div(entry, 2)], target, sem).start()

            @pl.when(lax.rem(entry, 2) == 0)
            def _():
                pltpu.make_async_copy(empty, target, sem).start()

        return carry

    lax.fori_loop(0, col_blocks, load, 0)
    pltpu.make_async_copy(out_ref, out_ref, sem).wait()


def dense_tile(core, w_packed, code, row_blocks, col_blocks):
    blk = w_packed.shape[-1]
    [weight] = core(
        functools.partial(dense_kernel, row_blocks, col_blocks),
        "dense_tile",
        [pltpu.VMEM((row_blocks * blk, col_blocks * blk), w_packed.dtype)],
        [in_vmem],
        [in_smem, anywhere],
        (code, w_packed),
        scratch=[pltpu.VMEM((blk, blk), w_packed.dtype), pltpu.SemaphoreType.DMA],
    )
    return weight


def arrange_kernel(groups, rows, pieces, pick, *refs):
    out_ref, turned_ref, all_ref = refs[pieces:]
    each = groups // pieces
    for m in range(pieces):
        for j in range(each):
            all_ref[m * each + j] = refs[m][j]
    for t in range(groups):
        out_ref[pl.ds(t * rows, rows), :] = all_ref[pick[t]]
    turned_ref[...] = out_ref[...].T


def arrange(core, pieces, pick):
    groups = pick.shape[0]
    rows, tall = pieces[0].shape[1:]
    kind = pieces[0].dtype
    return core(
        functools.partial(arrange_kernel, groups, rows, len(pieces)),
        "arrange",
        [pltpu.VMEM((groups * rows, tall), kind), pltpu.VMEM((tall, groups * rows), kind)],
        [in_vmem, in_vmem],
        [in_smem] + [in_vmem] * len(pieces),
        (pick, *pieces),
        scratch=[pltpu.VMEM((groups, rows, tall), kind)],
    )


def forward_kernel(first, wide, x_ref, w_ref, keep_ref, send_ref):
    half, width = keep_ref.shape
    for at in range(0, width, wide):
        product = jnp.dot(
            x_ref[...], w_ref[:, first + at : first + at + wide], preferred_element_type=jnp.float32
        )
        keep_ref[:, at : at + wide] = product[:half]
        send_ref[:, at : at + wide] = product[half:].astype(jnp.bfloat16)


def forward(core, features, weight, first, width):
    half = features.shape[0] // 2
    wide = 128 * group_of(width // 128, 4)
    return core(
        functools.partial(forward_kernel, first, wide),
        "forward",
        [pltpu.VMEM((half, width), jnp.float32), pltpu.VMEM((half, width), jnp.bfloat16)],
        [in_vmem, in_vmem],
        [in_vmem, in_vmem],
        (features, weight),
    )


def sides(left, bit):
    at = len(left) - 1 - left.index(bit)
    names = range(1 << len(left))
    return [g for g in names if not g >> at & 1], [g for g in names if g >> at & 1]


def add_kernel(rows, stay, leave, keep_ref, arrived_ref, next_ref, send_ref):
    for out_ref, groups in ((next_ref, stay), (send_ref, leave)):
        for at, g in enumerate(groups):
            here = slice(g * rows, (g + 1) * rows)
            total = keep_ref[here, :] + arrived_ref[here, :].astype(jnp.float32)
            out_ref[at * rows : (at + 1) * rows, :] = total.astype(out_ref.dtype)


def add_step(core, keep, arrived, left, bit):
    rows = keep.shape[0] >> len(left)
    half = (keep.shape[0] // 2, keep.shape[1])
    return core(
        functools.partial(add_kernel, rows, *sides(left, bit)),
        "add_step",
        [pltpu.VMEM(half, jnp.float32), pltpu.VMEM(half, jnp.bfloat16)],
        [in_vmem, in_vmem],
        [in_vmem, in_vmem],
        (keep, arrived),
    )


def join_kernel(rows, stay, come, near_ref, arrived_ref, out_ref):
    for in_ref, groups in ((near_ref, stay), (arrived_ref, come)):
        for at, g in enumerate(groups):
            out_ref[g * rows : (g + 1) * rows, :] = in_ref[at * rows : (at + 1) * rows, :]


def join_step(core, near, arrived, held, bit):
    rows = 2 * near.shape[0] >> len(held)
    [out] = core(
        functools.partial(join_kernel, rows, *sides(held, bit)),
        "join_step",
        [pltpu.VMEM((2 * near.shape[0], near.shape[1]), near.dtype)],
        [in_vmem],
        [in_vmem, in_vmem],
        (near, arrived),
    )
    return out


def gelu_kernel(top, first, keep_ref, arrived_ref, cotangent_ref, activation_ref, slope_ref):
    rows, width = keep_ref.shape
    hidden = keep_ref[...] + arrived_ref[...].astype(jnp.float32)
    cotangent = cotangent_ref[top : top + rows, first : first + width]
    activation_ref[...], slope_ref[...] = gelu_pair(hidden, cotangent)


def gelu(core, keep, arrived, cotangent, top, first):
    out = pltpu.VMEM(keep.shape, jnp.bfloat16)
    return core(
        functools.partial(gelu_kernel, top, first),
        "gelu",
        [out, out],
        [in_vmem, in_vmem],
        [in_vmem] * 3,
        (keep, arrived, cotangent),
    )


def input_kernel(first, groups, has_before, finished, given, place, near_ref, far_ref, w_ref, *refs):
    half, width = near_ref.shape
    rows = 2 * half // groups
    tall = w_ref.shape[0]
    before = refs[0] if has_before else None
    outs = refs[has_before : has_before + given]
    scratch = refs[has_before + given :]
    turned = scratch[0]
    total = scratch[1] if finished else outs[0]
    wide = 128 * group_of(width // 128, 4)
    for at in range(0, width, wide):
        here = slice(at, at + wide)
        grad = jnp.concatenate([near_ref[:, here], far_ref[:, here]], axis=0)
        turned[here, :] = grad.T
    high = 128 * group_of(tall // 128, 4)
    for at in range(0, tall, high):
        here = slice(at, at + high)
        product = jnp.dot(
            w_ref[here, first : first + width], turned[...], preferred_element_type=jnp.float32
        )
        total[here, :] = product + before[here, :] if has_before else product
    if finished:
        upright = scratch[2]
        upright[...] = total[...].T
        each = groups // given
        for i in range(groups):
            start = pl.multiple_of(place[i] * rows, rows)
            out_ref = outs[i // each]
            at = i % each * rows
            out_ref[at : at + rows, :] = upright[pl.ds(start, rows), :].astype(out_ref.dtype)


def input_partial(core, near, far, weight, first, place, before, pieces):
    half, width = near.shape
    tall = weight.shape[0]
    both = 2 * half
    if pieces:
        outs = [pltpu.VMEM((both // pieces, tall), jnp.float32)]
        outs += [pltpu.VMEM((both // pieces, tall), jnp.bfloat16)] * (pieces - 1)
    else:
        outs = [pltpu.VMEM((tall, both), jnp.float32)]
    has_before = before is not None
    scratch = [pltpu.VMEM((width, both), near.dtype)]
    if pieces:
        scratch += [pltpu.VMEM((tall, both), jnp.float32), pltpu.VMEM((both, tall), jnp.float32)]
    return core(
        functools.partial(
            input_kernel, first, place.shape[0], has_before, pieces > 0, len(outs)
        ),
        "input_partial",
        outs,
        [in_vmem] * len(outs),
        [in_smem] + [in_vmem] * (4 if has_before else 3),
        (place, near, far, weight) + ((before,) if has_before else ()),
        scratch=scratch,
    )


def weight_kernel(row_blocks, col_blocks, first, parts, has_before, code, *refs):
    turned = refs[:parts]
    grads = refs[parts : 3 * parts]
    out_ref, made, sem = refs[3 * parts + has_before :]
    blk = made.shape[-1]
    width = grads[0].shape[1]
    here = width // blk
    per_step = group_of(here, 2)
    wide = per_step * blk
    for j in range(here // per_step):
        features = jnp.concatenate([t[...] for t in turned], axis=1)
        grad = jnp.concatenate([g[:, j * wide : (j + 1) * wide] for g in grads], axis=0)
        product = jnp.dot(features, grad, preferred_element_type=jnp.float32)
        for r in range(row_blocks):
            for c in range(per_step):
                entry = code[r * col_blocks + first // blk + j * per_step + c]
                live = lax.rem(entry, 2).astype(jnp.float32)
                at = (j * row_blocks + r) * per_step + c
                block = product[r * blk : (r + 1) * blk, c * blk : (c + 1) * blk] * live
                made[at] = block.astype(made.dtype)
                pltpu.make_async_copy(
                    made.at[at], out_ref.at[0, 0, lax.div(entry, 2)], sem
                ).start()
    pltpu.make_async_copy(made, out_ref.at[0, 0, pl.ds(0, made.shape[0])], sem).wait()


def weight_gradient(core, turned, grads, code, first, row_blocks, col_blocks, blk, before):
    parts = len(turned)
    has_before = before is not None
    here = row_blocks * grads[0].shape[1] // blk
    arrays = [*turned, *grads]
    [out] = core(
        functools.partial(weight_kernel, row_blocks, col_blocks, first, parts, has_before),
        "weight_gradient",
        [jax.ShapeDtypeStruct((1, 1, row_blocks * col_blocks, blk, blk), jnp.bfloat16)],
        [anywhere],
        [in_smem] + [in_vmem] * len(arrays) + [anywhere] * has_before,
        (code, *arrays) + ((before,) if has_before else ()),
        scratch=[pltpu.VMEM((here, blk, blk), jnp.bfloat16), pltpu.SemaphoreType.DMA],
        aliases={1 + len(arrays): 0} if has_before else None,
    )
    return out


def swap(array, axis, size, bit):
    return lax.ppermute(array, axis, [(i, i ^ bit) for i in range(size)])


def on_device(tokens, w_packed, kept_rows, kept_cols, kept_count, grad_act):
    blk = w_packed.shape[-1]
    slot_count = w_packed.shape[2]
    tall = tokens.shape[1]
    row_tokens, hidden_here = grad_act.shape
    row_blocks = tall // blk
    col_blocks = hidden_here // blk
    n_row = lax.axis_size("row")
    n_col = lax.axis_size("col")
    row_me = lax.axis_index("row")
    col_me = lax.axis_index("col")
    col_groups = tokens.shape[0] // row_tokens
    parts = group_of(max(1, row_tokens // 16), token_parts)
    rows = row_tokens // parts
    slabs = group_of(col_blocks, column_parts)
    width = hidden_here // slabs
    direct = n_col <= 8
    core = Core()

    places = kept_rows[0, 0] * col_blocks + kept_cols[0, 0]
    slots = jnp.arange(slot_count, dtype=jnp.int32)
    coded = slots * 2 + (slots < kept_count[0, 0]).astype(jnp.int32)
    code = jnp.sum(jnp.where(places[None, :] == slots[:, None], coded[None, :], 0), axis=1)

    apart = row_me ^ (col_me * col_groups) if direct else row_me
    everyone = np.arange(n_row)
    order = np.concatenate([everyone[::2], everyone[1::2]]).astype(np.int32)
    pick = (jnp.asarray(order) ^ apart).astype(jnp.int32)
    distance = jnp.asarray(everyone.astype(np.int32)) ^ apart
    place = ((distance & 1) * (n_row // 2) + (distance >> 1)).astype(jnp.int32)

    mine = tokens.reshape(col_groups, parts, rows, tall)
    pieces = []
    for k in range(parts):
        if direct:
            pieces.append(
                [mine[:, k]] + [swap(mine[:, k], "col", n_col, m) for m in range(1, n_col)]
            )
        else:
            pieces.append([lax.all_gather(mine[:, k], "col", axis=0, tiled=True)])
    weight = dense_tile(core, w_packed, code, row_blocks, col_blocks)

    far_bits = [1 << b for b in range(1, n_row.bit_length() - 1)]
    units = [(k, c) for k in range(parts) for c in range(slabs)]
    paths = [far_bits if at % 2 == 0 else far_bits[::-1] for at in range(len(units))]
    state = {}
    full, turned = {}, {}
    activations, sums, input_grads = {}, {}, {}

    def begin(k, c, path):
        if c == 0:
            full[k], turned[k] = arrange(core, pieces[k], pick)
        keep, send = forward(core, full[k], weight, c * width, width)
        state[k, c] = (keep, swap(send, "row", n_row, 1))

    def add(at, k, c, path):
        left = sorted(path[at:], reverse=True)
        keep, send = add_step(core, *state[k, c], left, path[at])
        state[k, c] = (keep, swap(send, "row", n_row, path[at]))

    def bend(k, c, path):
        activations[k, c], near = gelu(core, *state[k, c], grad_act, k * rows, c * width)
        state[k, c] = (near, swap(near, "row", n_row, ([1] + path)[-1]))

    def join(at, k, c, path):
        held = sorted(path[at:], reverse=True)
        near = join_step(core, *state[k, c], held, path[at])
        state[k, c] = (near, swap(near, "row", n_row, ([1] + path)[at]))

    def finish(k, c, path):
        last = c + 1 == slabs
        cut = (n_col if direct else 1) * last
        found = input_partial(
            core, *state[k, c], weight, c * width, place, sums.get((k, c - 1)), cut
        )
        sums[k, c] = found[0]
        if last and direct:
            total = found[0]
            for m in range(1, n_col):
                total = total + swap(found[m], "col", n_col, m).astype(jnp.float32)
        elif last:
            total = found[0].reshape(n_col, col_groups * rows, tall)
            total = lax.psum_scatter(total, "col", scatter_dimension=0, tiled=True)[0]
        if last:
            total = total.astype(jnp.bfloat16)
            input_grads[k] = total.reshape(col_groups, 1, rows, tall)

    hops = len(far_bits)
    stages = [begin] + [functools.partial(add, at) for at in range(hops)] + [bend]
    stages += [functools.partial(join, at) for at in reversed(range(hops))] + [finish]
    plan = []
    if parts == 2 and hops == 2:
        plan = [(0, 0), (0, 1), (0, 2), (1, 0), (1, 1), (0, 3), (1, 2), (0, 4), (1, 3)]
        plan += [(0, 5), (1, 4), (0, 6), (1, 5), (1, 6)]
    else:
        plan = [(k, at) for at in range(len(stages)) for k in range(parts)]
    for k, at in plan:
        for c in range(slabs):
            stages[at](k, c, paths[units.index((k, c))])
    weight_grad = None
    for c in range(slabs):
        weight_grad = weight_gradient(
            core,
            [turned[k] for k in range(parts)],
            [g for k in range(parts) for g in state[k, c]],
            code,
            c * width,
            row_blocks,
            col_blocks,
            blk,
            weight_grad,
        )
    activation = jnp.concatenate(
        [jnp.concatenate([activations[k, c] for c in range(slabs)], axis=1) for k in range(parts)],
        axis=0,
    )
    input_grad = jnp.concatenate([input_grads[k] for k in range(parts)], axis=1).reshape(tokens.shape)
    return (activation, input_grad, weight_grad)


def solution(mesh):
    placed = (
        P("col", "row"),
        P("row", "col", None, None, None),
        P("row", "col", None),
        P("row", "col", None),
        P("row", "col"),
        P("row", "col"),
    )
    return jax.shard_map(
        on_device,
        mesh=mesh,
        in_specs=placed,
        out_specs=(P("row", "col"), P("col", "row"), P("row", "col", None, None, None)),
        check_vma=False,
    )
```

```python
import functools

import jax
import jax.numpy as jnp
import numpy as np
from jax import lax
from jax.experimental import pallas as pl
from jax.experimental.pallas import tpu as pltpu
from jax.sharding import PartitionSpec as P

gelu_scale = 0.7978845608
gelu_cubic = 0.044715
token_split = (3, 1)
column_parts = 2
vmem_limit = 16 * 1024 * 1024
in_vmem = pl.BlockSpec(memory_space=pltpu.VMEM)
in_smem = pl.BlockSpec(memory_space=pltpu.SMEM)
anywhere = pl.BlockSpec(memory_space=pltpu.HBM)


def gelu_pair(hidden, cotangent):
    inner = gelu_scale * (hidden + gelu_cubic * hidden * hidden * hidden)
    tangent = jnp.tanh(inner)
    activation = (0.5 * hidden * (1.0 + tangent)).astype(jnp.bfloat16)
    slope = 0.5 * (1.0 + tangent) + 0.5 * hidden * (1.0 - tangent * tangent) * gelu_scale * (
        1.0 + 3.0 * gelu_cubic * hidden * hidden
    )
    slope_grad = (cotangent.astype(jnp.float32) * slope).astype(jnp.bfloat16)
    return (activation, slope_grad)


def group_of(blocks, goal):
    return max(n for n in range(1, goal + 1) if blocks % n == 0)


class Core:
    def __init__(self):
        self.turn = None

    def __call__(self, kernel, name, out_shape, out_specs, in_specs, operands, scratch=(), aliases=None):
        homes = {id(in_vmem): pltpu.VMEM, id(anywhere): pltpu.HBM}
        in_specs, operands = list(in_specs), list(operands)
        if self.turn is not None:
            in_specs.append(in_vmem)
            operands.append(self.turn)
        taken = len(operands)
        given = len(out_shape)
        extra = self.turn is not None

        def body(*refs):
            refs[taken + given][...] = jnp.zeros((8, 128), jnp.float32)
            kernel(*refs[: taken - extra], *refs[taken : taken + given], *refs[taken + given + 1 :])

        placed = [
            pltpu.with_memory_space_constraint(x, homes[id(spec)]) if id(spec) in homes else x
            for x, spec in zip(operands, in_specs)
        ]
        *out, self.turn = pl.pallas_call(
            body,
            out_shape=[*out_shape, pltpu.VMEM((8, 128), jnp.float32)],
            in_specs=in_specs,
            out_specs=[*out_specs, in_vmem],
            scratch_shapes=list(scratch),
            input_output_aliases=aliases or {},
            compiler_params=pltpu.CompilerParams(vmem_limit_bytes=vmem_limit),
            cost_estimate=pl.CostEstimate(flops=1, transcendentals=0, bytes_accessed=1),
            name=name,
        )(*placed)
        return out


def dense_kernel(row_blocks, col_blocks, code, w_ref, out_ref, empty, sem):
    blk = w_ref.shape[-1]
    empty[...] = jnp.zeros_like(empty)

    def load(at, carry):
        for r in range(row_blocks):
            entry = code[r * col_blocks + at]
            start = pl.multiple_of(at * blk, blk)
            target = out_ref.at[pl.ds(r * blk, blk), pl.ds(start, blk)]

            @pl.when(lax.rem(entry, 2) == 1)
            def _():
                pltpu.make_async_copy(w_ref.at[0, 0, lax.div(entry, 2)], target, sem).start()

            @pl.when(lax.rem(entry, 2) == 0)
            def _():
                pltpu.make_async_copy(empty, target, sem).start()

        return carry

    lax.fori_loop(0, col_blocks, load, 0)
    pltpu.make_async_copy(out_ref, out_ref, sem).wait()


def dense_tile(core, w_packed, code, row_blocks, col_blocks):
    blk = w_packed.shape[-1]
    [weight] = core(
        functools.partial(dense_kernel, row_blocks, col_blocks),
        "dense_tile",
        [pltpu.VMEM((row_blocks * blk, col_blocks * blk), w_packed.dtype)],
        [in_vmem],
        [in_smem, anywhere],
        (code, w_packed),
        scratch=[pltpu.VMEM((blk, blk), w_packed.dtype), pltpu.SemaphoreType.DMA],
    )
    return weight


def arrange_kernel(groups, rows, pieces, pick, *refs):
    out_ref, turned_ref, all_ref = refs[pieces:]
    each = groups // pieces
    for m in range(pieces):
        for j in range(each):
            all_ref[m * each + j] = refs[m][j]
    for t in range(groups):
        out_ref[pl.ds(t * rows, rows), :] = all_ref[pick[t]]
    turned_ref[...] = out_ref[...].T


def arrange(core, pieces, pick):
    groups = pick.shape[0]
    rows, tall = pieces[0].shape[1:]
    kind = pieces[0].dtype
    return core(
        functools.partial(arrange_kernel, groups, rows, len(pieces)),
        "arrange",
        [pltpu.VMEM((groups * rows, tall), kind), pltpu.VMEM((tall, groups * rows), kind)],
        [in_vmem, in_vmem],
        [in_smem] + [in_vmem] * len(pieces),
        (pick, *pieces),
        scratch=[pltpu.VMEM((groups, rows, tall), kind)],
    )


def forward_kernel(first, wide, x_ref, w_ref, keep_ref, send_ref):
    half, width = keep_ref.shape
    for at in range(0, width, wide):
        product = jnp.dot(
            x_ref[...], w_ref[:, first + at : first + at + wide], preferred_element_type=jnp.float32
        )
        keep_ref[:, at : at + wide] = product[:half]
        send_ref[:, at : at + wide] = product[half:].astype(jnp.bfloat16)


def forward(core, features, weight, first, width):
    half = features.shape[0] // 2
    wide = 128 * group_of(width // 128, 4)
    return core(
        functools.partial(forward_kernel, first, wide),
        "forward",
        [pltpu.VMEM((half, width), jnp.float32), pltpu.VMEM((half, width), jnp.bfloat16)],
        [in_vmem, in_vmem],
        [in_vmem, in_vmem],
        (features, weight),
    )


def sides(left, bit):
    at = len(left) - 1 - left.index(bit)
    names = range(1 << len(left))
    return [g for g in names if not g >> at & 1], [g for g in names if g >> at & 1]


def add_kernel(rows, stay, leave, keep_ref, arrived_ref, next_ref, send_ref):
    for out_ref, groups in ((next_ref, stay), (send_ref, leave)):
        for at, g in enumerate(groups):
            here = slice(g * rows, (g + 1) * rows)
            total = keep_ref[here, :] + arrived_ref[here, :].astype(jnp.float32)
            out_ref[at * rows : (at + 1) * rows, :] = total.astype(out_ref.dtype)


def add_step(core, keep, arrived, left, bit):
    rows = keep.shape[0] >> len(left)
    half = (keep.shape[0] // 2, keep.shape[1])
    return core(
        functools.partial(add_kernel, rows, *sides(left, bit)),
        "add_step",
        [pltpu.VMEM(half, jnp.float32), pltpu.VMEM(half, jnp.bfloat16)],
        [in_vmem, in_vmem],
        [in_vmem, in_vmem],
        (keep, arrived),
    )


def join_kernel(rows, stay, come, near_ref, arrived_ref, out_ref):
    for in_ref, groups in ((near_ref, stay), (arrived_ref, come)):
        for at, g in enumerate(groups):
            out_ref[g * rows : (g + 1) * rows, :] = in_ref[at * rows : (at + 1) * rows, :]


def join_step(core, near, arrived, held, bit):
    rows = 2 * near.shape[0] >> len(held)
    [out] = core(
        functools.partial(join_kernel, rows, *sides(held, bit)),
        "join_step",
        [pltpu.VMEM((2 * near.shape[0], near.shape[1]), near.dtype)],
        [in_vmem],
        [in_vmem, in_vmem],
        (near, arrived),
    )
    return out


def gelu_kernel(top, first, keep_ref, arrived_ref, cotangent_ref, activation_ref, slope_ref):
    rows, width = keep_ref.shape
    hidden = keep_ref[...] + arrived_ref[...].astype(jnp.float32)
    cotangent = cotangent_ref[top : top + rows, first : first + width]
    activation_ref[...], slope_ref[...] = gelu_pair(hidden, cotangent)


def gelu(core, keep, arrived, cotangent, top, first):
    out = pltpu.VMEM(keep.shape, jnp.bfloat16)
    return core(
        functools.partial(gelu_kernel, top, first),
        "gelu",
        [out, out],
        [in_vmem, in_vmem],
        [in_vmem] * 3,
        (keep, arrived, cotangent),
    )


def input_kernel(first, groups, has_before, finished, given, place, near_ref, far_ref, w_ref, *refs):
    half, width = near_ref.shape
    rows = 2 * half // groups
    tall = w_ref.shape[0]
    before = refs[0] if has_before else None
    outs = refs[has_before : has_before + given]
    scratch = refs[has_before + given :]
    turned = scratch[0]
    total = scratch[1] if finished else outs[0]
    wide = 128 * group_of(width // 128, 4)
    for at in range(0, width, wide):
        here = slice(at, at + wide)
        grad = jnp.concatenate([near_ref[:, here], far_ref[:, here]], axis=0)
        turned[here, :] = grad.T
    high = 128 * group_of(tall // 128, 4)
    for at in range(0, tall, high):
        here = slice(at, at + high)
        product = jnp.dot(
            w_ref[here, first : first + width], turned[...], preferred_element_type=jnp.float32
        )
        total[here, :] = product + before[here, :] if has_before else product
    if finished:
        upright = scratch[2]
        upright[...] = total[...].T
        each = groups // given
        for i in range(groups):
            start = pl.multiple_of(place[i] * rows, rows)
            out_ref = outs[i // each]
            at = i % each * rows
            out_ref[at : at + rows, :] = upright[pl.ds(start, rows), :].astype(out_ref.dtype)


def input_partial(core, near, far, weight, first, place, before, pieces):
    half, width = near.shape
    tall = weight.shape[0]
    both = 2 * half
    if pieces:
        outs = [pltpu.VMEM((both // pieces, tall), jnp.float32)]
        outs += [pltpu.VMEM((both // pieces, tall), jnp.bfloat16)] * (pieces - 1)
    else:
        outs = [pltpu.VMEM((tall, both), jnp.float32)]
    has_before = before is not None
    scratch = [pltpu.VMEM((width, both), near.dtype)]
    if pieces:
        scratch += [pltpu.VMEM((tall, both), jnp.float32), pltpu.VMEM((both, tall), jnp.float32)]
    return core(
        functools.partial(
            input_kernel, first, place.shape[0], has_before, pieces > 0, len(outs)
        ),
        "input_partial",
        outs,
        [in_vmem] * len(outs),
        [in_smem] + [in_vmem] * (4 if has_before else 3),
        (place, near, far, weight) + ((before,) if has_before else ()),
        scratch=scratch,
    )


def weight_kernel(row_blocks, col_blocks, first, parts, has_before, code, *refs):
    turned = refs[:parts]
    grads = refs[parts : 3 * parts]
    out_ref, made, sem = refs[3 * parts + has_before :]
    blk = made.shape[-1]
    width = grads[0].shape[1]
    here = width // blk
    per_step = group_of(here, 2)
    wide = per_step * blk
    for j in range(here // per_step):
        features = jnp.concatenate([t[...] for t in turned], axis=1)
        grad = jnp.concatenate([g[:, j * wide : (j + 1) * wide] for g in grads], axis=0)
        product = jnp.dot(features, grad, preferred_element_type=jnp.float32)
        for r in range(row_blocks):
            for c in range(per_step):
                entry = code[r * col_blocks + first // blk + j * per_step + c]
                live = lax.rem(entry, 2).astype(jnp.float32)
                at = (j * row_blocks + r) * per_step + c
                block = product[r * blk : (r + 1) * blk, c * blk : (c + 1) * blk] * live
                made[at] = block.astype(made.dtype)
                pltpu.make_async_copy(
                    made.at[at], out_ref.at[0, 0, lax.div(entry, 2)], sem
                ).start()
    pltpu.make_async_copy(made, out_ref.at[0, 0, pl.ds(0, made.shape[0])], sem).wait()


def weight_gradient(core, turned, grads, code, first, row_blocks, col_blocks, blk, before):
    parts = len(turned)
    has_before = before is not None
    here = row_blocks * grads[0].shape[1] // blk
    arrays = [*turned, *grads]
    [out] = core(
        functools.partial(weight_kernel, row_blocks, col_blocks, first, parts, has_before),
        "weight_gradient",
        [jax.ShapeDtypeStruct((1, 1, row_blocks * col_blocks, blk, blk), jnp.bfloat16)],
        [anywhere],
        [in_smem] + [in_vmem] * len(arrays) + [anywhere] * has_before,
        (code, *arrays) + ((before,) if has_before else ()),
        scratch=[pltpu.VMEM((here, blk, blk), jnp.bfloat16), pltpu.SemaphoreType.DMA],
        aliases={1 + len(arrays): 0} if has_before else None,
    )
    return out


def swap(array, axis, size, bit):
    return lax.ppermute(array, axis, [(i, i ^ bit) for i in range(size)])


def on_device(tokens, w_packed, kept_rows, kept_cols, kept_count, grad_act):
    blk = w_packed.shape[-1]
    slot_count = w_packed.shape[2]
    tall = tokens.shape[1]
    row_tokens, hidden_here = grad_act.shape
    row_blocks = tall // blk
    col_blocks = hidden_here // blk
    n_row = lax.axis_size("row")
    n_col = lax.axis_size("col")
    row_me = lax.axis_index("row")
    col_me = lax.axis_index("col")
    col_groups = tokens.shape[0] // row_tokens
    tiles = row_tokens // 16
    shares = token_split if tiles % sum(token_split) == 0 else (1,)
    sizes = [16 * (tiles // sum(shares)) * share for share in shares]
    starts = [sum(sizes[:k]) for k in range(len(sizes))]
    parts = len(sizes)
    slabs = group_of(col_blocks, column_parts)
    width = hidden_here // slabs
    direct = n_col <= 8
    core = Core()

    places = kept_rows[0, 0] * col_blocks + kept_cols[0, 0]
    slots = jnp.arange(slot_count, dtype=jnp.int32)
    coded = slots * 2 + (slots < kept_count[0, 0]).astype(jnp.int32)
    code = jnp.sum(jnp.where(places[None, :] == slots[:, None], coded[None, :], 0), axis=1)

    apart = row_me ^ (col_me * col_groups) if direct else row_me
    everyone = np.arange(n_row)
    order = np.concatenate([everyone[::2], everyone[1::2]]).astype(np.int32)
    pick = (jnp.asarray(order) ^ apart).astype(jnp.int32)
    distance = jnp.asarray(everyone.astype(np.int32)) ^ apart
    place = ((distance & 1) * (n_row // 2) + (distance >> 1)).astype(jnp.int32)

    pieces = []
    for start, rows in zip(starts, sizes):
        mine = tokens.reshape(col_groups, row_tokens, tall)[:, start : start + rows]
        if direct:
            pieces.append([mine] + [swap(mine, "col", n_col, m) for m in range(1, n_col)])
        else:
            pieces.append([lax.all_gather(mine, "col", axis=0, tiled=True)])
    weight = dense_tile(core, w_packed, code, row_blocks, col_blocks)

    far_bits = [1 << b for b in range(1, n_row.bit_length() - 1)]
    units = [(k, c) for k in range(parts) for c in range(slabs)]
    paths = [far_bits if at % 2 == 0 else far_bits[::-1] for at in range(len(units))]
    state = {}
    full, turned = {}, {}
    activations, sums, input_grads = {}, {}, {}

    def begin(k, c, path):
        if c == 0:
            full[k], turned[k] = arrange(core, pieces[k], pick)
        keep, send = forward(core, full[k], weight, c * width, width)
        state[k, c] = (keep, swap(send, "row", n_row, 1))

    def add(at, k, c, path):
        left = sorted(path[at:], reverse=True)
        keep, send = add_step(core, *state[k, c], left, path[at])
        state[k, c] = (keep, swap(send, "row", n_row, path[at]))

    def bend(k, c, path):
        activations[k, c], near = gelu(core, *state[k, c], grad_act, starts[k], c * width)
        state[k, c] = (near, swap(near, "row", n_row, ([1] + path)[-1]))

    def join(at, k, c, path):
        held = sorted(path[at:], reverse=True)
        near = join_step(core, *state[k, c], held, path[at])
        state[k, c] = (near, swap(near, "row", n_row, ([1] + path)[at]))

    def finish(k, c, path):
        last = c + 1 == slabs
        cut = (n_col if direct else 1) * last
        found = input_partial(
            core, *state[k, c], weight, c * width, place, sums.get((k, c - 1)), cut
        )
        sums[k, c] = found[0]
        if last and direct:
            total = found[0]
            for m in range(1, n_col):
                total = total + swap(found[m], "col", n_col, m).astype(jnp.float32)
        elif last:
            total = found[0].reshape(n_col, col_groups * sizes[k], tall)
            total = lax.psum_scatter(total, "col", scatter_dimension=0, tiled=True)[0]
        if last:
            total = total.astype(jnp.bfloat16)
            input_grads[k] = total.reshape(col_groups, sizes[k], tall)

    hops = len(far_bits)
    stages = [begin] + [functools.partial(add, at) for at in range(hops)] + [bend]
    stages += [functools.partial(join, at) for at in reversed(range(hops))] + [finish]
    plan = []
    if parts == 2 and hops == 2:
        plan = [(0, 0), (0, 1), (1, 0), (1, 1), (0, 2), (1, 2), (0, 3), (1, 3), (0, 4), (1, 4)]
        plan += [(0, 5), (0, 6), (1, 5), (1, 6)]
    else:
        plan = [(k, at) for at in range(len(stages)) for k in range(parts)]
    for k, at in plan:
        for c in range(slabs):
            stages[at](k, c, paths[units.index((k, c))])
    weight_grad = None
    for c in range(slabs):
        weight_grad = weight_gradient(
            core,
            [turned[k] for k in range(parts)],
            [g for k in range(parts) for g in state[k, c]],
            code,
            c * width,
            row_blocks,
            col_blocks,
            blk,
            weight_grad,
        )
    activation = jnp.concatenate(
        [jnp.concatenate([activations[k, c] for c in range(slabs)], axis=1) for k in range(parts)],
        axis=0,
    )
    input_grad = jnp.concatenate([input_grads[k] for k in range(parts)], axis=1).reshape(tokens.shape)
    return (activation, input_grad, weight_grad)


def solution(mesh):
    placed = (
        P("col", "row"),
        P("row", "col", None, None, None),
        P("row", "col", None),
        P("row", "col", None),
        P("row", "col"),
        P("row", "col"),
    )
    return jax.shard_map(
        on_device,
        mesh=mesh,
        in_specs=placed,
        out_specs=(P("row", "col"), P("col", "row"), P("row", "col", None, None, None)),
        check_vma=False,
    )
```

```python
import functools

import jax
import jax.numpy as jnp
import numpy as np
from jax import lax
from jax.experimental import pallas as pl
from jax.experimental.pallas import tpu as pltpu
from jax.sharding import PartitionSpec as P

gelu_scale = 0.7978845608
gelu_cubic = 0.044715
token_split = (1, 1)
column_parts = 2
vmem_limit = 16 * 1024 * 1024
in_vmem = pl.BlockSpec(memory_space=pltpu.VMEM)
in_smem = pl.BlockSpec(memory_space=pltpu.SMEM)
anywhere = pl.BlockSpec(memory_space=pltpu.HBM)


def gelu_pair(hidden, cotangent):
    inner = gelu_scale * (hidden + gelu_cubic * hidden * hidden * hidden)
    tangent = jnp.tanh(inner)
    activation = (0.5 * hidden * (1.0 + tangent)).astype(jnp.bfloat16)
    slope = 0.5 * (1.0 + tangent) + 0.5 * hidden * (1.0 - tangent * tangent) * gelu_scale * (
        1.0 + 3.0 * gelu_cubic * hidden * hidden
    )
    slope_grad = (cotangent.astype(jnp.float32) * slope).astype(jnp.bfloat16)
    return (activation, slope_grad)


def group_of(blocks, goal):
    return max(n for n in range(1, goal + 1) if blocks % n == 0)


class Core:
    def __init__(self):
        self.turn = None

    def __call__(self, kernel, name, out_shape, out_specs, in_specs, operands, scratch=(), aliases=None):
        homes = {id(in_vmem): pltpu.VMEM, id(anywhere): pltpu.HBM}
        in_specs, operands = list(in_specs), list(operands)
        if self.turn is not None:
            in_specs.append(in_vmem)
            operands.append(self.turn)
        taken = len(operands)
        given = len(out_shape)
        extra = self.turn is not None

        def body(*refs):
            refs[taken + given][...] = jnp.zeros((8, 128), jnp.float32)
            kernel(*refs[: taken - extra], *refs[taken : taken + given], *refs[taken + given + 1 :])

        placed = [
            pltpu.with_memory_space_constraint(x, homes[id(spec)]) if id(spec) in homes else x
            for x, spec in zip(operands, in_specs)
        ]
        *out, self.turn = pl.pallas_call(
            body,
            out_shape=[*out_shape, pltpu.VMEM((8, 128), jnp.float32)],
            in_specs=in_specs,
            out_specs=[*out_specs, in_vmem],
            scratch_shapes=list(scratch),
            input_output_aliases=aliases or {},
            compiler_params=pltpu.CompilerParams(vmem_limit_bytes=vmem_limit),
            cost_estimate=pl.CostEstimate(flops=1, transcendentals=0, bytes_accessed=1),
            name=name,
        )(*placed)
        return out


def dense_kernel(row_blocks, col_blocks, code, w_ref, out_ref, empty, sem):
    blk = w_ref.shape[-1]
    empty[...] = jnp.zeros_like(empty)

    def load(at, carry):
        for r in range(row_blocks):
            entry = code[r * col_blocks + at]
            start = pl.multiple_of(at * blk, blk)
            target = out_ref.at[pl.ds(r * blk, blk), pl.ds(start, blk)]

            @pl.when(lax.rem(entry, 2) == 1)
            def _():
                pltpu.make_async_copy(w_ref.at[0, 0, lax.div(entry, 2)], target, sem).start()

            @pl.when(lax.rem(entry, 2) == 0)
            def _():
                pltpu.make_async_copy(empty, target, sem).start()

        return carry

    lax.fori_loop(0, col_blocks, load, 0)
    pltpu.make_async_copy(out_ref, out_ref, sem).wait()


def dense_tile(core, w_packed, code, row_blocks, col_blocks):
    blk = w_packed.shape[-1]
    [weight] = core(
        functools.partial(dense_kernel, row_blocks, col_blocks),
        "dense_tile",
        [pltpu.VMEM((row_blocks * blk, col_blocks * blk), w_packed.dtype)],
        [in_vmem],
        [in_smem, anywhere],
        (code, w_packed),
        scratch=[pltpu.VMEM((blk, blk), w_packed.dtype), pltpu.SemaphoreType.DMA],
    )
    return weight


def arrange_kernel(groups, rows, pieces, pick, *refs):
    out_ref, turned_ref, all_ref = refs[pieces:]
    each = groups // pieces
    for m in range(pieces):
        for j in range(each):
            all_ref[m * each + j] = refs[m][j]
    for t in range(groups):
        out_ref[pl.ds(t * rows, rows), :] = all_ref[pick[t]]
    turned_ref[...] = out_ref[...].T


def arrange(core, pieces, pick):
    groups = pick.shape[0]
    rows, tall = pieces[0].shape[1:]
    kind = pieces[0].dtype
    return core(
        functools.partial(arrange_kernel, groups, rows, len(pieces)),
        "arrange",
        [pltpu.VMEM((groups * rows, tall), kind), pltpu.VMEM((tall, groups * rows), kind)],
        [in_vmem, in_vmem],
        [in_smem] + [in_vmem] * len(pieces),
        (pick, *pieces),
        scratch=[pltpu.VMEM((groups, rows, tall), kind)],
    )


def forward_kernel(first, wide, x_ref, w_ref, keep_ref, send_ref):
    half, width = keep_ref.shape
    for at in range(0, width, wide):
        product = jnp.dot(
            x_ref[...], w_ref[:, first + at : first + at + wide], preferred_element_type=jnp.float32
        )
        keep_ref[:, at : at + wide] = product[:half]
        send_ref[:, at : at + wide] = product[half:].astype(jnp.bfloat16)


def forward(core, features, weight, first, width):
    half = features.shape[0] // 2
    wide = 128 * group_of(width // 128, 4)
    return core(
        functools.partial(forward_kernel, first, wide),
        "forward",
        [pltpu.VMEM((half, width), jnp.float32), pltpu.VMEM((half, width), jnp.bfloat16)],
        [in_vmem, in_vmem],
        [in_vmem, in_vmem],
        (features, weight),
    )


def sides(left, bit):
    at = len(left) - 1 - left.index(bit)
    names = range(1 << len(left))
    return [g for g in names if not g >> at & 1], [g for g in names if g >> at & 1]


def add_kernel(rows, stay, leave, keep_ref, arrived_ref, next_ref, send_ref):
    for out_ref, groups in ((next_ref, stay), (send_ref, leave)):
        for at, g in enumerate(groups):
            here = slice(g * rows, (g + 1) * rows)
            total = keep_ref[here, :] + arrived_ref[here, :].astype(jnp.float32)
            out_ref[at * rows : (at + 1) * rows, :] = total.astype(out_ref.dtype)


def add_step(core, keep, arrived, left, bit):
    rows = keep.shape[0] >> len(left)
    half = (keep.shape[0] // 2, keep.shape[1])
    return core(
        functools.partial(add_kernel, rows, *sides(left, bit)),
        "add_step",
        [pltpu.VMEM(half, jnp.float32), pltpu.VMEM(half, jnp.bfloat16)],
        [in_vmem, in_vmem],
        [in_vmem, in_vmem],
        (keep, arrived),
    )


def join_kernel(rows, stay, come, near_ref, arrived_ref, out_ref):
    for in_ref, groups in ((near_ref, stay), (arrived_ref, come)):
        for at, g in enumerate(groups):
            out_ref[g * rows : (g + 1) * rows, :] = in_ref[at * rows : (at + 1) * rows, :]


def join_step(core, near, arrived, held, bit):
    rows = 2 * near.shape[0] >> len(held)
    [out] = core(
        functools.partial(join_kernel, rows, *sides(held, bit)),
        "join_step",
        [pltpu.VMEM((2 * near.shape[0], near.shape[1]), near.dtype)],
        [in_vmem],
        [in_vmem, in_vmem],
        (near, arrived),
    )
    return out


def gelu_kernel(top, first, keep_ref, arrived_ref, cotangent_ref, activation_ref, slope_ref):
    rows, width = keep_ref.shape
    hidden = keep_ref[...] + arrived_ref[...].astype(jnp.float32)
    cotangent = cotangent_ref[top : top + rows, first : first + width]
    activation_ref[...], slope_ref[...] = gelu_pair(hidden, cotangent)


def gelu(core, keep, arrived, cotangent, top, first):
    out = pltpu.VMEM(keep.shape, jnp.bfloat16)
    return core(
        functools.partial(gelu_kernel, top, first),
        "gelu",
        [out, out],
        [in_vmem, in_vmem],
        [in_vmem] * 3,
        (keep, arrived, cotangent),
    )


def input_kernel(first, groups, has_before, finished, given, place, near_ref, far_ref, w_ref, *refs):
    half, width = near_ref.shape
    rows = 2 * half // groups
    tall = w_ref.shape[0]
    before = refs[0] if has_before else None
    outs = refs[has_before : has_before + given]
    scratch = refs[has_before + given :]
    turned = scratch[0]
    total = scratch[1] if finished else outs[0]
    wide = 128 * group_of(width // 128, 4)
    for at in range(0, width, wide):
        here = slice(at, at + wide)
        grad = jnp.concatenate([near_ref[:, here], far_ref[:, here]], axis=0)
        turned[here, :] = grad.T
    high = 128 * group_of(tall // 128, 4)
    for at in range(0, tall, high):
        here = slice(at, at + high)
        product = jnp.dot(
            w_ref[here, first : first + width], turned[...], preferred_element_type=jnp.float32
        )
        total[here, :] = product + before[here, :] if has_before else product
    if finished:
        upright = scratch[2]
        upright[...] = total[...].T
        each = groups // given
        for i in range(groups):
            start = pl.multiple_of(place[i] * rows, rows)
            out_ref = outs[i // each]
            at = i % each * rows
            out_ref[at : at + rows, :] = upright[pl.ds(start, rows), :].astype(out_ref.dtype)


def input_partial(core, near, far, weight, first, place, before, pieces):
    half, width = near.shape
    tall = weight.shape[0]
    both = 2 * half
    if pieces:
        outs = [pltpu.VMEM((both // pieces, tall), jnp.float32)]
        outs += [pltpu.VMEM((both // pieces, tall), jnp.bfloat16)] * (pieces - 1)
    else:
        outs = [pltpu.VMEM((tall, both), jnp.float32)]
    has_before = before is not None
    scratch = [pltpu.VMEM((width, both), near.dtype)]
    if pieces:
        scratch += [pltpu.VMEM((tall, both), jnp.float32), pltpu.VMEM((both, tall), jnp.float32)]
    return core(
        functools.partial(
            input_kernel, first, place.shape[0], has_before, pieces > 0, len(outs)
        ),
        "input_partial",
        outs,
        [in_vmem] * len(outs),
        [in_smem] + [in_vmem] * (4 if has_before else 3),
        (place, near, far, weight) + ((before,) if has_before else ()),
        scratch=scratch,
    )


def weight_kernel(row_blocks, col_blocks, parts, slabs, code, *refs):
    turned = refs[:parts]
    grads = refs[parts : parts + 2 * parts * slabs]
    out_ref, made, sems = refs[parts + 2 * parts * slabs :]
    blk = made.shape[-1]
    here = col_blocks // slabs
    per_step = group_of(here, 2)
    wide = per_step * blk
    per_slot = row_blocks * per_step
    depth = made.shape[0] // per_slot

    def drain(at):
        pltpu.make_async_copy(
            made.at[pl.ds(at * per_slot, per_slot)],
            out_ref.at[0, 0, pl.ds(0, per_slot)],
            sems.at[at],
        ).wait()

    features = jnp.concatenate([t[...] for t in turned], axis=1)
    steps = [(slab, j) for slab in range(slabs) for j in range(here // per_step)]
    for step, (slab, j) in enumerate(steps):
        slot = step % depth
        if step >= depth:
            drain(slot)
        mine = grads[2 * parts * slab : 2 * parts * (slab + 1)]
        grad = jnp.concatenate([g[:, j * wide : (j + 1) * wide] for g in mine], axis=0)
        product = jnp.dot(features, grad, preferred_element_type=jnp.float32)
        for r in range(row_blocks):
            for c in range(per_step):
                entry = code[r * col_blocks + slab * here + j * per_step + c]
                live = lax.rem(entry, 2).astype(jnp.float32)
                at = slot * per_slot + r * per_step + c
                block = product[r * blk : (r + 1) * blk, c * blk : (c + 1) * blk] * live
                made[at] = block.astype(made.dtype)
                pltpu.make_async_copy(
                    made.at[at], out_ref.at[0, 0, lax.div(entry, 2)], sems.at[slot]
                ).start()
    for slot in range(min(depth, len(steps))):
        drain(slot)


def weight_gradient(core, turned, grads, code, row_blocks, col_blocks, blk, slabs):
    parts = len(turned)
    arrays = [*turned, *grads]
    per_slot = row_blocks * group_of(col_blocks // slabs, 2)
    depth = 6
    [out] = core(
        functools.partial(weight_kernel, row_blocks, col_blocks, parts, slabs),
        "weight_gradient",
        [jax.ShapeDtypeStruct((1, 1, row_blocks * col_blocks, blk, blk), jnp.bfloat16)],
        [anywhere],
        [in_smem] + [in_vmem] * len(arrays),
        (code, *arrays),
        scratch=[
            pltpu.VMEM((depth * per_slot, blk, blk), jnp.bfloat16),
            pltpu.SemaphoreType.DMA((depth,)),
        ],
    )
    return out


def place_kernel(spots, *refs):
    blocks = refs[: len(spots)]
    out_ref, sems = refs[len(spots) :]
    copies = []
    for at, (top, first) in enumerate(spots):
        rows, width = blocks[at].shape
        target = out_ref.at[pl.ds(top, rows), pl.ds(first, width)]
        copies.append(pltpu.make_async_copy(blocks[at], target, sems.at[at]))
        copies[-1].start()
    for copy in copies:
        copy.wait()


def place_activation(core, blocks, spots, shape):
    [out] = core(
        functools.partial(place_kernel, spots),
        "place_activation",
        [jax.ShapeDtypeStruct(shape, jnp.bfloat16)],
        [anywhere],
        [in_vmem] * len(blocks),
        blocks,
        scratch=[pltpu.SemaphoreType.DMA((len(blocks),))],
    )
    return out


def total_kernel(each, many, starts, sizes, *refs):
    out_ref = refs[-1]
    own = sum(sizes)
    for k, (start, rows) in enumerate(zip(starts, sizes)):
        found = refs[k * many : (k + 1) * many]
        for j in range(each):
            here = slice(j * rows, (j + 1) * rows)
            total = found[0][here, :]
            for piece in found[1:]:
                total = total + piece[here, :].astype(jnp.float32)
            top = j * own + start
            out_ref[top : top + rows, :] = total.astype(jnp.bfloat16)


def total_input(core, found, each, starts, sizes):
    arrays = [x for part in found for x in part]
    shape = (each * sum(sizes), arrays[0].shape[1])
    [out] = core(
        functools.partial(total_kernel, each, len(found[0]), starts, sizes),
        "total_input",
        [jax.ShapeDtypeStruct(shape, jnp.bfloat16)],
        [pl.BlockSpec(shape, lambda: (0, 0))],
        [in_vmem] * len(arrays),
        arrays,
    )
    return out


def swap(array, axis, size, bit):
    return lax.ppermute(array, axis, [(i, i ^ bit) for i in range(size)])


def on_device(tokens, w_packed, kept_rows, kept_cols, kept_count, grad_act):
    blk = w_packed.shape[-1]
    slot_count = w_packed.shape[2]
    tall = tokens.shape[1]
    row_tokens, hidden_here = grad_act.shape
    row_blocks = tall // blk
    col_blocks = hidden_here // blk
    n_row = lax.axis_size("row")
    n_col = lax.axis_size("col")
    row_me = lax.axis_index("row")
    col_me = lax.axis_index("col")
    col_groups = tokens.shape[0] // row_tokens
    tiles = row_tokens // 16
    shares = token_split if tiles % sum(token_split) == 0 else (1,)
    sizes = [16 * (tiles // sum(shares)) * share for share in shares]
    starts = [sum(sizes[:k]) for k in range(len(sizes))]
    parts = len(sizes)
    slabs = group_of(col_blocks, column_parts)
    width = hidden_here // slabs
    direct = n_col <= 8
    core = Core()

    places = kept_rows[0, 0] * col_blocks + kept_cols[0, 0]
    slots = jnp.arange(slot_count, dtype=jnp.int32)
    coded = slots * 2 + (slots < kept_count[0, 0]).astype(jnp.int32)
    code = jnp.sum(jnp.where(places[None, :] == slots[:, None], coded[None, :], 0), axis=1)

    apart = row_me ^ (col_me * col_groups) if direct else row_me
    everyone = np.arange(n_row)
    order = np.concatenate([everyone[::2], everyone[1::2]]).astype(np.int32)
    pick = (jnp.asarray(order) ^ apart).astype(jnp.int32)
    distance = jnp.asarray(everyone.astype(np.int32)) ^ apart
    place = ((distance & 1) * (n_row // 2) + (distance >> 1)).astype(jnp.int32)

    pieces = []
    for start, rows in zip(starts, sizes):
        mine = tokens.reshape(col_groups, row_tokens, tall)[:, start : start + rows]
        if direct:
            pieces.append([mine] + [swap(mine, "col", n_col, m) for m in range(1, n_col)])
        else:
            pieces.append([lax.all_gather(mine, "col", axis=0, tiled=True)])
    weight = dense_tile(core, w_packed, code, row_blocks, col_blocks)

    far_bits = [1 << b for b in range(1, n_row.bit_length() - 1)]
    units = [(k, c) for k in range(parts) for c in range(slabs)]
    paths = [far_bits if at % 2 == 0 else far_bits[::-1] for at in range(len(units))]
    state = {}
    full, turned = {}, {}
    activations, sums, input_grads = {}, {}, {}

    def begin(k, c, path):
        if c == 0:
            full[k], turned[k] = arrange(core, pieces[k], pick)
        keep, send = forward(core, full[k], weight, c * width, width)
        state[k, c] = (keep, swap(send, "row", n_row, 1))

    def add(at, k, c, path):
        left = sorted(path[at:], reverse=True)
        keep, send = add_step(core, *state[k, c], left, path[at])
        state[k, c] = (keep, swap(send, "row", n_row, path[at]))

    def bend(k, c, path):
        activations[k, c], near = gelu(core, *state[k, c], grad_act, starts[k], c * width)
        state[k, c] = (near, swap(near, "row", n_row, ([1] + path)[-1]))

    def join(at, k, c, path):
        held = sorted(path[at:], reverse=True)
        near = join_step(core, *state[k, c], held, path[at])
        state[k, c] = (near, swap(near, "row", n_row, ([1] + path)[at]))

    def finish(k, c, path):
        last = c + 1 == slabs
        cut = (n_col if direct else 1) * last
        found = input_partial(
            core, *state[k, c], weight, c * width, place, sums.get((k, c - 1)), cut
        )
        sums[k, c] = found[0]
        if last and direct:
            input_grads[k] = [found[0]]
            input_grads[k] += [swap(found[m], "col", n_col, m) for m in range(1, n_col)]
        elif last:
            total = found[0].reshape(n_col, col_groups * sizes[k], tall)
            total = lax.psum_scatter(total, "col", scatter_dimension=0, tiled=True)[0]
            input_grads[k] = [total]

    hops = len(far_bits)
    stages = [begin] + [functools.partial(add, at) for at in range(hops)] + [bend]
    stages += [functools.partial(join, at) for at in reversed(range(hops))] + [finish]
    plan = [(k, at) for at in range(len(stages)) for k in range(parts)]
    if parts == 2 and hops == 2:
        plan = [(0, 0), (0, 1), (0, 2), (1, 0), (0, 3), (1, 1), (0, 4), (1, 2), (0, 5), (1, 3), (1, 4), (0, 6), (1, 5), (1, 6)]
    for k, at in plan:
        for c in range(slabs):
            stages[at](k, c, paths[units.index((k, c))])
        if (k, at) == (parts - 1, len(stages) - 3):
            activation = place_activation(
                core,
                [activations[k, c] for k, c in units],
                [(starts[k], c * width) for k, c in units],
                grad_act.shape,
            )
    weight_grad = weight_gradient(
        core,
        [turned[k] for k in range(parts)],
        [g for c in range(slabs) for k in range(parts) for g in state[k, c]],
        code,
        row_blocks,
        col_blocks,
        blk,
        slabs,
    )
    input_grad = total_input(
        core, [input_grads[k] for k in range(parts)], col_groups, starts, sizes
    )
    return (activation, input_grad, weight_grad)


def solution(mesh):
    placed = (
        P("col", "row"),
        P("row", "col", None, None, None),
        P("row", "col", None),
        P("row", "col", None),
        P("row", "col"),
        P("row", "col"),
    )
    return jax.shard_map(
        on_device,
        mesh=mesh,
        in_specs=placed,
        out_specs=(P("row", "col"), P("col", "row"), P("row", "col", None, None, None)),
        check_vma=False,
    )
```

```python
import functools

import jax
import jax.numpy as jnp
import numpy as np
from jax import lax
from jax.experimental import pallas as pl
from jax.experimental.pallas import tpu as pltpu
from jax.sharding import PartitionSpec as P

gelu_scale = 0.7978845608
gelu_cubic = 0.044715
token_split = (1, 1)
column_parts = 2
vmem_limit = 16 * 1024 * 1024
in_vmem = pl.BlockSpec(memory_space=pltpu.VMEM)
in_smem = pl.BlockSpec(memory_space=pltpu.SMEM)
anywhere = pl.BlockSpec(memory_space=pltpu.HBM)


def gelu_pair(hidden, cotangent):
    inner = gelu_scale * (hidden + gelu_cubic * hidden * hidden * hidden)
    tangent = jnp.tanh(inner)
    activation = (0.5 * hidden * (1.0 + tangent)).astype(jnp.bfloat16)
    slope = 0.5 * (1.0 + tangent) + 0.5 * hidden * (1.0 - tangent * tangent) * gelu_scale * (
        1.0 + 3.0 * gelu_cubic * hidden * hidden
    )
    slope_grad = (cotangent.astype(jnp.float32) * slope).astype(jnp.bfloat16)
    return (activation, slope_grad)


def group_of(blocks, goal):
    return max(n for n in range(1, goal + 1) if blocks % n == 0)


class Core:
    def __init__(self):
        self.turn = None

    def __call__(self, kernel, name, out_shape, out_specs, in_specs, operands, scratch=(), aliases=None):
        homes = {id(in_vmem): pltpu.VMEM, id(anywhere): pltpu.HBM}
        in_specs, operands = list(in_specs), list(operands)
        if self.turn is not None:
            in_specs.append(in_vmem)
            operands.append(self.turn)
        taken = len(operands)
        given = len(out_shape)
        extra = self.turn is not None

        def body(*refs):
            refs[taken + given][...] = jnp.zeros((8, 128), jnp.float32)
            kernel(*refs[: taken - extra], *refs[taken : taken + given], *refs[taken + given + 1 :])

        placed = [
            pltpu.with_memory_space_constraint(x, homes[id(spec)]) if id(spec) in homes else x
            for x, spec in zip(operands, in_specs)
        ]
        *out, self.turn = pl.pallas_call(
            body,
            out_shape=[*out_shape, pltpu.VMEM((8, 128), jnp.float32)],
            in_specs=in_specs,
            out_specs=[*out_specs, in_vmem],
            scratch_shapes=list(scratch),
            input_output_aliases=aliases or {},
            compiler_params=pltpu.CompilerParams(vmem_limit_bytes=vmem_limit),
            cost_estimate=pl.CostEstimate(flops=1, transcendentals=0, bytes_accessed=1),
            name=name,
        )(*placed)
        return out


def dense_kernel(row_blocks, col_blocks, code, w_ref, out_ref, empty, sem):
    blk = w_ref.shape[-1]
    empty[...] = jnp.zeros_like(empty)

    def load(at, carry):
        for r in range(row_blocks):
            entry = code[r * col_blocks + at]
            start = pl.multiple_of(at * blk, blk)
            target = out_ref.at[pl.ds(r * blk, blk), pl.ds(start, blk)]

            @pl.when(lax.rem(entry, 2) == 1)
            def _():
                pltpu.make_async_copy(w_ref.at[0, 0, lax.div(entry, 2)], target, sem).start()

            @pl.when(lax.rem(entry, 2) == 0)
            def _():
                pltpu.make_async_copy(empty, target, sem).start()

        return carry

    lax.fori_loop(0, col_blocks, load, 0)
    pltpu.make_async_copy(out_ref, out_ref, sem).wait()


def dense_tile(core, w_packed, code, row_blocks, col_blocks):
    blk = w_packed.shape[-1]
    [weight] = core(
        functools.partial(dense_kernel, row_blocks, col_blocks),
        "dense_tile",
        [pltpu.VMEM((row_blocks * blk, col_blocks * blk), w_packed.dtype)],
        [in_vmem],
        [in_smem, anywhere],
        (code, w_packed),
        scratch=[pltpu.VMEM((blk, blk), w_packed.dtype), pltpu.SemaphoreType.DMA],
    )
    return weight


def arrange_kernel(first, rows, each, pieces, pick, *refs):
    out_ref, turned_ref, all_ref = refs[pieces:]
    groups = all_ref.shape[0]
    own = pieces * refs[0].shape[0] // groups
    for m in range(pieces):
        for j in range(each):
            start = j * own + first
            all_ref[m * each + j] = refs[m][start : start + rows, :]
    for t in range(groups):
        out_ref[pl.ds(t * rows, rows), :] = all_ref[pick[t]]
    turned_ref[...] = out_ref[...].T


def arrange(core, pieces, pick, first, rows):
    groups = pick.shape[0]
    tall = pieces[0].shape[1]
    kind = pieces[0].dtype
    return core(
        functools.partial(arrange_kernel, first, rows, groups // len(pieces), len(pieces)),
        "arrange",
        [pltpu.VMEM((groups * rows, tall), kind), pltpu.VMEM((tall, groups * rows), kind)],
        [in_vmem, in_vmem],
        [in_smem] + [in_vmem] * len(pieces),
        (pick, *pieces),
        scratch=[pltpu.VMEM((groups, rows, tall), kind)],
    )


def forward_kernel(first, wide, x_ref, w_ref, keep_ref, send_ref):
    half, width = keep_ref.shape
    for at in range(0, width, wide):
        product = jnp.dot(
            x_ref[...], w_ref[:, first + at : first + at + wide], preferred_element_type=jnp.float32
        )
        keep_ref[:, at : at + wide] = product[:half]
        send_ref[:, at : at + wide] = product[half:].astype(jnp.bfloat16)


def forward(core, features, weight, first, width):
    half = features.shape[0] // 2
    wide = 128 * group_of(width // 128, 4)
    return core(
        functools.partial(forward_kernel, first, wide),
        "forward",
        [pltpu.VMEM((half, width), jnp.float32), pltpu.VMEM((half, width), jnp.bfloat16)],
        [in_vmem, in_vmem],
        [in_vmem, in_vmem],
        (features, weight),
    )


def sides(left, bit):
    at = len(left) - 1 - left.index(bit)
    names = range(1 << len(left))
    return [g for g in names if not g >> at & 1], [g for g in names if g >> at & 1]


def add_kernel(rows, stay, leave, keep_ref, arrived_ref, next_ref, send_ref):
    for out_ref, groups in ((next_ref, stay), (send_ref, leave)):
        for at, g in enumerate(groups):
            here = slice(g * rows, (g + 1) * rows)
            total = keep_ref[here, :] + arrived_ref[here, :].astype(jnp.float32)
            out_ref[at * rows : (at + 1) * rows, :] = total.astype(out_ref.dtype)


def add_step(core, keep, arrived, left, bit):
    rows = keep.shape[0] >> len(left)
    half = (keep.shape[0] // 2, keep.shape[1])
    return core(
        functools.partial(add_kernel, rows, *sides(left, bit)),
        "add_step",
        [pltpu.VMEM(half, jnp.float32), pltpu.VMEM(half, jnp.bfloat16)],
        [in_vmem, in_vmem],
        [in_vmem, in_vmem],
        (keep, arrived),
    )


def join_kernel(rows, stay, come, near_ref, arrived_ref, out_ref):
    for in_ref, groups in ((near_ref, stay), (arrived_ref, come)):
        for at, g in enumerate(groups):
            out_ref[g * rows : (g + 1) * rows, :] = in_ref[at * rows : (at + 1) * rows, :]


def join_step(core, near, arrived, held, bit):
    rows = 2 * near.shape[0] >> len(held)
    [out] = core(
        functools.partial(join_kernel, rows, *sides(held, bit)),
        "join_step",
        [pltpu.VMEM((2 * near.shape[0], near.shape[1]), near.dtype)],
        [in_vmem],
        [in_vmem, in_vmem],
        (near, arrived),
    )
    return out


def gelu_kernel(top, first, keep_ref, arrived_ref, cotangent_ref, activation_ref, slope_ref):
    rows, width = keep_ref.shape
    hidden = keep_ref[...] + arrived_ref[...].astype(jnp.float32)
    cotangent = cotangent_ref[top : top + rows, first : first + width]
    activation_ref[...], slope_ref[...] = gelu_pair(hidden, cotangent)


def gelu(core, keep, arrived, cotangent, top, first):
    out = pltpu.VMEM(keep.shape, jnp.bfloat16)
    return core(
        functools.partial(gelu_kernel, top, first),
        "gelu",
        [out, out],
        [in_vmem, in_vmem],
        [in_vmem] * 3,
        (keep, arrived, cotangent),
    )


def input_kernel(first, groups, has_before, finished, given, place, near_ref, far_ref, w_ref, *refs):
    half, width = near_ref.shape
    rows = 2 * half // groups
    tall = w_ref.shape[0]
    before = refs[0] if has_before else None
    outs = refs[has_before : has_before + given]
    scratch = refs[has_before + given :]
    turned = scratch[0]
    total = scratch[1] if finished else outs[0]
    wide = 128 * group_of(width // 128, 4)
    for at in range(0, width, wide):
        here = slice(at, at + wide)
        grad = jnp.concatenate([near_ref[:, here], far_ref[:, here]], axis=0)
        turned[here, :] = grad.T
    high = 128 * group_of(tall // 128, 4)
    for at in range(0, tall, high):
        here = slice(at, at + high)
        product = jnp.dot(
            w_ref[here, first : first + width], turned[...], preferred_element_type=jnp.float32
        )
        total[here, :] = product + before[here, :] if has_before else product
    if finished:
        upright = scratch[2]
        upright[...] = total[...].T
        each = groups // given
        for i in range(groups):
            start = pl.multiple_of(place[i] * rows, rows)
            out_ref = outs[i // each]
            at = i % each * rows
            out_ref[at : at + rows, :] = upright[pl.ds(start, rows), :].astype(out_ref.dtype)


def input_partial(core, near, far, weight, first, place, before, pieces):
    half, width = near.shape
    tall = weight.shape[0]
    both = 2 * half
    if pieces:
        outs = [pltpu.VMEM((both // pieces, tall), jnp.float32)]
        outs += [pltpu.VMEM((both // pieces, tall), jnp.bfloat16)] * (pieces - 1)
    else:
        outs = [pltpu.VMEM((tall, both), jnp.float32)]
    has_before = before is not None
    scratch = [pltpu.VMEM((width, both), near.dtype)]
    if pieces:
        scratch += [pltpu.VMEM((tall, both), jnp.float32), pltpu.VMEM((both, tall), jnp.float32)]
    return core(
        functools.partial(
            input_kernel, first, place.shape[0], has_before, pieces > 0, len(outs)
        ),
        "input_partial",
        outs,
        [in_vmem] * len(outs),
        [in_smem] + [in_vmem] * (4 if has_before else 3),
        (place, near, far, weight) + ((before,) if has_before else ()),
        scratch=scratch,
    )


def weight_kernel(row_blocks, col_blocks, first, parts, has_before, code, *refs):
    turned = refs[:parts]
    grads = refs[parts : 3 * parts]
    out_ref, made, sem = refs[3 * parts + has_before :]
    blk = made.shape[-1]
    width = grads[0].shape[1]
    here = width // blk
    per_step = group_of(here, 2)
    wide = per_step * blk
    for j in range(here // per_step):
        features = jnp.concatenate([t[...] for t in turned], axis=1)
        grad = jnp.concatenate([g[:, j * wide : (j + 1) * wide] for g in grads], axis=0)
        product = jnp.dot(features, grad, preferred_element_type=jnp.float32)
        for r in range(row_blocks):
            for c in range(per_step):
                entry = code[r * col_blocks + first // blk + j * per_step + c]
                live = lax.rem(entry, 2).astype(jnp.float32)
                at = (j * row_blocks + r) * per_step + c
                block = product[r * blk : (r + 1) * blk, c * blk : (c + 1) * blk] * live
                made[at] = block.astype(made.dtype)
                pltpu.make_async_copy(
                    made.at[at], out_ref.at[0, 0, lax.div(entry, 2)], sem
                ).start(priority=at % 2)
    pltpu.make_async_copy(made, out_ref.at[0, 0, pl.ds(0, made.shape[0])], sem).wait()


def weight_gradient(core, turned, grads, code, first, row_blocks, col_blocks, blk, before):
    parts = len(turned)
    has_before = before is not None
    here = row_blocks * grads[0].shape[1] // blk
    arrays = [*turned, *grads]
    [out] = core(
        functools.partial(weight_kernel, row_blocks, col_blocks, first, parts, has_before),
        "weight_gradient",
        [jax.ShapeDtypeStruct((1, 1, row_blocks * col_blocks, blk, blk), jnp.bfloat16)],
        [anywhere],
        [in_smem] + [in_vmem] * len(arrays) + [anywhere] * has_before,
        (code, *arrays) + ((before,) if has_before else ()),
        scratch=[pltpu.VMEM((here, blk, blk), jnp.bfloat16), pltpu.SemaphoreType.DMA],
        aliases={1 + len(arrays): 0} if has_before else None,
    )
    return out


def place_kernel(spots, *refs):
    blocks = refs[: len(spots)]
    out_ref, sems = refs[len(spots) :]
    copies = []
    for at, (top, first) in enumerate(spots):
        rows, width = blocks[at].shape
        target = out_ref.at[pl.ds(top, rows), pl.ds(first, width)]
        copies.append(pltpu.make_async_copy(blocks[at], target, sems.at[at]))
        copies[-1].start()
    for copy in copies:
        copy.wait()


def place_activation(core, blocks, spots, shape):
    [out] = core(
        functools.partial(place_kernel, spots),
        "place_activation",
        [jax.ShapeDtypeStruct(shape, jnp.bfloat16)],
        [anywhere],
        [in_vmem] * len(blocks),
        blocks,
        scratch=[pltpu.SemaphoreType.DMA((len(blocks),))],
    )
    return out


def total_kernel(each, many, starts, sizes, *refs):
    out_ref = refs[-1]
    own = sum(sizes)
    for k, (start, rows) in enumerate(zip(starts, sizes)):
        found = refs[k * many : (k + 1) * many]
        for j in range(each):
            here = slice(j * rows, (j + 1) * rows)
            total = found[0][here, :]
            for piece in found[1:]:
                total = total + piece[here, :].astype(jnp.float32)
            top = j * own + start
            out_ref[top : top + rows, :] = total.astype(jnp.bfloat16)


def total_input(core, found, each, starts, sizes):
    arrays = [x for part in found for x in part]
    shape = (each * sum(sizes), arrays[0].shape[1])
    [out] = core(
        functools.partial(total_kernel, each, len(found[0]), starts, sizes),
        "total_input",
        [jax.ShapeDtypeStruct(shape, jnp.bfloat16)],
        [pl.BlockSpec(shape, lambda: (0, 0))],
        [in_vmem] * len(arrays),
        arrays,
    )
    return out


def swap(array, axis, size, bit):
    return lax.ppermute(array, axis, [(i, i ^ bit) for i in range(size)])


def on_device(tokens, w_packed, kept_rows, kept_cols, kept_count, grad_act):
    blk = w_packed.shape[-1]
    slot_count = w_packed.shape[2]
    tall = tokens.shape[1]
    row_tokens, hidden_here = grad_act.shape
    row_blocks = tall // blk
    col_blocks = hidden_here // blk
    n_row = lax.axis_size("row")
    n_col = lax.axis_size("col")
    row_me = lax.axis_index("row")
    col_me = lax.axis_index("col")
    col_groups = tokens.shape[0] // row_tokens
    tiles = row_tokens // 16
    shares = token_split if tiles % sum(token_split) == 0 else (1,)
    sizes = [16 * (tiles // sum(shares)) * share for share in shares]
    starts = [sum(sizes[:k]) for k in range(len(sizes))]
    parts = len(sizes)
    slabs = group_of(col_blocks, column_parts)
    width = hidden_here // slabs
    direct = n_col <= 8
    core = Core()

    places = kept_rows[0, 0] * col_blocks + kept_cols[0, 0]
    slots = jnp.arange(slot_count, dtype=jnp.int32)
    coded = slots * 2 + (slots < kept_count[0, 0]).astype(jnp.int32)
    code = jnp.sum(jnp.where(places[None, :] == slots[:, None], coded[None, :], 0), axis=1)

    apart = row_me ^ (col_me * col_groups) if direct else row_me
    everyone = np.arange(n_row)
    order = np.concatenate([everyone[::2], everyone[1::2]]).astype(np.int32)
    pick = (jnp.asarray(order) ^ apart).astype(jnp.int32)
    distance = jnp.asarray(everyone.astype(np.int32)) ^ apart
    place = ((distance & 1) * (n_row // 2) + (distance >> 1)).astype(jnp.int32)

    if direct:
        pieces = [tokens] + [swap(tokens, "col", n_col, m) for m in range(1, n_col)]
    else:
        pieces = [lax.all_gather(tokens, "col", axis=0, tiled=True)]
    weight = dense_tile(core, w_packed, code, row_blocks, col_blocks)

    far_bits = [1 << b for b in range(1, n_row.bit_length() - 1)]
    units = [(k, c) for k in range(parts) for c in range(slabs)]
    paths = [far_bits if at % 2 == 0 else far_bits[::-1] for at in range(len(units))]
    state = {}
    full, turned = {}, {}
    activations, sums, input_grads = {}, {}, {}

    def begin(k, c, path):
        if c == 0:
            full[k], turned[k] = arrange(core, pieces, pick, starts[k], sizes[k])
        keep, send = forward(core, full[k], weight, c * width, width)
        state[k, c] = (keep, swap(send, "row", n_row, 1))

    def add(at, k, c, path):
        left = sorted(path[at:], reverse=True)
        keep, send = add_step(core, *state[k, c], left, path[at])
        state[k, c] = (keep, swap(send, "row", n_row, path[at]))

    def bend(k, c, path):
        activations[k, c], near = gelu(core, *state[k, c], grad_act, starts[k], c * width)
        state[k, c] = (near, swap(near, "row", n_row, ([1] + path)[-1]))

    def join(at, k, c, path):
        held = sorted(path[at:], reverse=True)
        near = join_step(core, *state[k, c], held, path[at])
        state[k, c] = (near, swap(near, "row", n_row, ([1] + path)[at]))

    def finish(k, c, path):
        last = c + 1 == slabs
        cut = (n_col if direct else 1) * last
        found = input_partial(
            core, *state[k, c], weight, c * width, place, sums.get((k, c - 1)), cut
        )
        sums[k, c] = found[0]
        if last and direct:
            input_grads[k] = [found[0]]
            input_grads[k] += [swap(found[m], "col", n_col, m) for m in range(1, n_col)]
        elif last:
            total = found[0].reshape(n_col, col_groups * sizes[k], tall)
            total = lax.psum_scatter(total, "col", scatter_dimension=0, tiled=True)[0]
            input_grads[k] = [total]

    hops = len(far_bits)
    stages = [begin] + [functools.partial(add, at) for at in range(hops)] + [bend]
    stages += [functools.partial(join, at) for at in reversed(range(hops))] + [finish]
    plan = [(k, at) for at in range(len(stages)) for k in range(parts)]
    if parts == 2 and hops == 2:
        plan = [(0, 0), (1, 0), (0, 1), (1, 1), (0, 2), (1, 2), (0, 3), (1, 3), (0, 4), (1, 4), (0, 5), (1, 5), (0, 6), (1, 6)]
    for k, at in plan:
        for c in range(slabs):
            stages[at](k, c, paths[units.index((k, c))])
        if (k, at) == (parts - 1, len(stages) - 3):
            activation = place_activation(
                core,
                [activations[k, c] for k, c in units],
                [(starts[k], c * width) for k, c in units],
                grad_act.shape,
            )
    weight_grad = None
    for c in range(slabs):
        weight_grad = weight_gradient(
            core,
            [turned[k] for k in range(parts)],
            [g for k in range(parts) for g in state[k, c]],
            code,
            c * width,
            row_blocks,
            col_blocks,
            blk,
            weight_grad,
        )
    input_grad = total_input(
        core, [input_grads[k] for k in range(parts)], col_groups, starts, sizes
    )
    return (activation, input_grad, weight_grad)


def solution(mesh):
    placed = (
        P("col", "row"),
        P("row", "col", None, None, None),
        P("row", "col", None),
        P("row", "col", None),
        P("row", "col"),
        P("row", "col"),
    )
    return jax.shard_map(
        on_device,
        mesh=mesh,
        in_specs=placed,
        out_specs=(P("row", "col"), P("col", "row"), P("row", "col", None, None, None)),
        check_vma=False,
    )
```

```python
import functools

import jax
import jax.numpy as jnp
import numpy as np
from jax import lax
from jax.experimental import pallas as pl
from jax.experimental.pallas import tpu as pltpu
from jax.sharding import PartitionSpec as P

gelu_scale = 0.7978845608
gelu_cubic = 0.044715
token_split = (1, 1)
column_parts = 2
vmem_limit = 16 * 1024 * 1024
in_vmem = pl.BlockSpec(memory_space=pltpu.VMEM)
in_smem = pl.BlockSpec(memory_space=pltpu.SMEM)
anywhere = pl.BlockSpec(memory_space=pltpu.HBM)


def gelu_pair(hidden, cotangent):
    inner = gelu_scale * (hidden + gelu_cubic * hidden * hidden * hidden)
    tangent = jnp.tanh(inner)
    activation = (0.5 * hidden * (1.0 + tangent)).astype(jnp.bfloat16)
    slope = 0.5 * (1.0 + tangent) + 0.5 * hidden * (1.0 - tangent * tangent) * gelu_scale * (
        1.0 + 3.0 * gelu_cubic * hidden * hidden
    )
    slope_grad = (cotangent.astype(jnp.float32) * slope).astype(jnp.bfloat16)
    return (activation, slope_grad)


def group_of(blocks, goal):
    return max(n for n in range(1, goal + 1) if blocks % n == 0)


class Core:
    def __init__(self):
        self.turn = None

    def __call__(self, kernel, name, out_shape, out_specs, in_specs, operands, scratch=(), aliases=None):
        homes = {id(in_vmem): pltpu.VMEM, id(anywhere): pltpu.HBM}
        in_specs, operands = list(in_specs), list(operands)
        if self.turn is not None:
            in_specs.append(in_vmem)
            operands.append(self.turn)
        taken = len(operands)
        given = len(out_shape)
        extra = self.turn is not None

        def body(*refs):
            refs[taken + given][...] = jnp.zeros((8, 128), jnp.float32)
            kernel(*refs[: taken - extra], *refs[taken : taken + given], *refs[taken + given + 1 :])

        placed = [
            pltpu.with_memory_space_constraint(x, homes[id(spec)]) if id(spec) in homes else x
            for x, spec in zip(operands, in_specs)
        ]
        *out, self.turn = pl.pallas_call(
            body,
            out_shape=[*out_shape, pltpu.VMEM((8, 128), jnp.float32)],
            in_specs=in_specs,
            out_specs=[*out_specs, in_vmem],
            scratch_shapes=list(scratch),
            input_output_aliases=aliases or {},
            compiler_params=pltpu.CompilerParams(vmem_limit_bytes=vmem_limit),
            cost_estimate=pl.CostEstimate(flops=1, transcendentals=0, bytes_accessed=1),
            name=name,
        )(*placed)
        return out


def dense_kernel(row_blocks, col_blocks, code, w_ref, *refs):
    out_ref, empty, sem = refs[-3:]
    blk = w_ref.shape[-1]
    empty[...] = jnp.zeros_like(empty)

    def load(at, carry):
        for r in range(row_blocks):
            entry = code[r * col_blocks + at]
            start = pl.multiple_of(at * blk, blk)
            target = out_ref.at[pl.ds(r * blk, blk), pl.ds(start, blk)]

            @pl.when(lax.rem(entry, 2) == 1)
            def _():
                pltpu.make_async_copy(w_ref.at[0, 0, lax.div(entry, 2)], target, sem).start()

            @pl.when(lax.rem(entry, 2) == 0)
            def _():
                pltpu.make_async_copy(empty, target, sem).start()

        return carry

    lax.fori_loop(0, col_blocks, load, 0)
    pltpu.make_async_copy(out_ref, out_ref, sem).wait()


def dense_tile(core, w_packed, code, row_blocks, col_blocks, ready):
    blk = w_packed.shape[-1]
    [weight] = core(
        functools.partial(dense_kernel, row_blocks, col_blocks),
        "dense_tile",
        [pltpu.VMEM((row_blocks * blk, col_blocks * blk), w_packed.dtype)],
        [in_vmem],
        [in_smem, anywhere] + [in_smem] * len(ready),
        (code, w_packed, *ready),
        scratch=[pltpu.VMEM((blk, blk), w_packed.dtype), pltpu.SemaphoreType.DMA],
    )
    return weight


def arrange_kernel(groups, rows, pieces, pick, *refs):
    out_ref, turned_ref, all_ref = refs[pieces:]
    each = groups // pieces
    for m in range(pieces):
        for j in range(each):
            all_ref[m * each + j] = refs[m][j]
    for t in range(groups):
        out_ref[pl.ds(t * rows, rows), :] = all_ref[pick[t]]
    turned_ref[...] = out_ref[...].T


def arrange(core, pieces, pick):
    groups = pick.shape[0]
    rows, tall = pieces[0].shape[1:]
    kind = pieces[0].dtype
    return core(
        functools.partial(arrange_kernel, groups, rows, len(pieces)),
        "arrange",
        [pltpu.VMEM((groups * rows, tall), kind), pltpu.VMEM((tall, groups * rows), kind)],
        [in_vmem, in_vmem],
        [in_smem] + [in_vmem] * len(pieces),
        (pick, *pieces),
        scratch=[pltpu.VMEM((groups, rows, tall), kind)],
    )


def forward_kernel(first, wide, x_ref, w_ref, keep_ref, send_ref):
    half, width = keep_ref.shape
    for at in range(0, width, wide):
        product = jnp.dot(
            x_ref[...], w_ref[:, first + at : first + at + wide], preferred_element_type=jnp.float32
        )
        keep_ref[:, at : at + wide] = product[:half]
        send_ref[:, at : at + wide] = product[half:].astype(jnp.bfloat16)


def forward(core, features, weight, first, width):
    half = features.shape[0] // 2
    wide = 128 * group_of(width // 128, 4)
    return core(
        functools.partial(forward_kernel, first, wide),
        "forward",
        [pltpu.VMEM((half, width), jnp.float32), pltpu.VMEM((half, width), jnp.bfloat16)],
        [in_vmem, in_vmem],
        [in_vmem, in_vmem],
        (features, weight),
    )


def sides(left, bit):
    at = len(left) - 1 - left.index(bit)
    names = range(1 << len(left))
    return [g for g in names if not g >> at & 1], [g for g in names if g >> at & 1]


def add_kernel(rows, stay, leave, keep_ref, arrived_ref, next_ref, send_ref):
    for out_ref, groups in ((next_ref, stay), (send_ref, leave)):
        for at, g in enumerate(groups):
            here = slice(g * rows, (g + 1) * rows)
            total = keep_ref[here, :] + arrived_ref[here, :].astype(jnp.float32)
            out_ref[at * rows : (at + 1) * rows, :] = total.astype(out_ref.dtype)


def add_step(core, keep, arrived, left, bit):
    rows = keep.shape[0] >> len(left)
    half = (keep.shape[0] // 2, keep.shape[1])
    return core(
        functools.partial(add_kernel, rows, *sides(left, bit)),
        "add_step",
        [pltpu.VMEM(half, jnp.float32), pltpu.VMEM(half, jnp.bfloat16)],
        [in_vmem, in_vmem],
        [in_vmem, in_vmem],
        (keep, arrived),
    )


def join_kernel(rows, stay, come, near_ref, arrived_ref, out_ref):
    for in_ref, groups in ((near_ref, stay), (arrived_ref, come)):
        for at, g in enumerate(groups):
            out_ref[g * rows : (g + 1) * rows, :] = in_ref[at * rows : (at + 1) * rows, :]


def join_step(core, near, arrived, held, bit):
    rows = 2 * near.shape[0] >> len(held)
    [out] = core(
        functools.partial(join_kernel, rows, *sides(held, bit)),
        "join_step",
        [pltpu.VMEM((2 * near.shape[0], near.shape[1]), near.dtype)],
        [in_vmem],
        [in_vmem, in_vmem],
        (near, arrived),
    )
    return out


def gelu_kernel(top, first, keep_ref, arrived_ref, cotangent_ref, activation_ref, slope_ref):
    rows, width = keep_ref.shape
    hidden = keep_ref[...] + arrived_ref[...].astype(jnp.float32)
    cotangent = cotangent_ref[top : top + rows, first : first + width]
    activation_ref[...], slope_ref[...] = gelu_pair(hidden, cotangent)


def gelu(core, keep, arrived, cotangent, top, first):
    out = pltpu.VMEM(keep.shape, jnp.bfloat16)
    return core(
        functools.partial(gelu_kernel, top, first),
        "gelu",
        [out, out],
        [in_vmem, in_vmem],
        [in_vmem] * 3,
        (keep, arrived, cotangent),
    )


def input_kernel(first, groups, has_before, finished, given, place, near_ref, far_ref, w_ref, *refs):
    half, width = near_ref.shape
    rows = 2 * half // groups
    tall = w_ref.shape[0]
    before = refs[0] if has_before else None
    outs = refs[has_before : has_before + given]
    scratch = refs[has_before + given :]
    turned = scratch[0]
    total = scratch[1] if finished else outs[0]
    wide = 128 * group_of(width // 128, 4)
    for at in range(0, width, wide):
        here = slice(at, at + wide)
        grad = jnp.concatenate([near_ref[:, here], far_ref[:, here]], axis=0)
        turned[here, :] = grad.T
    high = 128 * group_of(tall // 128, 4)
    for at in range(0, tall, high):
        here = slice(at, at + high)
        product = jnp.dot(
            w_ref[here, first : first + width], turned[...], preferred_element_type=jnp.float32
        )
        total[here, :] = product + before[here, :] if has_before else product
    if finished:
        upright = scratch[2]
        upright[...] = total[...].T
        each = groups // given
        for i in range(groups):
            start = pl.multiple_of(place[i] * rows, rows)
            out_ref = outs[i // each]
            at = i % each * rows
            out_ref[at : at + rows, :] = upright[pl.ds(start, rows), :].astype(out_ref.dtype)


def input_partial(core, near, far, weight, first, place, before, pieces):
    half, width = near.shape
    tall = weight.shape[0]
    both = 2 * half
    if pieces:
        outs = [pltpu.VMEM((both // pieces, tall), jnp.float32)]
        outs += [pltpu.VMEM((both // pieces, tall), jnp.bfloat16)] * (pieces - 1)
    else:
        outs = [pltpu.VMEM((tall, both), jnp.float32)]
    has_before = before is not None
    scratch = [pltpu.VMEM((width, both), near.dtype)]
    if pieces:
        scratch += [pltpu.VMEM((tall, both), jnp.float32), pltpu.VMEM((both, tall), jnp.float32)]
    return core(
        functools.partial(
            input_kernel, first, place.shape[0], has_before, pieces > 0, len(outs)
        ),
        "input_partial",
        outs,
        [in_vmem] * len(outs),
        [in_smem] + [in_vmem] * (4 if has_before else 3),
        (place, near, far, weight) + ((before,) if has_before else ()),
        scratch=scratch,
    )


def weight_kernel(row_blocks, col_blocks, first, parts, has_before, code, *refs):
    turned = refs[:parts]
    grads = refs[parts : 3 * parts]
    out_ref, made, sem = refs[3 * parts + has_before :]
    blk = made.shape[-1]
    width = grads[0].shape[1]
    here = width // blk
    per_step = group_of(here, 2)
    wide = per_step * blk
    for j in range(here // per_step):
        features = jnp.concatenate([t[...] for t in turned], axis=1)
        grad = jnp.concatenate([g[:, j * wide : (j + 1) * wide] for g in grads], axis=0)
        product = jnp.dot(features, grad, preferred_element_type=jnp.float32)
        for r in range(row_blocks):
            for c in range(per_step):
                entry = code[r * col_blocks + first // blk + j * per_step + c]
                live = lax.rem(entry, 2).astype(jnp.float32)
                at = (j * row_blocks + r) * per_step + c
                block = product[r * blk : (r + 1) * blk, c * blk : (c + 1) * blk] * live
                made[at] = block.astype(made.dtype)
                pltpu.make_async_copy(
                    made.at[at], out_ref.at[0, 0, lax.div(entry, 2)], sem
                ).start(priority=at % 2)
    pltpu.make_async_copy(made, out_ref.at[0, 0, pl.ds(0, made.shape[0])], sem).wait()


def weight_gradient(core, turned, grads, code, first, row_blocks, col_blocks, blk, before):
    parts = len(turned)
    has_before = before is not None
    here = row_blocks * grads[0].shape[1] // blk
    arrays = [*turned, *grads]
    [out] = core(
        functools.partial(weight_kernel, row_blocks, col_blocks, first, parts, has_before),
        "weight_gradient",
        [jax.ShapeDtypeStruct((1, 1, row_blocks * col_blocks, blk, blk), jnp.bfloat16)],
        [anywhere],
        [in_smem] + [in_vmem] * len(arrays) + [anywhere] * has_before,
        (code, *arrays) + ((before,) if has_before else ()),
        scratch=[pltpu.VMEM((here, blk, blk), jnp.bfloat16), pltpu.SemaphoreType.DMA],
        aliases={1 + len(arrays): 0} if has_before else None,
    )
    return out


def place_kernel(spots, *refs):
    blocks = refs[: len(spots)]
    out_ref, sems = refs[len(spots) :]
    copies = []
    for at, (top, first) in enumerate(spots):
        rows, width = blocks[at].shape
        target = out_ref.at[pl.ds(top, rows), pl.ds(first, width)]
        copies.append(pltpu.make_async_copy(blocks[at], target, sems.at[at]))
        copies[-1].start()
    for copy in copies:
        copy.wait()


def place_activation(core, blocks, spots, shape):
    [out] = core(
        functools.partial(place_kernel, spots),
        "place_activation",
        [jax.ShapeDtypeStruct(shape, jnp.bfloat16)],
        [anywhere],
        [in_vmem] * len(blocks),
        blocks,
        scratch=[pltpu.SemaphoreType.DMA((len(blocks),))],
    )
    return out


def total_kernel(each, many, starts, sizes, *refs):
    out_ref = refs[-1]
    own = sum(sizes)
    for k, (start, rows) in enumerate(zip(starts, sizes)):
        found = refs[sum(many[:k]) : sum(many[: k + 1])]
        for j in range(each):
            here = slice(j * rows, (j + 1) * rows)
            total = found[0][here, :]
            for piece in found[1:]:
                total = total + piece[here, :].astype(jnp.float32)
            top = j * own + start
            out_ref[top : top + rows, :] = total.astype(jnp.bfloat16)


def total_input(core, found, each, starts, sizes):
    arrays = [x for part in found for x in part]
    shape = (each * sum(sizes), arrays[0].shape[1])
    [out] = core(
        functools.partial(total_kernel, each, [len(part) for part in found], starts, sizes),
        "total_input",
        [jax.ShapeDtypeStruct(shape, jnp.bfloat16)],
        [pl.BlockSpec(shape, lambda: (0, 0))],
        [in_vmem] * len(arrays),
        arrays,
    )
    return out


def swap(array, axis, size, bit):
    return lax.ppermute(array, axis, [(i, i ^ bit) for i in range(size)])


def on_device(tokens, w_packed, kept_rows, kept_cols, kept_count, grad_act):
    blk = w_packed.shape[-1]
    slot_count = w_packed.shape[2]
    tall = tokens.shape[1]
    row_tokens, hidden_here = grad_act.shape
    row_blocks = tall // blk
    col_blocks = hidden_here // blk
    n_row = lax.axis_size("row")
    n_col = lax.axis_size("col")
    row_me = lax.axis_index("row")
    col_me = lax.axis_index("col")
    col_groups = tokens.shape[0] // row_tokens
    tiles = row_tokens // 16
    shares = token_split if tiles % sum(token_split) == 0 else (1,)
    sizes = [16 * (tiles // sum(shares)) * share for share in shares]
    starts = [sum(sizes[:k]) for k in range(len(sizes))]
    parts = len(sizes)
    slabs = group_of(col_blocks, column_parts)
    width = hidden_here // slabs
    direct = n_col <= 8
    core = Core()

    places = kept_rows[0, 0] * col_blocks + kept_cols[0, 0]
    slots = jnp.arange(slot_count, dtype=jnp.int32)
    coded = slots * 2 + (slots < kept_count[0, 0]).astype(jnp.int32)
    code = jnp.sum(jnp.where(places[None, :] == slots[:, None], coded[None, :], 0), axis=1)

    apart = row_me ^ (col_me * col_groups) if direct else row_me
    everyone = np.arange(n_row)
    order = np.concatenate([everyone[::2], everyone[1::2]]).astype(np.int32)
    pick = (jnp.asarray(order) ^ apart).astype(jnp.int32)
    homes = []
    for origin in (row_me, apart):
        distance = jnp.asarray(everyone.astype(np.int32)) ^ origin
        homes.append(((distance & 1) * (n_row // 2) + (distance >> 1)).astype(jnp.int32))

    pieces = []
    for start, rows in zip(starts, sizes):
        mine = tokens.reshape(col_groups, row_tokens, tall)[:, start : start + rows]
        if direct:
            pieces.append([mine] + [swap(mine, "col", n_col, m) for m in range(1, n_col)])
        else:
            pieces.append([lax.all_gather(mine, "col", axis=0, tiled=True)])
    weight = dense_tile(core, w_packed, code, row_blocks, col_blocks, [pick, *homes])

    far_bits = [1 << b for b in range(1, n_row.bit_length() - 1)]
    units = [(k, c) for k in range(parts) for c in range(slabs)]
    paths = [far_bits if at % 2 == 0 else far_bits[::-1] for at in range(len(units))]
    state = {}
    full, turned = {}, {}
    activations, sums, input_grads = {}, {}, {}

    def begin(k, c, path):
        if c == 0:
            full[k], turned[k] = arrange(core, pieces[k], pick)
        keep, send = forward(core, full[k], weight, c * width, width)
        state[k, c] = (keep, swap(send, "row", n_row, 1))

    def add(at, k, c, path):
        left = sorted(path[at:], reverse=True)
        keep, send = add_step(core, *state[k, c], left, path[at])
        state[k, c] = (keep, swap(send, "row", n_row, path[at]))

    def bend(k, c, path):
        activations[k, c], near = gelu(core, *state[k, c], grad_act, starts[k], c * width)
        state[k, c] = (near, swap(near, "row", n_row, ([1] + path)[-1]))

    def join(at, k, c, path):
        held = sorted(path[at:], reverse=True)
        near = join_step(core, *state[k, c], held, path[at])
        state[k, c] = (near, swap(near, "row", n_row, ([1] + path)[at]))

    def finish(k, c, path):
        last = c + 1 == slabs
        straight = direct and k + 1 == parts
        cut = (n_col if straight else 1) * last
        found = input_partial(
            core, *state[k, c], weight, c * width, homes[straight], sums.get((k, c - 1)), cut
        )
        sums[k, c] = found[0]
        if last and straight:
            input_grads[k] = [found[0]]
            input_grads[k] += [swap(found[m], "col", n_col, m) for m in range(1, n_col)]
        elif last:
            input_grads[k] = [lax.psum_scatter(found[0], "col", scatter_dimension=0, tiled=True)]

    hops = len(far_bits)
    stages = [begin] + [functools.partial(add, at) for at in range(hops)] + [bend]
    stages += [functools.partial(join, at) for at in reversed(range(hops))] + [finish]
    plan = [(k, at) for at in range(len(stages)) for k in range(parts)]
    if parts == 2 and hops == 2:
        plan = [(0, 0), (0, 1), (0, 2), (1, 0), (1, 1), (0, 3), (0, 4), (1, 2), (0, 5), (1, 3), (1, 4), (0, 6), (1, 5), (1, 6)]
    for k, at in plan:
        for c in range(slabs):
            stages[at](k, c, paths[units.index((k, c))])
        if (k, at) == (parts - 1, len(stages) - 3):
            activation = place_activation(
                core,
                [activations[k, c] for k, c in units],
                [(starts[k], c * width) for k, c in units],
                grad_act.shape,
            )
    weight_grad = None
    for c in range(slabs):
        weight_grad = weight_gradient(
            core,
            [turned[k] for k in range(parts)],
            [g for k in range(parts) for g in state[k, c]],
            code,
            c * width,
            row_blocks,
            col_blocks,
            blk,
            weight_grad,
        )
    input_grad = total_input(
        core, [input_grads[k] for k in range(parts)], col_groups, starts, sizes
    )
    return (activation, input_grad, weight_grad)


def solution(mesh):
    placed = (
        P("col", "row"),
        P("row", "col", None, None, None),
        P("row", "col", None),
        P("row", "col", None),
        P("row", "col"),
        P("row", "col"),
    )
    return jax.shard_map(
        on_device,
        mesh=mesh,
        in_specs=placed,
        out_specs=(P("row", "col"), P("col", "row"), P("row", "col", None, None, None)),
        check_vma=False,
    )
```

```python
import functools

import jax
import jax.numpy as jnp
import numpy as np
from jax import lax
from jax.experimental import pallas as pl
from jax.experimental.pallas import tpu as pltpu
from jax.sharding import PartitionSpec as P

gelu_scale = 0.7978845608
gelu_cubic = 0.044715
token_split = (1, 1)
core_cuts = (1, 1)
column_parts = 2
vmem_limit = 16 * 1024 * 1024
in_vmem = pl.BlockSpec(memory_space=pltpu.VMEM)
in_smem = pl.BlockSpec(memory_space=pltpu.SMEM)
anywhere = pl.BlockSpec(memory_space=pltpu.HBM)


def gelu_pair(hidden, cotangent):
    inner = gelu_scale * (hidden + gelu_cubic * hidden * hidden * hidden)
    tangent = jnp.tanh(inner)
    activation = (0.5 * hidden * (1.0 + tangent)).astype(jnp.bfloat16)
    slope = 0.5 * (1.0 + tangent) + 0.5 * hidden * (1.0 - tangent * tangent) * gelu_scale * (
        1.0 + 3.0 * gelu_cubic * hidden * hidden
    )
    slope_grad = (cotangent.astype(jnp.float32) * slope).astype(jnp.bfloat16)
    return (activation, slope_grad)


def group_of(blocks, goal):
    return max(n for n in range(1, goal + 1) if blocks % n == 0)


class Core:
    def __init__(self):
        self.turn = None

    def __call__(self, kernel, name, out_shape, out_specs, in_specs, operands, scratch=(), aliases=None):
        homes = {id(in_vmem): pltpu.VMEM, id(anywhere): pltpu.HBM}
        in_specs, operands = list(in_specs), list(operands)
        if self.turn is not None:
            in_specs.append(in_vmem)
            operands.append(self.turn)
        taken = len(operands)
        given = len(out_shape)
        extra = self.turn is not None

        def body(*refs):
            refs[taken + given][...] = jnp.zeros((8, 128), jnp.float32)
            kernel(*refs[: taken - extra], *refs[taken : taken + given], *refs[taken + given + 1 :])

        placed = [
            pltpu.with_memory_space_constraint(x, homes[id(spec)]) if id(spec) in homes else x
            for x, spec in zip(operands, in_specs)
        ]
        *out, self.turn = pl.pallas_call(
            body,
            out_shape=[*out_shape, pltpu.VMEM((8, 128), jnp.float32)],
            in_specs=in_specs,
            out_specs=[*out_specs, in_vmem],
            scratch_shapes=list(scratch),
            input_output_aliases=aliases or {},
            compiler_params=pltpu.CompilerParams(vmem_limit_bytes=vmem_limit),
            cost_estimate=pl.CostEstimate(flops=1, transcendentals=0, bytes_accessed=1),
            name=name,
        )(*placed)
        return out


def dense_kernel(row_blocks, col_blocks, code, w_ref, *refs):
    out_ref, empty, sem = refs[-3:]
    blk = w_ref.shape[-1]
    empty[...] = jnp.zeros_like(empty)

    def load(at, carry):
        for r in range(row_blocks):
            entry = code[r * col_blocks + at]
            start = pl.multiple_of(at * blk, blk)
            target = out_ref.at[pl.ds(r * blk, blk), pl.ds(start, blk)]

            @pl.when(lax.rem(entry, 2) == 1)
            def _():
                pltpu.make_async_copy(w_ref.at[0, 0, lax.div(entry, 2)], target, sem).start()

            @pl.when(lax.rem(entry, 2) == 0)
            def _():
                pltpu.make_async_copy(empty, target, sem).start()

        return carry

    lax.fori_loop(0, col_blocks, load, 0)
    pltpu.make_async_copy(out_ref, out_ref, sem).wait()


def dense_tile(core, w_packed, code, row_blocks, col_blocks, ready):
    blk = w_packed.shape[-1]
    [weight] = core(
        functools.partial(dense_kernel, row_blocks, col_blocks),
        "dense_tile",
        [pltpu.VMEM((row_blocks * blk, col_blocks * blk), w_packed.dtype)],
        [in_vmem],
        [in_smem, anywhere] + [in_smem] * len(ready),
        (code, w_packed, *ready),
        scratch=[pltpu.VMEM((blk, blk), w_packed.dtype), pltpu.SemaphoreType.DMA],
    )
    return weight


def arrange_kernel(groups, rows, pieces, pick, *refs):
    out_ref, turned_ref, all_ref = refs[pieces:]
    each = groups // pieces
    for m in range(pieces):
        for j in range(each):
            all_ref[m * each + j] = refs[m][j]
    for t in range(groups):
        out_ref[pl.ds(t * rows, rows), :] = all_ref[pick[t]]
    turned_ref[...] = out_ref[...].T


def arrange(core, pieces, pick):
    groups = pick.shape[0]
    rows, tall = pieces[0].shape[1:]
    kind = pieces[0].dtype
    return core(
        functools.partial(arrange_kernel, groups, rows, len(pieces)),
        "arrange",
        [pltpu.VMEM((groups * rows, tall), kind), pltpu.VMEM((tall, groups * rows), kind)],
        [in_vmem, in_vmem],
        [in_smem] + [in_vmem] * len(pieces),
        (pick, *pieces),
        scratch=[pltpu.VMEM((groups, rows, tall), kind)],
    )


def forward_kernel(first, wide, x_ref, w_ref, keep_ref, *send_refs):
    half, width = keep_ref.shape
    cut = half // len(send_refs)
    for at in range(0, width, wide):
        product = jnp.dot(
            x_ref[...], w_ref[:, first + at : first + at + wide], preferred_element_type=jnp.float32
        )
        keep_ref[:, at : at + wide] = product[:half]
        for i, send_ref in enumerate(send_refs):
            top = half + i * cut
            send_ref[:, at : at + wide] = product[top : top + cut].astype(jnp.bfloat16)


def forward(core, features, weight, first, width, cuts):
    half = features.shape[0] // 2
    wide = 128 * group_of(width // 128, 4)
    return core(
        functools.partial(forward_kernel, first, wide),
        "forward",
        [pltpu.VMEM((half, width), jnp.float32)]
        + [pltpu.VMEM((half // cuts, width), jnp.bfloat16)] * cuts,
        [in_vmem] * (1 + cuts),
        [in_vmem, in_vmem],
        (features, weight),
    )


def sides(left, bit):
    at = len(left) - 1 - left.index(bit)
    names = range(1 << len(left))
    return [g for g in names if not g >> at & 1], [g for g in names if g >> at & 1]


def add_kernel(rows, stay, leave, pieces, keep_ref, *refs):
    arrived = refs[:pieces]
    each = arrived[0].shape[0] // rows
    for out_ref, groups in zip(refs[pieces:], (stay, leave)):
        for at, g in enumerate(groups):
            other = arrived[g // each][g % each * rows : (g % each + 1) * rows, :]
            total = keep_ref[g * rows : (g + 1) * rows, :] + other.astype(jnp.float32)
            out_ref[at * rows : (at + 1) * rows, :] = total.astype(out_ref.dtype)


def add_step(core, keep, arrived, left, bit):
    rows = keep.shape[0] >> len(left)
    half = (keep.shape[0] // 2, keep.shape[1])
    return core(
        functools.partial(add_kernel, rows, *sides(left, bit), len(arrived)),
        "add_step",
        [pltpu.VMEM(half, jnp.float32), pltpu.VMEM(half, jnp.bfloat16)],
        [in_vmem, in_vmem],
        [in_vmem] * (1 + len(arrived)),
        (keep, *arrived),
    )


def join_kernel(rows, stay, come, near_ref, arrived_ref, out_ref):
    for in_ref, groups in ((near_ref, stay), (arrived_ref, come)):
        for at, g in enumerate(groups):
            out_ref[g * rows : (g + 1) * rows, :] = in_ref[at * rows : (at + 1) * rows, :]


def join_step(core, near, arrived, held, bit):
    rows = 2 * near.shape[0] >> len(held)
    [out] = core(
        functools.partial(join_kernel, rows, *sides(held, bit)),
        "join_step",
        [pltpu.VMEM((2 * near.shape[0], near.shape[1]), near.dtype)],
        [in_vmem],
        [in_vmem, in_vmem],
        (near, arrived),
    )
    return out


def gelu_kernel(top, first, keep_ref, arrived_ref, cotangent_ref, activation_ref, slope_ref):
    rows, width = keep_ref.shape
    hidden = keep_ref[...] + arrived_ref[...].astype(jnp.float32)
    cotangent = cotangent_ref[top : top + rows, first : first + width]
    activation_ref[...], slope_ref[...] = gelu_pair(hidden, cotangent)


def gelu(core, keep, arrived, cotangent, top, first):
    out = pltpu.VMEM(keep.shape, jnp.bfloat16)
    return core(
        functools.partial(gelu_kernel, top, first),
        "gelu",
        [out, out],
        [in_vmem, in_vmem],
        [in_vmem] * 3,
        (keep, arrived, cotangent),
    )


def input_kernel(first, groups, has_before, finished, given, place, near_ref, far_ref, w_ref, *refs):
    half, width = near_ref.shape
    rows = 2 * half // groups
    tall = w_ref.shape[0]
    before = refs[0] if has_before else None
    outs = refs[has_before : has_before + given]
    scratch = refs[has_before + given :]
    turned = scratch[0]
    total = scratch[1] if finished else outs[0]
    wide = 128 * group_of(width // 128, 4)
    for at in range(0, width, wide):
        here = slice(at, at + wide)
        grad = jnp.concatenate([near_ref[:, here], far_ref[:, here]], axis=0)
        turned[here, :] = grad.T
    high = 128 * group_of(tall // 128, 4)
    for at in range(0, tall, high):
        here = slice(at, at + high)
        product = jnp.dot(
            w_ref[here, first : first + width], turned[...], preferred_element_type=jnp.float32
        )
        total[here, :] = product + before[here, :] if has_before else product
    if finished:
        upright = scratch[2]
        upright[...] = total[...].T
        each = groups // given
        for i in range(groups):
            start = pl.multiple_of(place[i] * rows, rows)
            out_ref = outs[i // each]
            at = i % each * rows
            out_ref[at : at + rows, :] = upright[pl.ds(start, rows), :].astype(out_ref.dtype)


def input_partial(core, near, far, weight, first, place, before, pieces):
    half, width = near.shape
    tall = weight.shape[0]
    both = 2 * half
    if pieces:
        outs = [pltpu.VMEM((both // pieces, tall), jnp.float32)]
        outs += [pltpu.VMEM((both // pieces, tall), jnp.bfloat16)] * (pieces - 1)
    else:
        outs = [pltpu.VMEM((tall, both), jnp.float32)]
    has_before = before is not None
    scratch = [pltpu.VMEM((width, both), near.dtype)]
    if pieces:
        scratch += [pltpu.VMEM((tall, both), jnp.float32), pltpu.VMEM((both, tall), jnp.float32)]
    return core(
        functools.partial(
            input_kernel, first, place.shape[0], has_before, pieces > 0, len(outs)
        ),
        "input_partial",
        outs,
        [in_vmem] * len(outs),
        [in_smem] + [in_vmem] * (4 if has_before else 3),
        (place, near, far, weight) + ((before,) if has_before else ()),
        scratch=scratch,
    )


def weight_kernel(row_blocks, col_blocks, first, parts, has_before, code, *refs):
    turned = refs[:parts]
    grads = refs[parts : 3 * parts]
    out_ref, made, sem = refs[3 * parts + has_before :]
    blk = made.shape[-1]
    width = grads[0].shape[1]
    here = width // blk
    per_step = group_of(here, 2)
    wide = per_step * blk
    for j in range(here // per_step):
        features = jnp.concatenate([t[...] for t in turned], axis=1)
        grad = jnp.concatenate([g[:, j * wide : (j + 1) * wide] for g in grads], axis=0)
        product = jnp.dot(features, grad, preferred_element_type=jnp.float32)
        for r in range(row_blocks):
            for c in range(per_step):
                entry = code[r * col_blocks + first // blk + j * per_step + c]
                live = lax.rem(entry, 2).astype(jnp.float32)
                at = (j * row_blocks + r) * per_step + c
                block = product[r * blk : (r + 1) * blk, c * blk : (c + 1) * blk] * live
                made[at] = block.astype(made.dtype)
                pltpu.make_async_copy(
                    made.at[at], out_ref.at[0, 0, lax.div(entry, 2)], sem
                ).start(priority=at % 2)
    pltpu.make_async_copy(made, out_ref.at[0, 0, pl.ds(0, made.shape[0])], sem).wait()


def weight_gradient(core, turned, grads, code, first, row_blocks, col_blocks, blk, before):
    parts = len(turned)
    has_before = before is not None
    here = row_blocks * grads[0].shape[1] // blk
    arrays = [*turned, *grads]
    [out] = core(
        functools.partial(weight_kernel, row_blocks, col_blocks, first, parts, has_before),
        "weight_gradient",
        [jax.ShapeDtypeStruct((1, 1, row_blocks * col_blocks, blk, blk), jnp.bfloat16)],
        [anywhere],
        [in_smem] + [in_vmem] * len(arrays) + [anywhere] * has_before,
        (code, *arrays) + ((before,) if has_before else ()),
        scratch=[pltpu.VMEM((here, blk, blk), jnp.bfloat16), pltpu.SemaphoreType.DMA],
        aliases={1 + len(arrays): 0} if has_before else None,
    )
    return out


def place_kernel(spots, *refs):
    blocks = refs[: len(spots)]
    out_ref, sems = refs[len(spots) :]
    copies = []
    for at, (top, first) in enumerate(spots):
        rows, width = blocks[at].shape
        target = out_ref.at[pl.ds(top, rows), pl.ds(first, width)]
        copies.append(pltpu.make_async_copy(blocks[at], target, sems.at[at]))
        copies[-1].start()
    for copy in copies:
        copy.wait()


def place_activation(core, blocks, spots, shape):
    [out] = core(
        functools.partial(place_kernel, spots),
        "place_activation",
        [jax.ShapeDtypeStruct(shape, jnp.bfloat16)],
        [anywhere],
        [in_vmem] * len(blocks),
        blocks,
        scratch=[pltpu.SemaphoreType.DMA((len(blocks),))],
    )
    return out


def total_kernel(found, done, each, starts, sizes, *refs):
    out_ref = refs[-1]
    own = sum(sizes)
    for k, (start, rows) in enumerate(zip(starts, sizes)):
        for j in range(each):
            here = slice(j * rows, (j + 1) * rows)
            top = j * own + start
            if k < done:
                out_ref[top : top + rows, :] = refs[k][here, :]
            else:
                total = refs[done][here, :]
                for piece in refs[done + 1 : done + found]:
                    total = total + piece[here, :].astype(jnp.float32)
                out_ref[top : top + rows, :] = total.astype(jnp.bfloat16)


def total_input(core, found, done, each, starts, sizes, last):
    shape = (each * sum(sizes), found[0].shape[1])
    arrays = [*done, *found]
    [out] = core(
        functools.partial(total_kernel, len(found), len(done), each, starts, sizes),
        "total_input",
        [jax.ShapeDtypeStruct(shape, jnp.bfloat16) if last else pltpu.VMEM(shape, jnp.bfloat16)],
        [pl.BlockSpec(shape, lambda: (0, 0)) if last else in_vmem],
        [in_vmem] * len(arrays),
        arrays,
    )
    return out


def swap(array, axis, size, bit):
    return lax.ppermute(array, axis, [(i, i ^ bit) for i in range(size)])


def on_device(tokens, w_packed, kept_rows, kept_cols, kept_count, grad_act):
    blk = w_packed.shape[-1]
    slot_count = w_packed.shape[2]
    tall = tokens.shape[1]
    row_tokens, hidden_here = grad_act.shape
    row_blocks = tall // blk
    col_blocks = hidden_here // blk
    n_row = lax.axis_size("row")
    n_col = lax.axis_size("col")
    row_me = lax.axis_index("row")
    col_me = lax.axis_index("col")
    col_groups = tokens.shape[0] // row_tokens
    tiles = row_tokens // 16
    shares = token_split if tiles % sum(token_split) == 0 else (1,)
    sizes = [16 * (tiles // sum(shares)) * share for share in shares]
    starts = [sum(sizes[:k]) for k in range(len(sizes))]
    parts = len(sizes)
    slabs = group_of(col_blocks, column_parts)
    width = hidden_here // slabs
    direct = n_col <= 8
    core = Core()

    places = kept_rows[0, 0] * col_blocks + kept_cols[0, 0]
    slots = jnp.arange(slot_count, dtype=jnp.int32)
    coded = slots * 2 + (slots < kept_count[0, 0]).astype(jnp.int32)
    code = jnp.sum(jnp.where(places[None, :] == slots[:, None], coded[None, :], 0), axis=1)

    apart = row_me ^ (col_me * col_groups) if direct else row_me
    everyone = np.arange(n_row)
    order = np.concatenate([everyone[::2], everyone[1::2]]).astype(np.int32)
    pick = (jnp.asarray(order) ^ apart).astype(jnp.int32)
    distance = jnp.asarray(everyone.astype(np.int32)) ^ apart
    place = ((distance & 1) * (n_row // 2) + (distance >> 1)).astype(jnp.int32)

    pieces = []
    for start, rows in zip(starts, sizes):
        mine = tokens.reshape(col_groups, row_tokens, tall)[:, start : start + rows]
        if direct:
            pieces.append([mine] + [swap(mine, "col", n_col, m) for m in range(1, n_col)])
        else:
            pieces.append([lax.all_gather(mine, "col", axis=0, tiled=True)])
    weight = dense_tile(core, w_packed, code, row_blocks, col_blocks, [pick, place])

    far_bits = [1 << b for b in range(1, n_row.bit_length() - 1)]
    units = [(k, c) for k in range(parts) for c in range(slabs)]
    paths = [far_bits if at % 2 == 0 else far_bits[::-1] for at in range(len(units))]
    state = {}
    full, turned = {}, {}
    activations, sums, input_grads = {}, {}, {}

    def begin(k, c, path):
        if c == 0:
            full[k], turned[k] = arrange(core, pieces[k], pick)
        keep, *send = forward(core, full[k], weight, c * width, width, core_cuts[min(k, 1)])
        state[k, c] = (keep, [swap(x, "row", n_row, 1) for x in send])

    def add(at, k, c, path):
        left = sorted(path[at:], reverse=True)
        keep, send = add_step(core, *state[k, c], left, path[at])
        state[k, c] = (keep, [swap(send, "row", n_row, path[at])])

    def bend(k, c, path):
        activations[k, c], near = gelu(core, state[k, c][0], state[k, c][1][0], grad_act, starts[k], c * width)
        state[k, c] = (near, swap(near, "row", n_row, ([1] + path)[-1]))

    def join(at, k, c, path):
        held = sorted(path[at:], reverse=True)
        near = join_step(core, *state[k, c], held, path[at])
        state[k, c] = (near, swap(near, "row", n_row, ([1] + path)[at]))

    def finish(k, c, path):
        last = c + 1 == slabs
        cut = (n_col if direct else 1) * last
        found = input_partial(
            core, *state[k, c], weight, c * width, place, sums.get((k, c - 1)), cut
        )
        sums[k, c] = found[0]
        if last and direct:
            input_grads[k] = [found[0]]
            input_grads[k] += [swap(found[m], "col", n_col, m) for m in range(1, n_col)]
        elif last:
            total = found[0].reshape(n_col, col_groups * sizes[k], tall)
            total = lax.psum_scatter(total, "col", scatter_dimension=0, tiled=True)[0]
            input_grads[k] = [total]

    sums_done = {}

    def collect(k):
        sums_done[k] = total_input(
            core, input_grads[k], [], col_groups, [0], [sizes[k]], False
        )

    hops = len(far_bits)
    stages = [begin] + [functools.partial(add, at) for at in range(hops)] + [bend]
    stages += [functools.partial(join, at) for at in reversed(range(hops))] + [finish]
    plan = [(k, at) for at in range(len(stages)) for k in range(parts)]
    if parts == 2 and hops == 2:
        plan = [(0, 0), (0, 1), (0, 2), (1, 0), (1, 1), (0, 3), (0, 4), (1, 2), (0, 5), (1, 3), (1, 4), (0, 6), (1, 5), (1, 6)]
    plan += [(k, len(stages)) for k in range(parts - 1) if (k, len(stages)) not in plan]
    for k, at in plan:
        if at == len(stages):
            collect(k)
            continue
        for c in range(slabs):
            stages[at](k, c, paths[units.index((k, c))])
        if (k, at) == (parts - 1, len(stages) - 3):
            activation = place_activation(
                core,
                [activations[k, c] for k, c in units],
                [(starts[k], c * width) for k, c in units],
                grad_act.shape,
            )
    weight_grad = None
    for c in range(slabs):
        weight_grad = weight_gradient(
            core,
            [turned[k] for k in range(parts)],
            [g for k in range(parts) for g in state[k, c]],
            code,
            c * width,
            row_blocks,
            col_blocks,
            blk,
            weight_grad,
        )
    done = [sums_done[k] for k in range(parts - 1)]
    input_grad = total_input(core, input_grads[parts - 1], done, col_groups, starts, sizes, True)
    return (activation, input_grad, weight_grad)


def solution(mesh):
    placed = (
        P("col", "row"),
        P("row", "col", None, None, None),
        P("row", "col", None),
        P("row", "col", None),
        P("row", "col"),
        P("row", "col"),
    )
    return jax.shard_map(
        on_device,
        mesh=mesh,
        in_specs=placed,
        out_specs=(P("row", "col"), P("col", "row"), P("row", "col", None, None, None)),
        check_vma=False,
    )
```

```python
import functools

import jax
import jax.numpy as jnp
import numpy as np
from jax import lax
from jax.experimental import pallas as pl
from jax.experimental.pallas import tpu as pltpu
from jax.sharding import PartitionSpec as P

gelu_scale = 0.7978845608
gelu_cubic = 0.044715
token_split = (1, 1)
column_parts = 2
vmem_limit = 16 * 1024 * 1024
in_vmem = pl.BlockSpec(memory_space=pltpu.VMEM)
in_smem = pl.BlockSpec(memory_space=pltpu.SMEM)
anywhere = pl.BlockSpec(memory_space=pltpu.HBM)


def gelu_pair(hidden, cotangent):
    inner = gelu_scale * (hidden + gelu_cubic * hidden * hidden * hidden)
    tangent = jnp.tanh(inner)
    activation = (0.5 * hidden * (1.0 + tangent)).astype(jnp.bfloat16)
    slope = 0.5 * (1.0 + tangent) + 0.5 * hidden * (1.0 - tangent * tangent) * gelu_scale * (
        1.0 + 3.0 * gelu_cubic * hidden * hidden
    )
    slope_grad = (cotangent.astype(jnp.float32) * slope).astype(jnp.bfloat16)
    return (activation, slope_grad)


def group_of(blocks, goal):
    return max(n for n in range(1, goal + 1) if blocks % n == 0)


class Core:
    def __init__(self):
        self.turn = None

    def __call__(self, kernel, name, out_shape, out_specs, in_specs, operands, scratch=(), aliases=None):
        homes = {id(in_vmem): pltpu.VMEM, id(anywhere): pltpu.HBM}
        in_specs, operands = list(in_specs), list(operands)
        if self.turn is not None:
            in_specs.append(in_vmem)
            operands.append(self.turn)
        taken = len(operands)
        given = len(out_shape)
        extra = self.turn is not None

        def body(*refs):
            refs[taken + given][...] = jnp.zeros((8, 128), jnp.float32)
            kernel(*refs[: taken - extra], *refs[taken : taken + given], *refs[taken + given + 1 :])

        placed = [
            pltpu.with_memory_space_constraint(x, homes[id(spec)]) if id(spec) in homes else x
            for x, spec in zip(operands, in_specs)
        ]
        *out, self.turn = pl.pallas_call(
            body,
            out_shape=[*out_shape, pltpu.VMEM((8, 128), jnp.float32)],
            in_specs=in_specs,
            out_specs=[*out_specs, in_vmem],
            scratch_shapes=list(scratch),
            input_output_aliases=aliases or {},
            compiler_params=pltpu.CompilerParams(vmem_limit_bytes=vmem_limit),
            cost_estimate=pl.CostEstimate(flops=1, transcendentals=0, bytes_accessed=1),
            name=name,
        )(*placed)
        return out


def dense_kernel(row_blocks, col_blocks, code, w_ref, *refs):
    out_ref, empty, sem = refs[-3:]
    blk = w_ref.shape[-1]
    empty[...] = jnp.zeros_like(empty)

    def load(at, carry):
        for r in range(row_blocks):
            entry = code[r * col_blocks + at]
            start = pl.multiple_of(at * blk, blk)
            target = out_ref.at[pl.ds(r * blk, blk), pl.ds(start, blk)]

            @pl.when(lax.rem(entry, 2) == 1)
            def _():
                pltpu.make_async_copy(w_ref.at[0, 0, lax.div(entry, 2)], target, sem).start()

            @pl.when(lax.rem(entry, 2) == 0)
            def _():
                pltpu.make_async_copy(empty, target, sem).start()

        return carry

    lax.fori_loop(0, col_blocks, load, 0)
    pltpu.make_async_copy(out_ref, out_ref, sem).wait()


def dense_tile(core, w_packed, code, row_blocks, col_blocks, ready):
    blk = w_packed.shape[-1]
    [weight] = core(
        functools.partial(dense_kernel, row_blocks, col_blocks),
        "dense_tile",
        [pltpu.VMEM((row_blocks * blk, col_blocks * blk), w_packed.dtype)],
        [in_vmem],
        [in_smem, anywhere] + [in_smem] * len(ready),
        (code, w_packed, *ready),
        scratch=[pltpu.VMEM((blk, blk), w_packed.dtype), pltpu.SemaphoreType.DMA],
    )
    return weight


def arrange_kernel(groups, rows, pieces, pick, *refs):
    out_ref, turned_ref, all_ref = refs[pieces:]
    each = groups // pieces
    for m in range(pieces):
        for j in range(each):
            all_ref[m * each + j] = refs[m][j]
    for t in range(groups):
        out_ref[pl.ds(t * rows, rows), :] = all_ref[pick[t]]
    turned_ref[...] = out_ref[...].T


def arrange(core, pieces, pick):
    groups = pick.shape[0]
    rows, tall = pieces[0].shape[1:]
    kind = pieces[0].dtype
    return core(
        functools.partial(arrange_kernel, groups, rows, len(pieces)),
        "arrange",
        [pltpu.VMEM((groups * rows, tall), kind), pltpu.VMEM((tall, groups * rows), kind)],
        [in_vmem, in_vmem],
        [in_smem] + [in_vmem] * len(pieces),
        (pick, *pieces),
        scratch=[pltpu.VMEM((groups, rows, tall), kind)],
    )


def forward_kernel(first, wide, x_ref, w_ref, keep_ref, send_ref):
    half, width = keep_ref.shape
    for at in range(0, width, wide):
        product = jnp.dot(
            x_ref[...], w_ref[:, first + at : first + at + wide], preferred_element_type=jnp.float32
        )
        keep_ref[:, at : at + wide] = product[:half]
        send_ref[:, at : at + wide] = product[half:].astype(jnp.bfloat16)


def forward(core, features, weight, first, width):
    half = features.shape[0] // 2
    wide = 128 * group_of(width // 128, 4)
    return core(
        functools.partial(forward_kernel, first, wide),
        "forward",
        [pltpu.VMEM((half, width), jnp.float32), pltpu.VMEM((half, width), jnp.bfloat16)],
        [in_vmem, in_vmem],
        [in_vmem, in_vmem],
        (features, weight),
    )


def sides(left, bit):
    at = len(left) - 1 - left.index(bit)
    names = range(1 << len(left))
    return [g for g in names if not g >> at & 1], [g for g in names if g >> at & 1]


def add_kernel(rows, stay, leave, keep_ref, arrived_ref, next_ref, send_ref):
    for out_ref, groups in ((next_ref, stay), (send_ref, leave)):
        for at, g in enumerate(groups):
            here = slice(g * rows, (g + 1) * rows)
            total = keep_ref[here, :] + arrived_ref[here, :].astype(jnp.float32)
            out_ref[at * rows : (at + 1) * rows, :] = total.astype(out_ref.dtype)


def add_step(core, keep, arrived, left, bit):
    rows = keep.shape[0] >> len(left)
    half = (keep.shape[0] // 2, keep.shape[1])
    return core(
        functools.partial(add_kernel, rows, *sides(left, bit)),
        "add_step",
        [pltpu.VMEM(half, jnp.float32), pltpu.VMEM(half, jnp.bfloat16)],
        [in_vmem, in_vmem],
        [in_vmem, in_vmem],
        (keep, arrived),
    )


def join_kernel(rows, stay, come, near_ref, arrived_ref, out_ref):
    for in_ref, groups in ((near_ref, stay), (arrived_ref, come)):
        for at, g in enumerate(groups):
            out_ref[g * rows : (g + 1) * rows, :] = in_ref[at * rows : (at + 1) * rows, :]


def join_step(core, near, arrived, held, bit):
    rows = 2 * near.shape[0] >> len(held)
    [out] = core(
        functools.partial(join_kernel, rows, *sides(held, bit)),
        "join_step",
        [pltpu.VMEM((2 * near.shape[0], near.shape[1]), near.dtype)],
        [in_vmem],
        [in_vmem, in_vmem],
        (near, arrived),
    )
    return out


def gelu_kernel(top, first, keep_ref, arrived_ref, cotangent_ref, activation_ref, slope_ref):
    rows, width = keep_ref.shape
    hidden = keep_ref[...] + arrived_ref[...].astype(jnp.float32)
    cotangent = cotangent_ref[top : top + rows, first : first + width]
    activation_ref[...], slope_ref[...] = gelu_pair(hidden, cotangent)


def gelu(core, keep, arrived, cotangent, top, first):
    out = pltpu.VMEM(keep.shape, jnp.bfloat16)
    return core(
        functools.partial(gelu_kernel, top, first),
        "gelu",
        [out, out],
        [in_vmem, in_vmem],
        [in_vmem] * 3,
        (keep, arrived, cotangent),
    )


def input_kernel(first, groups, has_before, finished, given, place, near_ref, far_ref, w_ref, *refs):
    half, width = near_ref.shape
    rows = 2 * half // groups
    tall = w_ref.shape[0]
    before = refs[0] if has_before else None
    outs = refs[has_before : has_before + given]
    scratch = refs[has_before + given :]
    turned = scratch[0]
    total = scratch[1] if finished else outs[0]
    wide = 128 * group_of(width // 128, 4)
    for at in range(0, width, wide):
        here = slice(at, at + wide)
        grad = jnp.concatenate([near_ref[:, here], far_ref[:, here]], axis=0)
        turned[here, :] = grad.T
    high = 128 * group_of(tall // 128, 4)
    for at in range(0, tall, high):
        here = slice(at, at + high)
        product = jnp.dot(
            w_ref[here, first : first + width], turned[...], preferred_element_type=jnp.float32
        )
        total[here, :] = product + before[here, :] if has_before else product
    if finished:
        upright = scratch[2]
        upright[...] = total[...].T
        each = groups // given
        for i in range(groups):
            start = pl.multiple_of(place[i] * rows, rows)
            out_ref = outs[i // each]
            at = i % each * rows
            out_ref[at : at + rows, :] = upright[pl.ds(start, rows), :].astype(out_ref.dtype)


def input_partial(core, near, far, weight, first, place, before, pieces):
    half, width = near.shape
    tall = weight.shape[0]
    both = 2 * half
    if pieces:
        outs = [pltpu.VMEM((both // pieces, tall), jnp.float32)]
        outs += [pltpu.VMEM((both // pieces, tall), jnp.bfloat16)] * (pieces - 1)
    else:
        outs = [pltpu.VMEM((tall, both), jnp.float32)]
    has_before = before is not None
    scratch = [pltpu.VMEM((width, both), near.dtype)]
    if pieces:
        scratch += [pltpu.VMEM((tall, both), jnp.float32), pltpu.VMEM((both, tall), jnp.float32)]
    return core(
        functools.partial(
            input_kernel, first, place.shape[0], has_before, pieces > 0, len(outs)
        ),
        "input_partial",
        outs,
        [in_vmem] * len(outs),
        [in_smem] + [in_vmem] * (4 if has_before else 3),
        (place, near, far, weight) + ((before,) if has_before else ()),
        scratch=scratch,
    )


def weight_kernel(row_blocks, col_blocks, first, parts, has_before, code, *refs):
    turned = refs[:parts]
    grads = refs[parts : 3 * parts]
    out_ref, made, sem = refs[3 * parts + has_before :]
    blk = made.shape[-1]
    width = grads[0].shape[1]
    here = width // blk
    per_step = group_of(here, 2)
    wide = per_step * blk
    for j in range(here // per_step):
        features = jnp.concatenate([t[...] for t in turned], axis=1)
        grad = jnp.concatenate([g[:, j * wide : (j + 1) * wide] for g in grads], axis=0)
        product = jnp.dot(features, grad, preferred_element_type=jnp.float32)
        for r in range(row_blocks):
            for c in range(per_step):
                entry = code[r * col_blocks + first // blk + j * per_step + c]
                live = lax.rem(entry, 2).astype(jnp.float32)
                at = (j * row_blocks + r) * per_step + c
                block = product[r * blk : (r + 1) * blk, c * blk : (c + 1) * blk] * live
                made[at] = block.astype(made.dtype)
                pltpu.make_async_copy(
                    made.at[at], out_ref.at[0, 0, lax.div(entry, 2)], sem
                ).start(priority=at % 2)
    pltpu.make_async_copy(made, out_ref.at[0, 0, pl.ds(0, made.shape[0])], sem).wait()


def weight_gradient(core, turned, grads, code, first, row_blocks, col_blocks, blk, before):
    parts = len(turned)
    has_before = before is not None
    here = row_blocks * grads[0].shape[1] // blk
    arrays = [*turned, *grads]
    [out] = core(
        functools.partial(weight_kernel, row_blocks, col_blocks, first, parts, has_before),
        "weight_gradient",
        [jax.ShapeDtypeStruct((1, 1, row_blocks * col_blocks, blk, blk), jnp.bfloat16)],
        [anywhere],
        [in_smem] + [in_vmem] * len(arrays) + [anywhere] * has_before,
        (code, *arrays) + ((before,) if has_before else ()),
        scratch=[pltpu.VMEM((here, blk, blk), jnp.bfloat16), pltpu.SemaphoreType.DMA],
        aliases={1 + len(arrays): 0} if has_before else None,
    )
    return out


def place_kernel(spots, *refs):
    blocks = refs[: len(spots)]
    out_ref, sems = refs[len(spots) :]
    copies = []
    for at, (top, first) in enumerate(spots):
        rows, width = blocks[at].shape
        target = out_ref.at[pl.ds(top, rows), pl.ds(first, width)]
        copies.append(pltpu.make_async_copy(blocks[at], target, sems.at[at]))
        copies[-1].start()
    for copy in copies:
        copy.wait()


def place_activation(core, blocks, spots, shape):
    [out] = core(
        functools.partial(place_kernel, spots),
        "place_activation",
        [jax.ShapeDtypeStruct(shape, jnp.bfloat16)],
        [anywhere],
        [in_vmem] * len(blocks),
        blocks,
        scratch=[pltpu.SemaphoreType.DMA((len(blocks),))],
    )
    return out


def total_kernel(each, many, starts, sizes, *refs):
    out_ref = refs[-1]
    own = sum(sizes)
    for k, (start, rows) in enumerate(zip(starts, sizes)):
        found = refs[k * many : (k + 1) * many]
        for j in range(each):
            here = slice(j * rows, (j + 1) * rows)
            total = found[0][here, :]
            for piece in found[1:]:
                total = total + piece[here, :].astype(jnp.float32)
            top = j * own + start
            out_ref[top : top + rows, :] = total.astype(jnp.bfloat16)


def total_input(core, found, each, starts, sizes):
    arrays = [x for part in found for x in part]
    shape = (each * sum(sizes), arrays[0].shape[1])
    [out] = core(
        functools.partial(total_kernel, each, len(found[0]), starts, sizes),
        "total_input",
        [jax.ShapeDtypeStruct(shape, jnp.bfloat16)],
        [pl.BlockSpec(shape, lambda: (0, 0))],
        [in_vmem] * len(arrays),
        arrays,
    )
    return out


def swap(array, axis, size, bit):
    return lax.ppermute(array, axis, [(i, i ^ bit) for i in range(size)])


def on_device(tokens, w_packed, kept_rows, kept_cols, kept_count, grad_act):
    blk = w_packed.shape[-1]
    slot_count = w_packed.shape[2]
    tall = tokens.shape[1]
    row_tokens, hidden_here = grad_act.shape
    row_blocks = tall // blk
    col_blocks = hidden_here // blk
    n_row = lax.axis_size("row")
    n_col = lax.axis_size("col")
    row_me = lax.axis_index("row")
    col_me = lax.axis_index("col")
    col_groups = tokens.shape[0] // row_tokens
    tiles = row_tokens // 16
    shares = token_split if tiles % sum(token_split) == 0 else (1,)
    sizes = [16 * (tiles // sum(shares)) * share for share in shares]
    starts = [sum(sizes[:k]) for k in range(len(sizes))]
    parts = len(sizes)
    slabs = group_of(col_blocks, column_parts)
    width = hidden_here // slabs
    direct = n_col <= 8
    core = Core()

    places = kept_rows[0, 0] * col_blocks + kept_cols[0, 0]
    slots = jnp.arange(slot_count, dtype=jnp.int32)
    coded = slots * 2 + (slots < kept_count[0, 0]).astype(jnp.int32)
    code = jnp.sum(jnp.where(places[None, :] == slots[:, None], coded[None, :], 0), axis=1)

    apart = row_me ^ (col_me * col_groups) if direct else row_me
    everyone = np.arange(n_row)
    order = np.concatenate([everyone[::2], everyone[1::2]]).astype(np.int32)
    pick = (jnp.asarray(order) ^ apart).astype(jnp.int32)
    distance = jnp.asarray(everyone.astype(np.int32)) ^ apart
    place = ((distance & 1) * (n_row // 2) + (distance >> 1)).astype(jnp.int32)

    pieces = []
    for start, rows in zip(starts, sizes):
        mine = tokens.reshape(col_groups, row_tokens, tall)[:, start : start + rows]
        if direct:
            pieces.append([mine] + [swap(mine, "col", n_col, m) for m in range(1, n_col)])
        else:
            pieces.append([lax.all_gather(mine, "col", axis=0, tiled=True)])
    weight = dense_tile(core, w_packed, code, row_blocks, col_blocks, [pick, place])

    far_bits = [1 << b for b in range(1, n_row.bit_length() - 1)]
    units = [(k, c) for k in range(parts) for c in range(slabs)]
    paths = [far_bits if at % 2 == 0 else far_bits[::-1] for at in range(len(units))]
    state = {}
    full, turned = {}, {}
    activations, sums, input_grads = {}, {}, {}

    def begin(k, c, path):
        if c == 0:
            full[k], turned[k] = arrange(core, pieces[k], pick)
        keep, send = forward(core, full[k], weight, c * width, width)
        state[k, c] = (keep, swap(send, "row", n_row, 1))

    def add(at, k, c, path):
        left = sorted(path[at:], reverse=True)
        keep, send = add_step(core, *state[k, c], left, path[at])
        state[k, c] = (keep, swap(send, "row", n_row, path[at]))

    def bend(k, c, path):
        activations[k, c], near = gelu(core, *state[k, c], grad_act, starts[k], c * width)
        state[k, c] = (near, swap(near, "row", n_row, ([1] + path)[-1]))

    def join(at, k, c, path):
        held = sorted(path[at:], reverse=True)
        near = join_step(core, *state[k, c], held, path[at])
        state[k, c] = (near, swap(near, "row", n_row, ([1] + path)[at]))

    def finish(k, c, path):
        last = c + 1 == slabs
        cut = (n_col if direct else 1) * last
        found = input_partial(
            core, *state[k, c], weight, c * width, place, sums.get((k, c - 1)), cut
        )
        sums[k, c] = found[0]
        if last and direct:
            input_grads[k] = [found[0]]
            input_grads[k] += [swap(found[m], "col", n_col, m) for m in range(1, n_col)]
        elif last:
            total = found[0].reshape(n_col, col_groups * sizes[k], tall)
            total = lax.psum_scatter(total, "col", scatter_dimension=0, tiled=True)[0]
            input_grads[k] = [total]

    hops = len(far_bits)
    stages = [begin] + [functools.partial(add, at) for at in range(hops)] + [bend]
    stages += [functools.partial(join, at) for at in reversed(range(hops))] + [finish]
    plan = [(k, at) for at in range(len(stages)) for k in range(parts)]
    if parts == 2 and hops == 2:
        plan = [(0, 0), (0, 1), (0, 2), (1, 0), (1, 1), (0, 3), (0, 4), (1, 2), (0, 5), (1, 3), (1, 4), (0, 6), (1, 5), (1, 6)]
    for k, at in plan:
        for c in range(slabs):
            stages[at](k, c, paths[units.index((k, c))])
        if (k, at) == (parts - 1, len(stages) - 3):
            activation = place_activation(
                core,
                [activations[k, c] for k, c in units],
                [(starts[k], c * width) for k, c in units],
                grad_act.shape,
            )
    weight_grad = None
    for c in range(slabs):
        weight_grad = weight_gradient(
            core,
            [turned[k] for k in range(parts)],
            [g for k in range(parts) for g in state[k, c]],
            code,
            c * width,
            row_blocks,
            col_blocks,
            blk,
            weight_grad,
        )
    input_grad = total_input(
        core, [input_grads[k] for k in range(parts)], col_groups, starts, sizes
    )
    return (activation, input_grad, weight_grad)


def solution(mesh):
    placed = (
        P("col", "row"),
        P("row", "col", None, None, None),
        P("row", "col", None),
        P("row", "col", None),
        P("row", "col"),
        P("row", "col"),
    )
    return jax.shard_map(
        on_device,
        mesh=mesh,
        in_specs=placed,
        out_specs=(P("row", "col"), P("col", "row"), P("row", "col", None, None, None)),
        check_vma=False,
    )
```

```python
import functools

import jax
import jax.numpy as jnp
import numpy as np
from jax import lax
from jax.experimental import pallas as pl
from jax.experimental.pallas import tpu as pltpu
from jax.sharding import PartitionSpec as P

gelu_scale = 0.7978845608
gelu_cubic = 0.044715
token_split = (1, 1)
column_parts = 2
vmem_limit = 16 * 1024 * 1024
in_vmem = pl.BlockSpec(memory_space=pltpu.VMEM)
in_smem = pl.BlockSpec(memory_space=pltpu.SMEM)
anywhere = pl.BlockSpec(memory_space=pltpu.HBM)


def gelu_pair(hidden, cotangent):
    inner = gelu_scale * (hidden + gelu_cubic * hidden * hidden * hidden)
    tangent = jnp.tanh(inner)
    activation = (0.5 * hidden * (1.0 + tangent)).astype(jnp.bfloat16)
    slope = 0.5 * (1.0 + tangent) + 0.5 * hidden * (1.0 - tangent * tangent) * gelu_scale * (
        1.0 + 3.0 * gelu_cubic * hidden * hidden
    )
    slope_grad = (cotangent.astype(jnp.float32) * slope).astype(jnp.bfloat16)
    return (activation, slope_grad)


def group_of(blocks, goal):
    return max(n for n in range(1, goal + 1) if blocks % n == 0)


class Core:
    def __init__(self):
        self.turn = None

    def __call__(self, kernel, name, out_shape, out_specs, in_specs, operands, scratch=(), aliases=None):
        homes = {id(in_vmem): pltpu.VMEM, id(anywhere): pltpu.HBM}
        in_specs, operands = list(in_specs), list(operands)
        if self.turn is not None:
            in_specs.append(in_vmem)
            operands.append(self.turn)
        taken = len(operands)
        given = len(out_shape)
        extra = self.turn is not None

        def body(*refs):
            refs[taken + given][...] = jnp.zeros((8, 128), jnp.float32)
            kernel(*refs[: taken - extra], *refs[taken : taken + given], *refs[taken + given + 1 :])

        placed = [
            pltpu.with_memory_space_constraint(x, homes[id(spec)]) if id(spec) in homes else x
            for x, spec in zip(operands, in_specs)
        ]
        *out, self.turn = pl.pallas_call(
            body,
            out_shape=[*out_shape, pltpu.VMEM((8, 128), jnp.float32)],
            in_specs=in_specs,
            out_specs=[*out_specs, in_vmem],
            scratch_shapes=list(scratch),
            input_output_aliases=aliases or {},
            compiler_params=pltpu.CompilerParams(vmem_limit_bytes=vmem_limit),
            cost_estimate=pl.CostEstimate(flops=1, transcendentals=0, bytes_accessed=1),
            name=name,
        )(*placed)
        return out


def dense_kernel(row_blocks, col_blocks, code, w_ref, *refs):
    out_ref, empty, sem = refs[-3:]
    blk = w_ref.shape[-1]
    empty[...] = jnp.zeros_like(empty)

    def load(at, carry):
        for r in range(row_blocks):
            entry = code[r * col_blocks + at]
            start = pl.multiple_of(at * blk, blk)
            target = out_ref.at[pl.ds(r * blk, blk), pl.ds(start, blk)]

            @pl.when(lax.rem(entry, 2) == 1)
            def _():
                pltpu.make_async_copy(w_ref.at[0, 0, lax.div(entry, 2)], target, sem).start()

            @pl.when(lax.rem(entry, 2) == 0)
            def _():
                pltpu.make_async_copy(empty, target, sem).start()

        return carry

    lax.fori_loop(0, col_blocks, load, 0)
    pltpu.make_async_copy(out_ref, out_ref, sem).wait()


def dense_tile(core, w_packed, code, row_blocks, col_blocks, ready):
    blk = w_packed.shape[-1]
    [weight] = core(
        functools.partial(dense_kernel, row_blocks, col_blocks),
        "dense_tile",
        [pltpu.VMEM((row_blocks * blk, col_blocks * blk), w_packed.dtype)],
        [in_vmem],
        [in_smem, anywhere] + [in_smem] * len(ready),
        (code, w_packed, *ready),
        scratch=[pltpu.VMEM((blk, blk), w_packed.dtype), pltpu.SemaphoreType.DMA],
    )
    return weight


def arrange_kernel(groups, rows, pieces, pick, *refs):
    out_ref, turned_ref, all_ref = refs[pieces:]
    each = groups // pieces
    for m in range(pieces):
        for j in range(each):
            all_ref[m * each + j] = refs[m][j]
    for t in range(groups):
        out_ref[pl.ds(t * rows, rows), :] = all_ref[pick[t]]
    turned_ref[...] = out_ref[...].T


def arrange(core, pieces, pick):
    groups = pick.shape[0]
    rows, tall = pieces[0].shape[1:]
    kind = pieces[0].dtype
    return core(
        functools.partial(arrange_kernel, groups, rows, len(pieces)),
        "arrange",
        [pltpu.VMEM((groups * rows, tall), kind), pltpu.VMEM((tall, groups * rows), kind)],
        [in_vmem, in_vmem],
        [in_smem] + [in_vmem] * len(pieces),
        (pick, *pieces),
        scratch=[pltpu.VMEM((groups, rows, tall), kind)],
    )


def forward_kernel(first, wide, x_ref, w_ref, keep_ref, send_ref):
    half, width = keep_ref.shape
    for at in range(0, width, wide):
        product = jnp.dot(
            x_ref[...], w_ref[:, first + at : first + at + wide], preferred_element_type=jnp.float32
        )
        keep_ref[:, at : at + wide] = product[:half]
        send_ref[:, at : at + wide] = product[half:].astype(jnp.bfloat16)


def forward(core, features, weight, first, width):
    half = features.shape[0] // 2
    wide = 128 * group_of(width // 128, 4)
    return core(
        functools.partial(forward_kernel, first, wide),
        "forward",
        [pltpu.VMEM((half, width), jnp.float32), pltpu.VMEM((half, width), jnp.bfloat16)],
        [in_vmem, in_vmem],
        [in_vmem, in_vmem],
        (features, weight),
    )


def sides(left, bit):
    at = len(left) - 1 - left.index(bit)
    names = range(1 << len(left))
    return [g for g in names if not g >> at & 1], [g for g in names if g >> at & 1]


def add_kernel(rows, stay, leave, keep_ref, arrived_ref, next_ref, send_ref):
    for out_ref, groups in ((next_ref, stay), (send_ref, leave)):
        for at, g in enumerate(groups):
            here = slice(g * rows, (g + 1) * rows)
            total = keep_ref[here, :] + arrived_ref[here, :].astype(jnp.float32)
            out_ref[at * rows : (at + 1) * rows, :] = total.astype(out_ref.dtype)


def add_step(core, keep, arrived, left, bit):
    rows = keep.shape[0] >> len(left)
    half = (keep.shape[0] // 2, keep.shape[1])
    return core(
        functools.partial(add_kernel, rows, *sides(left, bit)),
        "add_step",
        [pltpu.VMEM(half, jnp.float32), pltpu.VMEM(half, jnp.bfloat16)],
        [in_vmem, in_vmem],
        [in_vmem, in_vmem],
        (keep, arrived),
    )


def join_kernel(rows, stay, come, near_ref, arrived_ref, out_ref):
    for in_ref, groups in ((near_ref, stay), (arrived_ref, come)):
        for at, g in enumerate(groups):
            out_ref[g * rows : (g + 1) * rows, :] = in_ref[at * rows : (at + 1) * rows, :]


def join_step(core, near, arrived, held, bit):
    rows = 2 * near.shape[0] >> len(held)
    [out] = core(
        functools.partial(join_kernel, rows, *sides(held, bit)),
        "join_step",
        [pltpu.VMEM((2 * near.shape[0], near.shape[1]), near.dtype)],
        [in_vmem],
        [in_vmem, in_vmem],
        (near, arrived),
    )
    return out


def gelu_kernel(top, first, keep_ref, arrived_ref, cotangent_ref, activation_ref, slope_ref):
    rows, width = keep_ref.shape
    hidden = keep_ref[...] + arrived_ref[...].astype(jnp.float32)
    cotangent = cotangent_ref[top : top + rows, first : first + width]
    activation_ref[...], slope_ref[...] = gelu_pair(hidden, cotangent)


def gelu(core, keep, arrived, cotangent, top, first):
    out = pltpu.VMEM(keep.shape, jnp.bfloat16)
    return core(
        functools.partial(gelu_kernel, top, first),
        "gelu",
        [out, out],
        [in_vmem, in_vmem],
        [in_vmem] * 3,
        (keep, arrived, cotangent),
    )


def input_kernel(first, groups, has_before, finished, given, place, near_ref, far_ref, w_ref, *refs):
    half, width = near_ref.shape
    rows = 2 * half // groups
    tall = w_ref.shape[0]
    before = refs[0] if has_before else None
    outs = refs[has_before : has_before + given]
    scratch = refs[has_before + given :]
    turned = scratch[0]
    total = scratch[1] if finished else outs[0]
    wide = 128 * group_of(width // 128, 4)
    for at in range(0, width, wide):
        here = slice(at, at + wide)
        grad = jnp.concatenate([near_ref[:, here], far_ref[:, here]], axis=0)
        turned[here, :] = grad.T
    high = 128 * group_of(tall // 128, 2)
    for at in range(0, tall, high):
        here = slice(at, at + high)
        product = jnp.dot(
            w_ref[here, first : first + width], turned[...], preferred_element_type=jnp.float32
        )
        total[here, :] = product + before[here, :] if has_before else product
    if finished:
        upright = scratch[2]
        upright[...] = total[...].T
        each = groups // given
        for i in range(groups):
            start = pl.multiple_of(place[i] * rows, rows)
            out_ref = outs[i // each]
            at = i % each * rows
            out_ref[at : at + rows, :] = upright[pl.ds(start, rows), :].astype(out_ref.dtype)


def input_partial(core, near, far, weight, first, place, before, pieces):
    half, width = near.shape
    tall = weight.shape[0]
    both = 2 * half
    if pieces:
        outs = [pltpu.VMEM((both // pieces, tall), jnp.float32)]
        outs += [pltpu.VMEM((both // pieces, tall), jnp.bfloat16)] * (pieces - 1)
    else:
        outs = [pltpu.VMEM((tall, both), jnp.float32)]
    has_before = before is not None
    scratch = [pltpu.VMEM((width, both), near.dtype)]
    if pieces:
        scratch += [pltpu.VMEM((tall, both), jnp.float32), pltpu.VMEM((both, tall), jnp.float32)]
    return core(
        functools.partial(
            input_kernel, first, place.shape[0], has_before, pieces > 0, len(outs)
        ),
        "input_partial",
        outs,
        [in_vmem] * len(outs),
        [in_smem] + [in_vmem] * (4 if has_before else 3),
        (place, near, far, weight) + ((before,) if has_before else ()),
        scratch=scratch,
    )


def weight_kernel(row_blocks, col_blocks, first, parts, has_before, code, *refs):
    turned = refs[:parts]
    grads = refs[parts : 3 * parts]
    out_ref, made, sem = refs[3 * parts + has_before :]
    blk = made.shape[-1]
    width = grads[0].shape[1]
    here = width // blk
    per_step = group_of(here, 4)
    wide = per_step * blk
    high = group_of(row_blocks, 2)
    for j in range(here // per_step):
        grad = jnp.concatenate([g[:, j * wide : (j + 1) * wide] for g in grads], axis=0)
        for r in range(0, row_blocks, high):
            rows = slice(r * blk, (r + high) * blk)
            features = jnp.concatenate([t[rows, :] for t in turned], axis=1)
            product = jnp.dot(features, grad, preferred_element_type=jnp.float32)
            for i in range(high):
                for c in range(per_step):
                    entry = code[(r + i) * col_blocks + first // blk + j * per_step + c]
                    live = lax.rem(entry, 2).astype(jnp.float32)
                    at = (j * row_blocks + r + i) * per_step + c
                    block = product[i * blk : (i + 1) * blk, c * blk : (c + 1) * blk] * live
                    made[at] = block.astype(made.dtype)
                    pltpu.make_async_copy(
                        made.at[at], out_ref.at[0, 0, lax.div(entry, 2)], sem
                    ).start(priority=at % 2)
    pltpu.make_async_copy(made, out_ref.at[0, 0, pl.ds(0, made.shape[0])], sem).wait()


def weight_gradient(core, turned, grads, code, first, row_blocks, col_blocks, blk, before):
    parts = len(turned)
    has_before = before is not None
    here = row_blocks * grads[0].shape[1] // blk
    arrays = [*turned, *grads]
    [out] = core(
        functools.partial(weight_kernel, row_blocks, col_blocks, first, parts, has_before),
        "weight_gradient",
        [jax.ShapeDtypeStruct((1, 1, row_blocks * col_blocks, blk, blk), jnp.bfloat16)],
        [anywhere],
        [in_smem] + [in_vmem] * len(arrays) + [anywhere] * has_before,
        (code, *arrays) + ((before,) if has_before else ()),
        scratch=[pltpu.VMEM((here, blk, blk), jnp.bfloat16), pltpu.SemaphoreType.DMA],
        aliases={1 + len(arrays): 0} if has_before else None,
    )
    return out


def place_kernel(spots, *refs):
    blocks = refs[: len(spots)]
    out_ref, sems = refs[len(spots) :]
    copies = []
    for at, (top, first) in enumerate(spots):
        rows, width = blocks[at].shape
        target = out_ref.at[pl.ds(top, rows), pl.ds(first, width)]
        copies.append(pltpu.make_async_copy(blocks[at], target, sems.at[at]))
        copies[-1].start()
    for copy in copies:
        copy.wait()


def place_activation(core, blocks, spots, shape):
    [out] = core(
        functools.partial(place_kernel, spots),
        "place_activation",
        [jax.ShapeDtypeStruct(shape, jnp.bfloat16)],
        [anywhere],
        [in_vmem] * len(blocks),
        blocks,
        scratch=[pltpu.SemaphoreType.DMA((len(blocks),))],
    )
    return out


def total_kernel(each, many, starts, sizes, *refs):
    out_ref = refs[-1]
    own = sum(sizes)
    for k, (start, rows) in enumerate(zip(starts, sizes)):
        found = refs[k * many : (k + 1) * many]
        for j in range(each):
            here = slice(j * rows, (j + 1) * rows)
            total = found[0][here, :]
            for piece in found[1:]:
                total = total + piece[here, :].astype(jnp.float32)
            top = j * own + start
            out_ref[top : top + rows, :] = total.astype(jnp.bfloat16)


def total_input(core, found, each, starts, sizes):
    arrays = [x for part in found for x in part]
    shape = (each * sum(sizes), arrays[0].shape[1])
    [out] = core(
        functools.partial(total_kernel, each, len(found[0]), starts, sizes),
        "total_input",
        [jax.ShapeDtypeStruct(shape, jnp.bfloat16)],
        [pl.BlockSpec(shape, lambda: (0, 0))],
        [in_vmem] * len(arrays),
        arrays,
    )
    return out


def swap(array, axis, size, bit):
    return lax.ppermute(array, axis, [(i, i ^ bit) for i in range(size)])


def on_device(tokens, w_packed, kept_rows, kept_cols, kept_count, grad_act):
    blk = w_packed.shape[-1]
    slot_count = w_packed.shape[2]
    tall = tokens.shape[1]
    row_tokens, hidden_here = grad_act.shape
    row_blocks = tall // blk
    col_blocks = hidden_here // blk
    n_row = lax.axis_size("row")
    n_col = lax.axis_size("col")
    row_me = lax.axis_index("row")
    col_me = lax.axis_index("col")
    col_groups = tokens.shape[0] // row_tokens
    tiles = row_tokens // 16
    shares = token_split if tiles % sum(token_split) == 0 else (1,)
    sizes = [16 * (tiles // sum(shares)) * share for share in shares]
    starts = [sum(sizes[:k]) for k in range(len(sizes))]
    parts = len(sizes)
    slabs = group_of(col_blocks, column_parts)
    width = hidden_here // slabs
    direct = n_col <= 8
    core = Core()

    places = kept_rows[0, 0] * col_blocks + kept_cols[0, 0]
    slots = jnp.arange(slot_count, dtype=jnp.int32)
    coded = slots * 2 + (slots < kept_count[0, 0]).astype(jnp.int32)
    code = jnp.sum(jnp.where(places[None, :] == slots[:, None], coded[None, :], 0), axis=1)

    apart = row_me ^ (col_me * col_groups) if direct else row_me
    everyone = np.arange(n_row)
    order = np.concatenate([everyone[::2], everyone[1::2]]).astype(np.int32)
    pick = (jnp.asarray(order) ^ apart).astype(jnp.int32)
    distance = jnp.asarray(everyone.astype(np.int32)) ^ apart
    place = ((distance & 1) * (n_row // 2) + (distance >> 1)).astype(jnp.int32)

    pieces = []
    for start, rows in zip(starts, sizes):
        mine = tokens.reshape(col_groups, row_tokens, tall)[:, start : start + rows]
        if direct:
            pieces.append([mine] + [swap(mine, "col", n_col, m) for m in range(1, n_col)])
        else:
            pieces.append([lax.all_gather(mine, "col", axis=0, tiled=True)])
    weight = dense_tile(core, w_packed, code, row_blocks, col_blocks, [pick, place])

    far_bits = [1 << b for b in range(1, n_row.bit_length() - 1)]
    units = [(k, c) for k in range(parts) for c in range(slabs)]
    paths = [far_bits if at % 2 == 0 else far_bits[::-1] for at in range(len(units))]
    state = {}
    full, turned = {}, {}
    activations, sums, input_grads = {}, {}, {}

    def begin(k, c, path):
        if c == 0:
            full[k], turned[k] = arrange(core, pieces[k], pick)
        keep, send = forward(core, full[k], weight, c * width, width)
        state[k, c] = (keep, swap(send, "row", n_row, 1))

    def add(at, k, c, path):
        left = sorted(path[at:], reverse=True)
        keep, send = add_step(core, *state[k, c], left, path[at])
        state[k, c] = (keep, swap(send, "row", n_row, path[at]))

    def bend(k, c, path):
        activations[k, c], near = gelu(core, *state[k, c], grad_act, starts[k], c * width)
        state[k, c] = (near, swap(near, "row", n_row, ([1] + path)[-1]))

    def join(at, k, c, path):
        held = sorted(path[at:], reverse=True)
        near = join_step(core, *state[k, c], held, path[at])
        state[k, c] = (near, swap(near, "row", n_row, ([1] + path)[at]))

    def finish(k, c, path):
        last = c + 1 == slabs
        cut = (n_col if direct else 1) * last
        found = input_partial(
            core, *state[k, c], weight, c * width, place, sums.get((k, c - 1)), cut
        )
        sums[k, c] = found[0]
        if last and direct:
            input_grads[k] = [found[0]]
            input_grads[k] += [swap(found[m], "col", n_col, m) for m in range(1, n_col)]
        elif last:
            total = found[0].reshape(n_col, col_groups * sizes[k], tall)
            total = lax.psum_scatter(total, "col", scatter_dimension=0, tiled=True)[0]
            input_grads[k] = [total]

    hops = len(far_bits)
    stages = [begin] + [functools.partial(add, at) for at in range(hops)] + [bend]
    stages += [functools.partial(join, at) for at in reversed(range(hops))] + [finish]
    plan = [(k, at) for at in range(len(stages)) for k in range(parts)]
    if parts == 2 and hops == 2:
        plan = [(0, 0), (0, 1), (0, 2), (1, 0), (1, 1), (0, 3), (0, 4), (1, 2), (0, 5), (1, 3), (1, 4), (0, 6), (1, 5), (1, 6)]
    for k, at in plan:
        for c in range(slabs):
            stages[at](k, c, paths[units.index((k, c))])
        if (k, at) == (parts - 1, len(stages) - 3):
            activation = place_activation(
                core,
                [activations[k, c] for k, c in units],
                [(starts[k], c * width) for k, c in units],
                grad_act.shape,
            )
    weight_grad = None
    for c in range(slabs):
        weight_grad = weight_gradient(
            core,
            [turned[k] for k in range(parts)],
            [g for k in range(parts) for g in state[k, c]],
            code,
            c * width,
            row_blocks,
            col_blocks,
            blk,
            weight_grad,
        )
    input_grad = total_input(
        core, [input_grads[k] for k in range(parts)], col_groups, starts, sizes
    )
    return (activation, input_grad, weight_grad)


def solution(mesh):
    placed = (
        P("col", "row"),
        P("row", "col", None, None, None),
        P("row", "col", None),
        P("row", "col", None),
        P("row", "col"),
        P("row", "col"),
    )
    return jax.shard_map(
        on_device,
        mesh=mesh,
        in_specs=placed,
        out_specs=(P("row", "col"), P("col", "row"), P("row", "col", None, None, None)),
        check_vma=False,
    )
```

```python
import functools

import jax
import jax.numpy as jnp
import numpy as np
from jax import lax
from jax.experimental import pallas as pl
from jax.experimental.pallas import tpu as pltpu
from jax.sharding import PartitionSpec as P

gelu_scale = 0.7978845608
gelu_cubic = 0.044715
token_split = (1, 1)
column_parts = 2
vmem_limit = 16 * 1024 * 1024
in_vmem = pl.BlockSpec(memory_space=pltpu.VMEM)
in_smem = pl.BlockSpec(memory_space=pltpu.SMEM)
anywhere = pl.BlockSpec(memory_space=pltpu.HBM)


def gelu_pair(hidden, cotangent):
    inner = gelu_scale * (hidden + gelu_cubic * hidden * hidden * hidden)
    tangent = jnp.tanh(inner)
    activation = (0.5 * hidden * (1.0 + tangent)).astype(jnp.bfloat16)
    slope = 0.5 * (1.0 + tangent) + 0.5 * hidden * (1.0 - tangent * tangent) * gelu_scale * (
        1.0 + 3.0 * gelu_cubic * hidden * hidden
    )
    slope_grad = (cotangent.astype(jnp.float32) * slope).astype(jnp.bfloat16)
    return (activation, slope_grad)


def group_of(blocks, goal):
    return max(n for n in range(1, goal + 1) if blocks % n == 0)


class Core:
    def __init__(self):
        self.turn = None

    def __call__(self, kernel, name, out_shape, out_specs, in_specs, operands, scratch=(), limit=vmem_limit):
        homes = {id(in_vmem): pltpu.VMEM, id(anywhere): pltpu.HBM}
        in_specs, operands = list(in_specs), list(operands)
        if self.turn is not None:
            in_specs.append(in_vmem)
            operands.append(self.turn)
        taken = len(operands)
        given = len(out_shape)
        extra = self.turn is not None

        def body(*refs):
            refs[taken + given][...] = jnp.zeros((8, 128), jnp.float32)
            kernel(*refs[: taken - extra], *refs[taken : taken + given], *refs[taken + given + 1 :])

        placed = [
            pltpu.with_memory_space_constraint(x, homes[id(spec)]) if id(spec) in homes else x
            for x, spec in zip(operands, in_specs)
        ]
        *out, self.turn = pl.pallas_call(
            body,
            out_shape=[*out_shape, pltpu.VMEM((8, 128), jnp.float32)],
            in_specs=in_specs,
            out_specs=[*out_specs, in_vmem],
            scratch_shapes=list(scratch),
            compiler_params=pltpu.CompilerParams(vmem_limit_bytes=limit),
            cost_estimate=pl.CostEstimate(flops=1, transcendentals=0, bytes_accessed=1),
            name=name,
        )(*placed)
        return out


def dense_kernel(row_blocks, col_blocks, code, w_ref, *refs):
    out_ref, empty, sem = refs[-3:]
    blk = w_ref.shape[-1]
    empty[...] = jnp.zeros_like(empty)

    def load(at, carry):
        for r in range(row_blocks):
            entry = code[r * col_blocks + at]
            start = pl.multiple_of(at * blk, blk)
            target = out_ref.at[pl.ds(r * blk, blk), pl.ds(start, blk)]

            @pl.when(lax.rem(entry, 2) == 1)
            def _():
                pltpu.make_async_copy(w_ref.at[0, 0, lax.div(entry, 2)], target, sem).start()

            @pl.when(lax.rem(entry, 2) == 0)
            def _():
                pltpu.make_async_copy(empty, target, sem).start()

        return carry

    lax.fori_loop(0, col_blocks, load, 0)
    pltpu.make_async_copy(out_ref, out_ref, sem).wait()


def dense_tile(core, w_packed, code, row_blocks, col_blocks, ready):
    blk = w_packed.shape[-1]
    [weight] = core(
        functools.partial(dense_kernel, row_blocks, col_blocks),
        "dense_tile",
        [pltpu.VMEM((row_blocks * blk, col_blocks * blk), w_packed.dtype)],
        [in_vmem],
        [in_smem, anywhere] + [in_smem] * len(ready),
        (code, w_packed, *ready),
        scratch=[pltpu.VMEM((blk, blk), w_packed.dtype), pltpu.SemaphoreType.DMA],
    )
    return weight


def arrange_kernel(groups, rows, pieces, pick, *refs):
    out_ref, turned_ref, all_ref = refs[pieces:]
    each = groups // pieces
    for m in range(pieces):
        for j in range(each):
            all_ref[m * each + j] = refs[m][j]
    for t in range(groups):
        out_ref[pl.ds(t * rows, rows), :] = all_ref[pick[t]]
    turned_ref[...] = out_ref[...].T


def arrange(core, pieces, pick):
    groups = pick.shape[0]
    rows, tall = pieces[0].shape[1:]
    kind = pieces[0].dtype
    return core(
        functools.partial(arrange_kernel, groups, rows, len(pieces)),
        "arrange",
        [pltpu.VMEM((groups * rows, tall), kind), pltpu.VMEM((tall, groups * rows), kind)],
        [in_vmem, in_vmem],
        [in_smem] + [in_vmem] * len(pieces),
        (pick, *pieces),
        scratch=[pltpu.VMEM((groups, rows, tall), kind)],
    )


def forward_kernel(first, wide, x_ref, w_ref, keep_ref, send_ref):
    half, width = keep_ref.shape
    for at in range(0, width, wide):
        product = jnp.dot(
            x_ref[...], w_ref[:, first + at : first + at + wide], preferred_element_type=jnp.float32
        )
        keep_ref[:, at : at + wide] = product[:half]
        send_ref[:, at : at + wide] = product[half:].astype(jnp.bfloat16)


def forward(core, features, weight, first, width):
    half = features.shape[0] // 2
    wide = 128 * group_of(width // 128, 4)
    return core(
        functools.partial(forward_kernel, first, wide),
        "forward",
        [pltpu.VMEM((half, width), jnp.float32), pltpu.VMEM((half, width), jnp.bfloat16)],
        [in_vmem, in_vmem],
        [in_vmem, in_vmem],
        (features, weight),
    )


def sides(left, bit):
    at = len(left) - 1 - left.index(bit)
    names = range(1 << len(left))
    return [g for g in names if not g >> at & 1], [g for g in names if g >> at & 1]


def add_kernel(rows, stay, leave, keep_ref, arrived_ref, next_ref, send_ref):
    for out_ref, groups in ((next_ref, stay), (send_ref, leave)):
        for at, g in enumerate(groups):
            here = slice(g * rows, (g + 1) * rows)
            total = keep_ref[here, :] + arrived_ref[here, :].astype(jnp.float32)
            out_ref[at * rows : (at + 1) * rows, :] = total.astype(out_ref.dtype)


def add_step(core, keep, arrived, left, bit):
    rows = keep.shape[0] >> len(left)
    half = (keep.shape[0] // 2, keep.shape[1])
    return core(
        functools.partial(add_kernel, rows, *sides(left, bit)),
        "add_step",
        [pltpu.VMEM(half, jnp.float32), pltpu.VMEM(half, jnp.bfloat16)],
        [in_vmem, in_vmem],
        [in_vmem, in_vmem],
        (keep, arrived),
    )


def join_kernel(rows, stay, come, near_ref, arrived_ref, out_ref):
    for in_ref, groups in ((near_ref, stay), (arrived_ref, come)):
        for at, g in enumerate(groups):
            out_ref[g * rows : (g + 1) * rows, :] = in_ref[at * rows : (at + 1) * rows, :]


def join_step(core, near, arrived, held, bit):
    rows = 2 * near.shape[0] >> len(held)
    [out] = core(
        functools.partial(join_kernel, rows, *sides(held, bit)),
        "join_step",
        [pltpu.VMEM((2 * near.shape[0], near.shape[1]), near.dtype)],
        [in_vmem],
        [in_vmem, in_vmem],
        (near, arrived),
    )
    return out


def gelu_kernel(top, first, keep_ref, arrived_ref, cotangent_ref, activation_ref, slope_ref):
    rows, width = keep_ref.shape
    hidden = keep_ref[...] + arrived_ref[...].astype(jnp.float32)
    cotangent = cotangent_ref[top : top + rows, first : first + width]
    activation_ref[...], slope_ref[...] = gelu_pair(hidden, cotangent)


def gelu(core, keep, arrived, cotangent, top, first):
    out = pltpu.VMEM(keep.shape, jnp.bfloat16)
    return core(
        functools.partial(gelu_kernel, top, first),
        "gelu",
        [out, out],
        [in_vmem, in_vmem],
        [in_vmem] * 3,
        (keep, arrived, cotangent),
    )


def input_kernel(groups, slabs, given, place, *refs):
    grads = [refs[2 * c : 2 * c + 2] for c in range(slabs)]
    w_ref = refs[2 * slabs]
    outs = refs[2 * slabs + 1 : 2 * slabs + 1 + given]
    turned, total, upright = refs[2 * slabs + 1 + given :]
    half, width = grads[0][0].shape
    rows = 2 * half // groups
    tall = w_ref.shape[0]
    wide = 128 * group_of(width // 128, 4)
    for c in range(slabs):
        for at in range(0, width, wide):
            here = slice(at, at + wide)
            grad = jnp.concatenate([g[:, here] for g in grads[c]], axis=0)
            turned[c * width + at : c * width + at + wide, :] = grad.T
    high = 128 * group_of(tall // 128, 4)
    for at in range(0, tall, high):
        here = slice(at, at + high)
        total[here, :] = jnp.dot(w_ref[here, :], turned[...], preferred_element_type=jnp.float32)
    upright[...] = total[...].T
    each = groups // given
    for i in range(groups):
        start = pl.multiple_of(place[i] * rows, rows)
        out_ref = outs[i // each]
        at = i % each * rows
        out_ref[at : at + rows, :] = upright[pl.ds(start, rows), :].astype(out_ref.dtype)


def input_partial(core, grads, weight, place, pieces):
    slabs = len(grads)
    half, width = grads[0][0].shape
    tall = weight.shape[0]
    both = 2 * half
    outs = [pltpu.VMEM((both // pieces, tall), jnp.float32)]
    outs += [pltpu.VMEM((both // pieces, tall), jnp.bfloat16)] * (pieces - 1)
    return core(
        functools.partial(input_kernel, place.shape[0], slabs, len(outs)),
        "input_partial",
        outs,
        [in_vmem] * len(outs),
        [in_smem] + [in_vmem] * (2 * slabs + 1),
        (place, *(g for pair in grads for g in pair), weight),
        scratch=[
            pltpu.VMEM((slabs * width, both), weight.dtype),
            pltpu.VMEM((tall, both), jnp.float32),
            pltpu.VMEM((both, tall), jnp.float32),
        ],
    )


def weight_kernel(row_blocks, col_blocks, slabs, parts, code, *refs):
    turned = refs[:parts]
    grads = [refs[parts * (1 + 2 * c) : parts * (3 + 2 * c)] for c in range(slabs)]
    out_ref, made, sem = refs[parts * (1 + 2 * slabs) :]
    blk = made.shape[-1]
    here = col_blocks // slabs
    per_step = group_of(here, 4)
    wide = per_step * blk
    high = group_of(row_blocks, 2)
    for j in range(col_blocks // per_step):
        c, left = divmod(j * per_step, here)
        columns = slice(left * blk, left * blk + wide)
        grad = jnp.concatenate([g[:, columns] for g in grads[c]], axis=0)
        for r in range(0, row_blocks, high):
            rows = slice(r * blk, (r + high) * blk)
            features = jnp.concatenate([t[rows, :] for t in turned], axis=1)
            product = jnp.dot(features, grad, preferred_element_type=jnp.float32)
            for i in range(high):
                for b in range(per_step):
                    entry = code[(r + i) * col_blocks + j * per_step + b]
                    live = lax.rem(entry, 2).astype(jnp.float32)
                    at = (j * row_blocks + r + i) * per_step + b
                    block = product[i * blk : (i + 1) * blk, b * blk : (b + 1) * blk] * live
                    made[at] = block.astype(made.dtype)
                    pltpu.make_async_copy(
                        made.at[at], out_ref.at[0, 0, lax.div(entry, 2)], sem
                    ).start(priority=at % 2)
    pltpu.make_async_copy(made, out_ref.at[0, 0], sem).wait()


def weight_gradient(core, turned, grads, code, row_blocks, col_blocks, blk, slabs):
    arrays = [*turned, *grads]
    blocks = row_blocks * col_blocks
    [out] = core(
        functools.partial(weight_kernel, row_blocks, col_blocks, slabs, len(turned)),
        "weight_gradient",
        [jax.ShapeDtypeStruct((1, 1, blocks, blk, blk), jnp.bfloat16)],
        [anywhere],
        [in_smem] + [in_vmem] * len(arrays),
        (code, *arrays),
        scratch=[pltpu.VMEM((blocks, blk, blk), jnp.bfloat16), pltpu.SemaphoreType.DMA],
        limit=vmem_limit + 2 * blocks * blk * blk,
    )
    return out


def place_kernel(spots, *refs):
    blocks = refs[: len(spots)]
    out_ref, sems = refs[len(spots) :]
    copies = []
    for at, (top, first) in enumerate(spots):
        rows, width = blocks[at].shape
        target = out_ref.at[pl.ds(top, rows), pl.ds(first, width)]
        copies.append(pltpu.make_async_copy(blocks[at], target, sems.at[at]))
        copies[-1].start()
    for copy in copies:
        copy.wait()


def place_activation(core, blocks, spots, shape):
    [out] = core(
        functools.partial(place_kernel, spots),
        "place_activation",
        [jax.ShapeDtypeStruct(shape, jnp.bfloat16)],
        [anywhere],
        [in_vmem] * len(blocks),
        blocks,
        scratch=[pltpu.SemaphoreType.DMA((len(blocks),))],
    )
    return out


def total_kernel(each, many, starts, sizes, *refs):
    out_ref = refs[-1]
    own = sum(sizes)
    for k, (start, rows) in enumerate(zip(starts, sizes)):
        found = refs[k * many : (k + 1) * many]
        for j in range(each):
            here = slice(j * rows, (j + 1) * rows)
            total = found[0][here, :]
            for piece in found[1:]:
                total = total + piece[here, :].astype(jnp.float32)
            top = j * own + start
            out_ref[top : top + rows, :] = total.astype(jnp.bfloat16)


def total_input(core, found, each, starts, sizes):
    arrays = [x for part in found for x in part]
    shape = (each * sum(sizes), arrays[0].shape[1])
    [out] = core(
        functools.partial(total_kernel, each, len(found[0]), starts, sizes),
        "total_input",
        [jax.ShapeDtypeStruct(shape, jnp.bfloat16)],
        [pl.BlockSpec(shape, lambda: (0, 0))],
        [in_vmem] * len(arrays),
        arrays,
    )
    return out


def swap(array, axis, size, bit):
    return lax.ppermute(array, axis, [(i, i ^ bit) for i in range(size)])


def on_device(tokens, w_packed, kept_rows, kept_cols, kept_count, grad_act):
    blk = w_packed.shape[-1]
    slot_count = w_packed.shape[2]
    tall = tokens.shape[1]
    row_tokens, hidden_here = grad_act.shape
    row_blocks = tall // blk
    col_blocks = hidden_here // blk
    n_row = lax.axis_size("row")
    n_col = lax.axis_size("col")
    row_me = lax.axis_index("row")
    col_me = lax.axis_index("col")
    col_groups = tokens.shape[0] // row_tokens
    tiles = row_tokens // 16
    shares = token_split if tiles % sum(token_split) == 0 else (1,)
    sizes = [16 * (tiles // sum(shares)) * share for share in shares]
    starts = [sum(sizes[:k]) for k in range(len(sizes))]
    parts = len(sizes)
    slabs = group_of(col_blocks, column_parts)
    width = hidden_here // slabs
    direct = n_col <= 8
    core = Core()

    places = kept_rows[0, 0] * col_blocks + kept_cols[0, 0]
    slots = jnp.arange(slot_count, dtype=jnp.int32)
    coded = slots * 2 + (slots < kept_count[0, 0]).astype(jnp.int32)
    code = jnp.sum(jnp.where(places[None, :] == slots[:, None], coded[None, :], 0), axis=1)

    apart = row_me ^ (col_me * col_groups) if direct else row_me
    everyone = np.arange(n_row)
    order = np.concatenate([everyone[::2], everyone[1::2]]).astype(np.int32)
    pick = (jnp.asarray(order) ^ apart).astype(jnp.int32)
    distance = jnp.asarray(everyone.astype(np.int32)) ^ apart
    place = ((distance & 1) * (n_row // 2) + (distance >> 1)).astype(jnp.int32)

    pieces = []
    for start, rows in zip(starts, sizes):
        mine = tokens.reshape(col_groups, row_tokens, tall)[:, start : start + rows]
        if direct:
            pieces.append([mine] + [swap(mine, "col", n_col, m) for m in range(1, n_col)])
        else:
            pieces.append([lax.all_gather(mine, "col", axis=0, tiled=True)])
    weight = dense_tile(core, w_packed, code, row_blocks, col_blocks, [pick, place])

    far_bits = [1 << b for b in range(1, n_row.bit_length() - 1)]
    units = [(k, c) for k in range(parts) for c in range(slabs)]
    paths = [far_bits if at % 2 == 0 else far_bits[::-1] for at in range(len(units))]
    state = {}
    full, turned = {}, {}
    activations, input_grads = {}, {}

    def begin(k, c, path):
        if c == 0:
            full[k], turned[k] = arrange(core, pieces[k], pick)
        keep, send = forward(core, full[k], weight, c * width, width)
        state[k, c] = (keep, swap(send, "row", n_row, 1))

    def add(at, k, c, path):
        left = sorted(path[at:], reverse=True)
        keep, send = add_step(core, *state[k, c], left, path[at])
        state[k, c] = (keep, swap(send, "row", n_row, path[at]))

    def bend(k, c, path):
        activations[k, c], near = gelu(core, *state[k, c], grad_act, starts[k], c * width)
        state[k, c] = (near, swap(near, "row", n_row, ([1] + path)[-1]))

    def join(at, k, c, path):
        held = sorted(path[at:], reverse=True)
        near = join_step(core, *state[k, c], held, path[at])
        state[k, c] = (near, swap(near, "row", n_row, ([1] + path)[at]))

    def finish(k, c, path):
        if c + 1 < slabs:
            return
        grads = [state[k, c] for c in range(slabs)]
        found = input_partial(core, grads, weight, place, n_col if direct else 1)
        if direct:
            input_grads[k] = [found[0]]
            input_grads[k] += [swap(found[m], "col", n_col, m) for m in range(1, n_col)]
        else:
            total = found[0].reshape(n_col, col_groups * sizes[k], tall)
            total = lax.psum_scatter(total, "col", scatter_dimension=0, tiled=True)[0]
            input_grads[k] = [total]

    hops = len(far_bits)
    stages = [begin] + [functools.partial(add, at) for at in range(hops)] + [bend]
    stages += [functools.partial(join, at) for at in reversed(range(hops))] + [finish]
    plan = [(k, at) for at in range(len(stages)) for k in range(parts)]
    if parts == 2 and hops == 2:
        plan = [(0, 0), (0, 1), (0, 2), (1, 0), (1, 1), (0, 3), (0, 4), (1, 2), (0, 5), (1, 3), (1, 4), (0, 6), (1, 5), (1, 6)]
    for k, at in plan:
        for c in range(slabs):
            stages[at](k, c, paths[units.index((k, c))])
        if (k, at) == (parts - 1, len(stages) - 3):
            activation = place_activation(
                core,
                [activations[k, c] for k, c in units],
                [(starts[k], c * width) for k, c in units],
                grad_act.shape,
            )
    weight_grad = weight_gradient(
        core,
        [turned[k] for k in range(parts)],
        [g for c in range(slabs) for k in range(parts) for g in state[k, c]],
        code,
        row_blocks,
        col_blocks,
        blk,
        slabs,
    )
    input_grad = total_input(
        core, [input_grads[k] for k in range(parts)], col_groups, starts, sizes
    )
    return (activation, input_grad, weight_grad)


def solution(mesh):
    placed = (
        P("col", "row"),
        P("row", "col", None, None, None),
        P("row", "col", None),
        P("row", "col", None),
        P("row", "col"),
        P("row", "col"),
    )
    return jax.shard_map(
        on_device,
        mesh=mesh,
        in_specs=placed,
        out_specs=(P("row", "col"), P("col", "row"), P("row", "col", None, None, None)),
        check_vma=False,
    )
```

```python
import functools

import jax
import jax.numpy as jnp
import numpy as np
from jax import lax
from jax.experimental import pallas as pl
from jax.experimental.pallas import tpu as pltpu
from jax.sharding import PartitionSpec as P

gelu_scale = 0.7978845608
gelu_cubic = 0.044715
token_split = (1, 1)
column_parts = 2
vmem_limit = 16 * 1024 * 1024
in_vmem = pl.BlockSpec(memory_space=pltpu.VMEM)
in_smem = pl.BlockSpec(memory_space=pltpu.SMEM)
anywhere = pl.BlockSpec(memory_space=pltpu.HBM)


def gelu_pair(hidden, cotangent):
    inner = gelu_scale * (hidden + gelu_cubic * hidden * hidden * hidden)
    tangent = jnp.tanh(inner)
    activation = (0.5 * hidden * (1.0 + tangent)).astype(jnp.bfloat16)
    slope = 0.5 * (1.0 + tangent) + 0.5 * hidden * (1.0 - tangent * tangent) * gelu_scale * (
        1.0 + 3.0 * gelu_cubic * hidden * hidden
    )
    slope_grad = (cotangent.astype(jnp.float32) * slope).astype(jnp.bfloat16)
    return (activation, slope_grad)


def group_of(blocks, goal):
    return max(n for n in range(1, goal + 1) if blocks % n == 0)


class Core:
    def __init__(self):
        self.turn = None

    def __call__(self, kernel, name, out_shape, out_specs, in_specs, operands, scratch=(), limit=vmem_limit):
        homes = {id(in_vmem): pltpu.VMEM, id(anywhere): pltpu.HBM}
        in_specs, operands = list(in_specs), list(operands)
        if self.turn is not None:
            in_specs.append(in_vmem)
            operands.append(self.turn)
        taken = len(operands)
        given = len(out_shape)
        extra = self.turn is not None

        def body(*refs):
            refs[taken + given][...] = jnp.zeros((8, 128), jnp.float32)
            kernel(*refs[: taken - extra], *refs[taken : taken + given], *refs[taken + given + 1 :])

        placed = [
            pltpu.with_memory_space_constraint(x, homes[id(spec)]) if id(spec) in homes else x
            for x, spec in zip(operands, in_specs)
        ]
        *out, self.turn = pl.pallas_call(
            body,
            out_shape=[*out_shape, pltpu.VMEM((8, 128), jnp.float32)],
            in_specs=in_specs,
            out_specs=[*out_specs, in_vmem],
            scratch_shapes=list(scratch),
            compiler_params=pltpu.CompilerParams(vmem_limit_bytes=limit),
            cost_estimate=pl.CostEstimate(flops=1, transcendentals=0, bytes_accessed=1),
            name=name,
        )(*placed)
        return out


def dense_kernel(row_blocks, col_blocks, code, w_ref, *refs):
    out_ref, empty, sem = refs[-3:]
    blk = w_ref.shape[-1]
    empty[...] = jnp.zeros_like(empty)

    def load(at, carry):
        for r in range(row_blocks):
            entry = code[r * col_blocks + at]
            start = pl.multiple_of(at * blk, blk)
            target = out_ref.at[pl.ds(r * blk, blk), pl.ds(start, blk)]

            @pl.when(lax.rem(entry, 2) == 1)
            def _():
                pltpu.make_async_copy(w_ref.at[0, 0, lax.div(entry, 2)], target, sem).start()

            @pl.when(lax.rem(entry, 2) == 0)
            def _():
                pltpu.make_async_copy(empty, target, sem).start()

        return carry

    lax.fori_loop(0, col_blocks, load, 0)
    pltpu.make_async_copy(out_ref, out_ref, sem).wait()


def dense_tile(core, w_packed, code, row_blocks, col_blocks, ready):
    blk = w_packed.shape[-1]
    [weight] = core(
        functools.partial(dense_kernel, row_blocks, col_blocks),
        "dense_tile",
        [pltpu.VMEM((row_blocks * blk, col_blocks * blk), w_packed.dtype)],
        [in_vmem],
        [in_smem, anywhere] + [in_smem] * len(ready),
        (code, w_packed, *ready),
        scratch=[pltpu.VMEM((blk, blk), w_packed.dtype), pltpu.SemaphoreType.DMA],
    )
    return weight


def arrange_kernel(groups, rows, pieces, pick, *refs):
    out_ref, turned_ref, all_ref = refs[pieces:]
    each = groups // pieces
    for m in range(pieces):
        for j in range(each):
            all_ref[m * each + j] = refs[m][j]
    for t in range(groups):
        out_ref[pl.ds(t * rows, rows), :] = all_ref[pick[t]]
    turned_ref[...] = out_ref[...].T


def arrange(core, pieces, pick):
    groups = pick.shape[0]
    rows, tall = pieces[0].shape[1:]
    kind = pieces[0].dtype
    return core(
        functools.partial(arrange_kernel, groups, rows, len(pieces)),
        "arrange",
        [pltpu.VMEM((groups * rows, tall), kind), pltpu.VMEM((tall, groups * rows), kind)],
        [in_vmem, in_vmem],
        [in_smem] + [in_vmem] * len(pieces),
        (pick, *pieces),
        scratch=[pltpu.VMEM((groups, rows, tall), kind)],
    )


def forward_kernel(first, wide, x_ref, w_ref, keep_ref, send_ref):
    half, width = keep_ref.shape
    for at in range(0, width, wide):
        product = jnp.dot(
            x_ref[...], w_ref[:, first + at : first + at + wide], preferred_element_type=jnp.float32
        )
        keep_ref[:, at : at + wide] = product[:half]
        send_ref[:, at : at + wide] = product[half:].astype(jnp.bfloat16)


def forward(core, features, weight, first, width):
    half = features.shape[0] // 2
    wide = 128 * group_of(width // 128, 4)
    return core(
        functools.partial(forward_kernel, first, wide),
        "forward",
        [pltpu.VMEM((half, width), jnp.float32), pltpu.VMEM((half, width), jnp.bfloat16)],
        [in_vmem, in_vmem],
        [in_vmem, in_vmem],
        (features, weight),
    )


def sides(left, bit):
    at = len(left) - 1 - left.index(bit)
    names = range(1 << len(left))
    return [g for g in names if not g >> at & 1], [g for g in names if g >> at & 1]


def add_kernel(rows, stay, leave, keep_ref, arrived_ref, next_ref, send_ref):
    for out_ref, groups in ((next_ref, stay), (send_ref, leave)):
        for at, g in enumerate(groups):
            here = slice(g * rows, (g + 1) * rows)
            total = keep_ref[here, :] + arrived_ref[here, :].astype(jnp.float32)
            out_ref[at * rows : (at + 1) * rows, :] = total.astype(out_ref.dtype)


def add_step(core, keep, arrived, left, bit):
    rows = keep.shape[0] >> len(left)
    half = (keep.shape[0] // 2, keep.shape[1])
    return core(
        functools.partial(add_kernel, rows, *sides(left, bit)),
        "add_step",
        [pltpu.VMEM(half, jnp.float32), pltpu.VMEM(half, jnp.bfloat16)],
        [in_vmem, in_vmem],
        [in_vmem, in_vmem],
        (keep, arrived),
    )


def join_kernel(rows, stay, come, near_ref, arrived_ref, out_ref):
    for in_ref, groups in ((near_ref, stay), (arrived_ref, come)):
        for at, g in enumerate(groups):
            out_ref[g * rows : (g + 1) * rows, :] = in_ref[at * rows : (at + 1) * rows, :]


def join_step(core, near, arrived, held, bit):
    rows = 2 * near.shape[0] >> len(held)
    [out] = core(
        functools.partial(join_kernel, rows, *sides(held, bit)),
        "join_step",
        [pltpu.VMEM((2 * near.shape[0], near.shape[1]), near.dtype)],
        [in_vmem],
        [in_vmem, in_vmem],
        (near, arrived),
    )
    return out


def gelu_kernel(top, first, keep_ref, arrived_ref, cotangent_ref, activation_ref, slope_ref):
    rows, width = keep_ref.shape
    hidden = keep_ref[...] + arrived_ref[...].astype(jnp.float32)
    cotangent = cotangent_ref[top : top + rows, first : first + width]
    activation_ref[...], slope_ref[...] = gelu_pair(hidden, cotangent)


def gelu(core, keep, arrived, cotangent, top, first):
    out = pltpu.VMEM(keep.shape, jnp.bfloat16)
    return core(
        functools.partial(gelu_kernel, top, first),
        "gelu",
        [out, out],
        [in_vmem, in_vmem],
        [in_vmem] * 3,
        (keep, arrived, cotangent),
    )


def input_kernel(groups, slabs, given, place, *refs):
    grads = [refs[2 * c : 2 * c + 2] for c in range(slabs)]
    w_ref = refs[2 * slabs]
    outs = refs[2 * slabs + 1 : 2 * slabs + 1 + given]
    turned, total, upright = refs[2 * slabs + 1 + given :]
    half, width = grads[0][0].shape
    rows = 2 * half // groups
    tall = w_ref.shape[0]
    wide = 128 * group_of(width // 128, 4)
    for c in range(slabs):
        for at in range(0, width, wide):
            here = slice(at, at + wide)
            grad = jnp.concatenate([g[:, here] for g in grads[c]], axis=0)
            turned[c * width + at : c * width + at + wide, :] = grad.T
    high = 128 * group_of(tall // 128, 4)
    for at in range(0, tall, high):
        here = slice(at, at + high)
        total[here, :] = jnp.dot(w_ref[here, :], turned[...], preferred_element_type=jnp.float32)
    upright[...] = total[...].T
    each = groups // given
    for i in range(groups):
        start = pl.multiple_of(place[i] * rows, rows)
        out_ref = outs[i // each]
        at = i % each * rows
        out_ref[at : at + rows, :] = upright[pl.ds(start, rows), :].astype(out_ref.dtype)


def input_partial(core, grads, weight, place, pieces):
    slabs = len(grads)
    half, width = grads[0][0].shape
    tall = weight.shape[0]
    both = 2 * half
    outs = [pltpu.VMEM((both // pieces, tall), jnp.float32)]
    outs += [pltpu.VMEM((both // pieces, tall), jnp.bfloat16)] * (pieces - 1)
    return core(
        functools.partial(input_kernel, place.shape[0], slabs, len(outs)),
        "input_partial",
        outs,
        [in_vmem] * len(outs),
        [in_smem] + [in_vmem] * (2 * slabs + 1),
        (place, *(g for pair in grads for g in pair), weight),
        scratch=[
            pltpu.VMEM((slabs * width, both), weight.dtype),
            pltpu.VMEM((tall, both), jnp.float32),
            pltpu.VMEM((both, tall), jnp.float32),
        ],
    )


def weight_kernel(row_blocks, col_blocks, slabs, parts, code, *refs):
    turned = refs[:parts]
    grads = [refs[parts * (1 + 2 * c) : parts * (3 + 2 * c)] for c in range(slabs)]
    out_ref, made, sem = refs[parts * (1 + 2 * slabs) :]
    blk = made.shape[-1]
    here = col_blocks // slabs
    per_step = group_of(here, 4)
    wide = per_step * blk
    high = group_of(row_blocks, 2)
    for j in range(col_blocks // per_step):
        c, left = divmod(j * per_step, here)
        columns = slice(left * blk, left * blk + wide)
        grad = jnp.concatenate([g[:, columns] for g in grads[c]], axis=0)
        for r in range(0, row_blocks, high):
            rows = slice(r * blk, (r + high) * blk)
            features = jnp.concatenate([t[rows, :] for t in turned], axis=1)
            product = jnp.dot(features, grad, preferred_element_type=jnp.float32)
            for i in range(high):
                for b in range(per_step):
                    entry = code[(r + i) * col_blocks + j * per_step + b]
                    live = lax.rem(entry, 2).astype(jnp.float32)
                    at = (j * row_blocks + r + i) * per_step + b
                    block = product[i * blk : (i + 1) * blk, b * blk : (b + 1) * blk] * live
                    made[at] = block.astype(made.dtype)
                    pltpu.make_async_copy(
                        made.at[at], out_ref.at[0, 0, lax.div(entry, 2)], sem
                    ).start(priority=at % 2)
    pltpu.make_async_copy(made, out_ref.at[0, 0], sem).wait()


def weight_gradient(core, turned, grads, code, row_blocks, col_blocks, blk, slabs):
    arrays = [*turned, *grads]
    blocks = row_blocks * col_blocks
    [out] = core(
        functools.partial(weight_kernel, row_blocks, col_blocks, slabs, len(turned)),
        "weight_gradient",
        [jax.ShapeDtypeStruct((1, 1, blocks, blk, blk), jnp.bfloat16)],
        [anywhere],
        [in_smem] + [in_vmem] * len(arrays),
        (code, *arrays),
        scratch=[pltpu.VMEM((blocks, blk, blk), jnp.bfloat16), pltpu.SemaphoreType.DMA],
        limit=vmem_limit + 2 * blocks * blk * blk,
    )
    return out


def place_kernel(spots, *refs):
    blocks = refs[: len(spots)]
    out_ref, sems = refs[len(spots) :]
    copies = []
    for at, (top, first) in enumerate(spots):
        rows, width = blocks[at].shape
        target = out_ref.at[pl.ds(top, rows), pl.ds(first, width)]
        copies.append(pltpu.make_async_copy(blocks[at], target, sems.at[at]))
        copies[-1].start()
    for copy in copies:
        copy.wait()


def place_activation(core, blocks, spots, shape):
    [out] = core(
        functools.partial(place_kernel, spots),
        "place_activation",
        [jax.ShapeDtypeStruct(shape, jnp.bfloat16)],
        [anywhere],
        [in_vmem] * len(blocks),
        blocks,
        scratch=[pltpu.SemaphoreType.DMA((len(blocks),))],
    )
    return out


def total_kernel(each, many, starts, sizes, *refs):
    out_ref = refs[-1]
    own = sum(sizes)
    for k, (start, rows) in enumerate(zip(starts, sizes)):
        found = refs[sum(many[:k]) : sum(many[: k + 1])]
        for j in range(each):
            here = slice(j * rows, (j + 1) * rows)
            total = found[0][here, :]
            for piece in found[1:]:
                total = total + piece[here, :].astype(jnp.float32)
            top = j * own + start
            out_ref[top : top + rows, :] = total.astype(jnp.bfloat16)


def total_input(core, found, each, starts, sizes):
    arrays = [x for part in found for x in part]
    shape = (each * sum(sizes), arrays[0].shape[1])
    [out] = core(
        functools.partial(total_kernel, each, [len(part) for part in found], starts, sizes),
        "total_input",
        [jax.ShapeDtypeStruct(shape, jnp.bfloat16)],
        [pl.BlockSpec(shape, lambda: (0, 0))],
        [in_vmem] * len(arrays),
        arrays,
    )
    return out


def swap(array, axis, size, bit):
    return lax.ppermute(array, axis, [(i, i ^ bit) for i in range(size)])


def on_device(tokens, w_packed, kept_rows, kept_cols, kept_count, grad_act):
    blk = w_packed.shape[-1]
    slot_count = w_packed.shape[2]
    tall = tokens.shape[1]
    row_tokens, hidden_here = grad_act.shape
    row_blocks = tall // blk
    col_blocks = hidden_here // blk
    n_row = lax.axis_size("row")
    n_col = lax.axis_size("col")
    row_me = lax.axis_index("row")
    col_me = lax.axis_index("col")
    col_groups = tokens.shape[0] // row_tokens
    tiles = row_tokens // 16
    shares = token_split if tiles % sum(token_split) == 0 else (1,)
    sizes = [16 * (tiles // sum(shares)) * share for share in shares]
    starts = [sum(sizes[:k]) for k in range(len(sizes))]
    parts = len(sizes)
    slabs = group_of(col_blocks, column_parts)
    width = hidden_here // slabs
    direct = n_col <= 8
    core = Core()

    places = kept_rows[0, 0] * col_blocks + kept_cols[0, 0]
    slots = jnp.arange(slot_count, dtype=jnp.int32)
    coded = slots * 2 + (slots < kept_count[0, 0]).astype(jnp.int32)
    code = jnp.sum(jnp.where(places[None, :] == slots[:, None], coded[None, :], 0), axis=1)

    apart = row_me ^ (col_me * col_groups) if direct else row_me
    everyone = np.arange(n_row)
    order = np.concatenate([everyone[::2], everyone[1::2]]).astype(np.int32)
    pick = (jnp.asarray(order) ^ apart).astype(jnp.int32)
    distance = jnp.asarray(everyone.astype(np.int32)) ^ apart
    place = ((distance & 1) * (n_row // 2) + (distance >> 1)).astype(jnp.int32)

    pieces = []
    for start, rows in zip(starts, sizes):
        mine = tokens.reshape(col_groups, row_tokens, tall)[:, start : start + rows]
        if direct:
            pieces.append([mine] + [swap(mine, "col", n_col, m) for m in range(1, n_col)])
        else:
            pieces.append([lax.all_gather(mine, "col", axis=0, tiled=True)])
    weight = dense_tile(core, w_packed, code, row_blocks, col_blocks, [pick, place])

    far_bits = [1 << b for b in range(1, n_row.bit_length() - 1)]
    units = [(k, c) for k in range(parts) for c in range(slabs)]
    paths = [far_bits if at % 2 == 0 else far_bits[::-1] for at in range(len(units))]
    state = {}
    full, turned = {}, {}
    activations, input_grads = {}, {}

    def begin(k, c, path):
        if c == 0:
            full[k], turned[k] = arrange(core, pieces[k], pick)
        keep, send = forward(core, full[k], weight, c * width, width)
        state[k, c] = (keep, swap(send, "row", n_row, 1))

    def add(at, k, c, path):
        left = sorted(path[at:], reverse=True)
        keep, send = add_step(core, *state[k, c], left, path[at])
        state[k, c] = (keep, swap(send, "row", n_row, path[at]))

    def bend(k, c, path):
        activations[k, c], near = gelu(core, *state[k, c], grad_act, starts[k], c * width)
        state[k, c] = (near, swap(near, "row", n_row, ([1] + path)[-1]))

    def join(at, k, c, path):
        held = sorted(path[at:], reverse=True)
        near = join_step(core, *state[k, c], held, path[at])
        state[k, c] = (near, swap(near, "row", n_row, ([1] + path)[at]))

    def finish(k, c, path):
        if c + 1 < slabs:
            return
        grads = [state[k, c] for c in range(slabs)]
        halved = n_col == 4 and k + 1 < parts
        spots = place.reshape(n_col, -1)[jnp.array([0, 2, 1, 3])].reshape(-1) if halved else place
        found = input_partial(
            core, grads, weight, spots, 2 if halved else n_col if direct else 1
        )
        if halved:
            keep, send = add_step(core, found[0], swap(found[1], "col", n_col, 1), [2], 2)
            input_grads[k] = [keep, swap(send, "col", n_col, 2)]
        elif direct:
            input_grads[k] = [found[0]]
            input_grads[k] += [swap(found[m], "col", n_col, m) for m in range(1, n_col)]
        else:
            total = found[0].reshape(n_col, col_groups * sizes[k], tall)
            total = lax.psum_scatter(total, "col", scatter_dimension=0, tiled=True)[0]
            input_grads[k] = [total]

    hops = len(far_bits)
    stages = [begin] + [functools.partial(add, at) for at in range(hops)] + [bend]
    stages += [functools.partial(join, at) for at in reversed(range(hops))] + [finish]
    plan = [(k, at) for at in range(len(stages)) for k in range(parts)]
    if parts == 2 and hops == 2:
        plan = [(0, 0), (0, 1), (0, 2), (1, 0), (1, 1), (0, 3), (0, 4), (1, 2), (0, 5), (1, 3), (1, 4), (0, 6), (1, 5), (1, 6)]
    for k, at in plan:
        for c in range(slabs):
            stages[at](k, c, paths[units.index((k, c))])
        if (k, at) == (parts - 1, len(stages) - 3):
            activation = place_activation(
                core,
                [activations[k, c] for k, c in units],
                [(starts[k], c * width) for k, c in units],
                grad_act.shape,
            )
    weight_grad = weight_gradient(
        core,
        [turned[k] for k in range(parts)],
        [g for c in range(slabs) for k in range(parts) for g in state[k, c]],
        code,
        row_blocks,
        col_blocks,
        blk,
        slabs,
    )
    input_grad = total_input(
        core, [input_grads[k] for k in range(parts)], col_groups, starts, sizes
    )
    return (activation, input_grad, weight_grad)


def solution(mesh):
    placed = (
        P("col", "row"),
        P("row", "col", None, None, None),
        P("row", "col", None),
        P("row", "col", None),
        P("row", "col"),
        P("row", "col"),
    )
    return jax.shard_map(
        on_device,
        mesh=mesh,
        in_specs=placed,
        out_specs=(P("row", "col"), P("col", "row"), P("row", "col", None, None, None)),
        check_vma=False,
    )
```
